32 devices in a mesh: rows: 4 (over z), seq: 8 (over y, x, core).
Axes of the slice: x: 2, y: 2, z: 4, core: 2. Of those that a mesh axis runs over, the one named last changes fastest.
Arguments:
- tokens: bfloat16 [8, 2048, 1024], P('rows', 'seq'), may hold values from -6 to 6
- cotangent: bfloat16 [8, 2048, 1024], P('rows', 'seq'), may hold values from -6 to 6
- bounds: int32 [8, 2], P('rows'), may hold values from 1 to 2048, as said below
- ln1_gain: bfloat16 [1024], replicated, may hold values from 0.5 to 1.5
- ln1_bias: bfloat16 [1024], replicated, may hold values from -1.25 to 1.25
- in_weight: bfloat16 [1024, 3072], replicated, may hold values from -0.1875 to 0.1875
- in_bias: bfloat16 [3072], replicated, may hold values from -1.75 to 1.75
- short_weight: bfloat16 [3, 3072], replicated, may hold values from -3.5 to 3.5
- short_bias: bfloat16 [3072], replicated, may hold values from -1.75 to 1.75
- f1_weight: bfloat16 [33, 64], replicated, may hold values from -6 to 6
- f1_bias: bfloat16 [64], replicated, may hold values from -6 to 6
- f2_weight: bfloat16 [64, 64], replicated, may hold values from -0.75 to 0.75
- f2_bias: bfloat16 [64], replicated, may hold values from -3 to 3
- f3_weight: bfloat16 [64, 1024], P(None, 'seq'), may hold values from -0.09375 to 0.09375
- filter_skip: bfloat16 [1024], P('seq'), may hold values from -6 to 6
- out_weight: bfloat16 [1024, 1024], replicated, may hold values from -0.1875 to 0.1875
- out_bias: bfloat16 [1024], replicated, may hold values from -1.25 to 1.25
- ln2_gain: bfloat16 [1024], replicated, may hold values from 0.5 to 1.5
- ln2_bias: bfloat16 [1024], replicated, may hold values from -1.25 to 1.25
- up_weight: bfloat16 [1024, 4096], replicated, may hold values from -0.1875 to 0.1875
- up_bias: bfloat16 [4096], replicated, may hold values from -1.75 to 1.75
- down_weight: bfloat16 [4096, 1024], replicated, may hold values from -0.09375 to 0.09375
- down_bias: bfloat16 [1024], replicated, may hold values from -1.25 to 1.25
Outputs:
- output: bfloat16 [8, 2048, 1024], P('rows', 'seq')
- grad_tokens: float32 [8, 2048, 1024], P('rows', 'seq')
- grad_ln1_gain: float32 [1024], P(('rows', 'seq'))
- grad_ln1_bias: float32 [1024], P(('rows', 'seq'))
- grad_in_weight: float32 [1024, 3072], P(('rows', 'seq'))
- grad_in_bias: float32 [3072], P(('rows', 'seq'))
- grad_short_weight: float32 [3, 3072], P(None, ('rows', 'seq'))
- grad_short_bias: float32 [3072], P(('rows', 'seq'))
- grad_f1_weight: float32 [33, 64], replicated
- grad_f1_bias: float32 [64], replicated
- grad_f2_weight: float32 [64, 64], replicated
- grad_f2_bias: float32 [64], replicated
- grad_f3_weight: float32 [64, 1024], P(None, 'seq')
- grad_filter_skip: float32 [1024], P('seq')
- grad_out_weight: float32 [1024, 1024], P(('rows', 'seq'))
- grad_out_bias: float32 [1024], P(('rows', 'seq'))
- grad_ln2_gain: float32 [1024], P(('rows', 'seq'))
- grad_ln2_bias: float32 [1024], P(('rows', 'seq'))
- grad_up_weight: float32 [1024, 4096], P(('rows', 'seq'))
- grad_up_bias: float32 [4096], P(('rows', 'seq'))
- grad_down_weight: float32 [4096, 1024], P(('rows', 'seq'))
- grad_down_bias: float32 [1024], P(('rows', 'seq'))
The draws below stay inside these ranges and needn't reach their ends.
Inputs may be any that keep to these rules, and one draw needn't show every extreme that they name: `bounds`: in each row the cut points do not fall; a cut at 2048 starts no document; in every group of 2 rows on one index of rows one row is a single document.
All inputs are finite; a program needn't handle non-finite values.
Results may differ from the reference program's by a relative error of at most 0.0097.
Values may be sent and summed in bfloat16 or wider, within the bound.
No kernel may reach another device: no remote copies, remote signals or barrier semaphores. Data moves between devices by JAX's collectives and lax.ppermute only.
A program may use at most 384 MiB of HBM per device.

```python
import math
import jax
import jax.numpy as jnp
from jax import lax

D = 1024
FF = 4096
EMB = 33
FILTER = 64
CUTS = 2
ROWS_DEV = 2
SEQ_LEN = 2048
ROWS = 8


def draw_bounds(key, part):
    key = jax.random.fold_in(key, 7)
    key_cut, key_pick = jax.random.split(key)
    cuts = jnp.sort(jax.random.randint(key_cut, (ROWS, CUTS), 1, SEQ_LEN + 1, dtype=jnp.int32), axis=1)
    picked = jax.random.randint(key_pick, (ROWS // ROWS_DEV,), 0, ROWS_DEV, dtype=jnp.int32)
    whole = jnp.arange(ROWS, dtype=jnp.int32) % ROWS_DEV == jnp.repeat(picked, ROWS_DEV, total_repeat_length=ROWS)
    return jnp.where(whole[:, None], SEQ_LEN, cuts).astype(jnp.int32)


def levels(own_key, extent, cuts, smallest, high):
    level, own = 1.0, jax.random.fold_in(own_key, 6)
    for position, parts in cuts:
        draws = jnp.exp(jax.random.uniform(jax.random.fold_in(own, position), (parts,), jnp.float32, smallest / len(cuts), high / len(cuts)))
        level = level * jnp.repeat(draws, extent[position] // parts).reshape([-1 if axis == position else 1 for axis in range(len(extent))])
    return level


def gaussian(key, shape, deviation, most, pieces=(), held_as=jnp.bfloat16):
    values = jax.random.normal(key, shape, jnp.float32) * deviation
    if len(pieces) > 0:
        values = levels(key, shape, pieces, -0.22, 0.18) * values
    return jnp.clip(values, min=-most, max=most).astype(held_as)


def setup_inputs(seed: int = 0) -> dict:
    arg_keys = jax.random.split(jax.random.key(seed), 24)
    tokens = gaussian(arg_keys[0], (ROWS, SEQ_LEN, D), 1.0, 6.0, ((0, 4), (1, 8)))
    cotangent = gaussian(arg_keys[1], (ROWS, SEQ_LEN, D), 1.0, 6.0, ((0, 4), (1, 8)))
    bounds = draw_bounds(jax.random.fold_in(arg_keys[23], 71), 0)
    ln1_gain = jnp.clip(1.0 + 0.1 * jax.random.normal(arg_keys[3], (D,), jnp.float32), 0.5, 1.5).astype(jnp.bfloat16)
    ln1_bias = gaussian(arg_keys[4], (D,), 0.2, 1.25)
    in_weight = gaussian(arg_keys[5], (D, 3 * D), D ** -0.5, 0.1875)
    in_bias = gaussian(arg_keys[6], (3 * D,), 0.3, 1.75)
    short_weight = gaussian(arg_keys[7], (3, 3 * D), 0.6, 3.5)
    short_bias = gaussian(arg_keys[8], (3 * D,), 0.3, 1.75)
    f1_weight = gaussian(arg_keys[9], (EMB, FILTER), 1.0, 6.0)
    f1_bias = gaussian(arg_keys[10], (FILTER,), 1.0, 6.0)
    f2_weight = gaussian(arg_keys[11], (FILTER, FILTER), FILTER ** -0.5, 0.75)
    f2_bias = gaussian(arg_keys[12], (FILTER,), 0.5, 3.0)
    f3_weight = gaussian(arg_keys[13], (FILTER, D), (2 * SEQ_LEN) ** -0.5, 0.09375, ((1, 8),))
    filter_skip = gaussian(arg_keys[14], (D,), 1.0, 6.0, ((0, 8),))
    out_weight = gaussian(arg_keys[15], (D, D), D ** -0.5, 0.1875)
    out_bias = gaussian(arg_keys[16], (D,), 0.2, 1.25)
    ln2_gain = jnp.clip(1.0 + 0.1 * jax.random.normal(arg_keys[17], (D,), jnp.float32), 0.5, 1.5).astype(jnp.bfloat16)
    ln2_bias = gaussian(arg_keys[18], (D,), 0.2, 1.25)
    up_weight = gaussian(arg_keys[19], (D, FF), D ** -0.5, 0.1875)
    up_bias = gaussian(arg_keys[20], (FF,), 0.3, 1.75)
    down_weight = gaussian(arg_keys[21], (FF, D), FF ** -0.5, 0.09375)
    down_bias = gaussian(arg_keys[22], (D,), 0.2, 1.25)
    return {"tokens": tokens, "cotangent": cotangent, "bounds": bounds, "ln1_gain": ln1_gain, "ln1_bias": ln1_bias, "in_weight": in_weight, "in_bias": in_bias, "short_weight": short_weight, "short_bias": short_bias, "f1_weight": f1_weight, "f1_bias": f1_bias, "f2_weight": f2_weight, "f2_bias": f2_bias, "f3_weight": f3_weight, "filter_skip": filter_skip, "out_weight": out_weight, "out_bias": out_bias, "ln2_gain": ln2_gain, "ln2_bias": ln2_bias, "up_weight": up_weight, "up_bias": up_bias, "down_weight": down_weight, "down_bias": down_bias}


HIGH = lax.Precision.HIGHEST
eps = 1e-05
slow_rate = math.log(100.0) / 1.5
fast_rate = math.log(100.0) / 0.3

@jax.custom_vjp
def low(v):
    return lax.optimization_barrier(v.astype(jnp.bfloat16)).astype(jnp.float32)

@jax.custom_vjp
def low_back(v):
    return v

def low_keep(v):
    return (low(v), None)

def low_pass(kept, grad):
    return (grad,)

def back_keep(v):
    return (v, None)

def back_low(kept, grad):
    return (low(grad),)
low.defvjp(low_keep, low_pass)
low_back.defvjp(back_keep, back_low)

def layer_norm(values, gain, shift):
    center = values - lax.optimization_barrier(jnp.mean(values, axis=-1, keepdims=True))
    spread = lax.optimization_barrier(jnp.mean(center * center, axis=-1, keepdims=True))
    return center * lax.rsqrt(spread + eps) * gain + shift

def features(length):
    steps = jnp.arange(length, dtype=jnp.int32).astype(jnp.float32)
    bands = (EMB - 1) // 2
    freqs = 0.0001 + jnp.arange(bands, dtype=jnp.int32).astype(jnp.float32) * ((bands - 1 - 0.0001) / (bands - 1))
    angles = (steps * (2.0 * math.pi / length))[:, None] * freqs[None, :]
    timeline = steps / (length - 1)
    return (jnp.concatenate([timeline[:, None], jnp.cos(angles), -jnp.sin(angles)], axis=1), timeline)

def filter_taps(w_one, b_one, w_two, b_two, w_three, first, length):
    feats, timeline = features(length)
    hidden = jnp.sin(jnp.dot(feats, w_one, precision=HIGH) + b_one)
    hidden = jnp.sin(jnp.dot(hidden, w_two, precision=HIGH) + b_two)
    raw_taps = jnp.dot(hidden, w_three, precision=HIGH)
    channels = (first + jnp.arange(w_three.shape[1], dtype=jnp.int32)).astype(jnp.float32)
    rates = slow_rate + channels * ((fast_rate - slow_rate) / (D - 1))
    return raw_taps * jnp.exp(-timeline[:, None] * rates[None, :])

def document_masks(bounds, positions, length):
    lower = jnp.concatenate([jnp.zeros_like(bounds[:, :1]), bounds], axis=1)
    upper = jnp.concatenate([bounds, jnp.full_like(bounds[:, :1], length)], axis=1)
    inside = (positions[None, None, :] >= lower[:, :, None]) & (positions[None, None, :] < upper[:, :, None])
    return inside.astype(jnp.float32)

def forward_row(params, row, cuts):
    ln1_gain, ln1_bias, in_weight, in_bias, short_weight, short_bias, f1_weight, f1_bias, f2_weight, f2_bias, f3_weight, filter_skip, out_weight, out_bias, ln2_gain, ln2_bias, up_weight, up_bias, down_weight, down_bias = params
    length, width = row.shape
    here = jnp.arange(length, dtype=jnp.int32)
    n1 = low(layer_norm(row, ln1_gain, ln1_bias))
    proj = low(low_back(jnp.dot(n1, in_weight, precision=HIGH) + in_bias))
    starts = lax.optimization_barrier(jnp.max(jnp.where(cuts[:, None] <= here[None, :], cuts[:, None], 0), axis=0))
    keep_one = (here - 1 >= starts).astype(jnp.float32)[:, None]
    keep_two = (here - 2 >= starts).astype(jnp.float32)[:, None]
    zero_line = jnp.zeros((1, 3 * width), jnp.float32)
    before_one = jnp.concatenate([zero_line, proj[:-1]], axis=0)
    before_two = jnp.concatenate([zero_line, zero_line, proj[:-2]], axis=0)
    shorted = short_weight[0] * proj + keep_one * short_weight[1] * before_one + keep_two * short_weight[2] * before_two + short_bias
    gate_out = shorted[:, :width]
    gate_in = shorted[:, width:2 * width]
    values = shorted[:, 2 * width:]
    carried = low(low_back(gate_in * values))
    taps = filter_taps(f1_weight, f1_bias, f2_weight, f2_bias, f3_weight, 0, length)
    masks = document_masks(cuts[None, :], here, length)[0][:, :, None]
    spec_carried = jnp.fft.rfft(masks * carried[None], n=2 * length, axis=1)
    spec_taps = jnp.fft.rfft(taps, n=2 * length, axis=0)
    conv = jnp.fft.irfft(spec_carried * spec_taps[None], n=2 * length, axis=1)[:, :length]
    conv = lax.optimization_barrier(jnp.sum(masks * conv, axis=0))
    long_val = low(low_back(conv + filter_skip * carried))
    mixed = low(gate_out * long_val)
    branch = low_back(jnp.dot(mixed, out_weight, precision=HIGH) + out_bias)
    resid = row + branch
    n2 = low(layer_norm(resid, ln2_gain, ln2_bias))
    pre = low_back(jnp.dot(n2, up_weight, precision=HIGH) + up_bias)
    act = low(jax.nn.gelu(pre, approximate=True))
    return resid + jnp.dot(act, down_weight, precision=HIGH) + down_bias

def reference(tokens, cotangent, bounds, ln1_gain, ln1_bias, in_weight, in_bias, short_weight, short_bias, f1_weight, f1_bias, f2_weight, f2_bias, f3_weight, filter_skip, out_weight, out_bias, ln2_gain, ln2_bias, up_weight, up_bias, down_weight, down_bias):
    params = (ln1_gain.astype(jnp.float32), ln1_bias.astype(jnp.float32), in_weight.astype(jnp.float32), in_bias.astype(jnp.float32), short_weight.astype(jnp.float32), short_bias.astype(jnp.float32), f1_weight.astype(jnp.float32), f1_bias.astype(jnp.float32), f2_weight.astype(jnp.float32), f2_bias.astype(jnp.float32), f3_weight.astype(jnp.float32), filter_skip.astype(jnp.float32), out_weight.astype(jnp.float32), out_bias.astype(jnp.float32), ln2_gain.astype(jnp.float32), ln2_bias.astype(jnp.float32), up_weight.astype(jnp.float32), up_bias.astype(jnp.float32), down_weight.astype(jnp.float32), down_bias.astype(jnp.float32))

    def one_row(totals, item):
        row, grad_row, cuts = item
        result, pull = jax.vjp(lambda weights, inputs: forward_row(weights, inputs, cuts), params, row)
        grads, grad_in = pull(grad_row)
        totals = jax.tree.map(lambda left, right: left + right, totals, grads)
        return (totals, (result.astype(jnp.bfloat16), grad_in))
    start_totals = jax.tree.map(jnp.zeros_like, params)
    totals, (output, grad_tokens) = lax.scan(one_row, start_totals, (tokens.astype(jnp.float32), cotangent.astype(jnp.float32), bounds))
    g_ln1_gain, g_ln1_bias, g_in_weight, g_in_bias, g_short_weight, g_short_bias, g_f1_weight, g_f1_bias, g_f2_weight, g_f2_bias, g_f3_weight, g_filter_skip, g_out_weight, g_out_bias, g_ln2_gain, g_ln2_bias, g_up_weight, g_up_bias, g_down_weight, g_down_bias = totals
    return (output, grad_tokens, g_ln1_gain, g_ln1_bias, g_in_weight, g_in_bias, g_short_weight, g_short_bias, g_f1_weight, g_f1_bias, g_f2_weight, g_f2_bias, g_f3_weight, g_filter_skip, g_out_weight, g_out_bias, g_ln2_gain, g_ln2_bias, g_up_weight, g_up_bias, g_down_weight, g_down_bias)
```

```python
import functools
import math

import jax
import jax.numpy as jnp
import ml_dtypes
import numpy as np
from jax import lax
from jax.experimental import pallas as pl
from jax.experimental.pallas import tpu as pltpu
from jax.sharding import PartitionSpec as P

D = 1024
EMB = 33
HIGH = lax.Precision.HIGHEST
eps = 1e-05
slow_rate = math.log(100.0) / 1.5
fast_rate = math.log(100.0) / 0.3
BOTH = ("rows", "seq")
F32 = jnp.float32
BF16 = jnp.bfloat16
VMEM_LIMIT = 56 * 1024 * 1024


def passed_along(value, axis, steps):
    count = lax.axis_size(axis)
    first, last = (max(0, -steps), min(count, count - steps))
    return lax.ppermute(value, axis, [(source, source + steps) for source in range(first, last)])


def layer_norm(values, gain, shift):
    center = values - jnp.mean(values, axis=-1, keepdims=True)
    spread = jnp.mean(center * center, axis=-1, keepdims=True)
    return center * lax.rsqrt(spread + eps) * gain + shift


def gelu_tanh(values):
    return jax.nn.gelu(values, approximate=True)


def features(length):
    steps = np.arange(length, dtype=np.float64)
    bands = (EMB - 1) // 2
    freqs = 0.0001 + np.arange(bands, dtype=np.float64) * ((bands - 1 - 0.0001) / (bands - 1))
    angles = (steps * (2.0 * math.pi / length))[:, None] * freqs[None, :]
    timeline = steps / (length - 1)
    table = np.concatenate([timeline[:, None], np.cos(angles), -np.sin(angles)], axis=1)
    return jnp.asarray(table.astype(np.float32)), jnp.asarray(timeline.astype(np.float32))


def filter_taps(w_one, b_one, w_two, b_two, w_three, first, length):
    feats, timeline = features(length)
    hidden = jnp.sin(jnp.dot(feats, w_one, precision=HIGH) + b_one)
    hidden = jnp.sin(jnp.dot(hidden, w_two, precision=HIGH) + b_two)
    raw_taps = jnp.dot(hidden, w_three, precision=HIGH)
    channels = (first + jnp.arange(w_three.shape[1], dtype=jnp.int32)).astype(F32)
    rates = slow_rate + channels * ((fast_rate - slow_rate) / (D - 1))
    return raw_taps * jnp.exp(-timeline[:, None] * rates[None, :])


def split16(values):
    high = values.astype(ml_dtypes.bfloat16)
    return high, (values - high.astype(np.float64)).astype(ml_dtypes.bfloat16)


def transform_tables(block):
    freq = np.arange(block)[:, None]
    time = np.arange(block)[None, :]
    angles = ((2 * freq + 1) * time % (4 * block)) * (math.pi / (2 * block))
    ahead = np.concatenate([np.cos(angles), -np.sin(angles)], axis=0)
    ahead_high, ahead_low = split16(ahead)
    back_high, back_low = split16(ahead.T / block)
    return tuple(jnp.asarray(t) for t in (ahead_high, ahead_low, back_high, back_low))


def piece_table(bounds, blocks, block):
    length = blocks * block
    edges = jnp.broadcast_to(jnp.arange(blocks, dtype=jnp.int32) * block, (bounds.shape[0], blocks))
    for cut in range(bounds.shape[1]):
        one = bounds[:, cut : cut + 1]
        low = jnp.concatenate([jnp.full_like(one, -1), edges], axis=1)
        high = jnp.concatenate([edges, jnp.full_like(one, length)], axis=1)
        edges = jnp.maximum(low, jnp.minimum(one, high))
    ends = jnp.concatenate([edges[:, 1:], jnp.full_like(edges[:, :1], length)], axis=1)
    index = jnp.minimum(edges // block, blocks - 1)
    start = jnp.max(
        jnp.where(bounds[:, :, None] <= edges[:, None, :], bounds[:, :, None], 0), axis=1
    )
    stop = jnp.min(
        jnp.where(bounds[:, :, None] > edges[:, None, :], bounds[:, :, None], length), axis=1
    )
    empty = ends <= edges
    earlier = jnp.where(empty, 0, index - start // block + 1)
    later = jnp.where(empty, 0, (stop - 1) // block - index + 1)
    return jnp.stack([edges, ends, index, earlier, later]).astype(jnp.int32)


def dot32(left, right):
    return jnp.dot(left, right, preferred_element_type=F32)


def split32(values):
    high = values.astype(BF16)
    return high, (values - high.astype(F32)).astype(BF16)


def wide_dot(high, low, values):
    top, rest = split32(values)
    return dot32(high, top) + dot32(high, rest) + dot32(low, top)


def alternating(rows, lanes):
    odd = lax.broadcasted_iota(jnp.int32, (rows, lanes), 0) % 2
    return 1.0 - 2.0 * odd.astype(F32)


def taps_spectrum_kernel(taps_ref, high_ref, low_ref, out_ref, own):
    blocks, block, lanes = taps_ref.shape
    for k in range(blocks):
        own[k] = wide_dot(high_ref[...], low_ref[...], taps_ref[k])
    sign = alternating(block, lanes)
    out_ref[0] = own[0]
    for k in range(1, blocks):
        out_ref[k, :block] = own[k, :block] - sign * own[k - 1, block:]
        out_ref[k, block:] = own[k, block:] + sign * own[k - 1, :block]


def taps_spectrum(taps, tables):
    blocks, block, lanes = taps.shape
    return pl.pallas_call(
        taps_spectrum_kernel,
        out_shape=jax.ShapeDtypeStruct((blocks, 2 * block, lanes), F32),
        scratch_shapes=[pltpu.VMEM((blocks, 2 * block, lanes), F32)],
        compiler_params=pltpu.CompilerParams(vmem_limit_bytes=VMEM_LIMIT),
        name="taps_spectrum",
    )(taps, tables[0], tables[1])


def piece_mask(table_ref, row, piece, block, lanes):
    at = table_ref[2, row, piece]
    spot = lax.broadcasted_iota(jnp.int32, (block, lanes), 0) + at * block
    return at, (spot >= table_ref[0, row, piece]) & (spot < table_ref[1, row, piece])


def piece_spectra(table_ref, series_ref, high_ref, low_ref, out_ref):
    blocks, rows, block, lanes = series_ref.shape
    for piece in range(out_ref.shape[0]):
        parts = []
        for row in range(rows):
            at, inside = piece_mask(table_ref, row, piece, block, lanes)
            values = series_ref[at, row].astype(F32)
            parts.append(jnp.where(inside, values, 0.0).astype(BF16))
        both = jnp.concatenate(parts, axis=1)
        out_ref[piece] = dot32(high_ref[...], both) + dot32(low_ref[...], both)


def couple(count, step, taps_ref, series_ref, piece, row, into_ref, conjugate):
    block = taps_ref.shape[1] // 2
    lanes = taps_ref.shape[2]
    lane = pl.ds(row * lanes, lanes)
    tile = 64

    def part(index, carry):
        real_rows = pl.ds(pl.multiple_of(index * tile, tile), tile)
        imag_rows = pl.ds(pl.multiple_of(block + index * tile, tile), tile)

        def add(k, total):
            real, imag = total
            tap_r, tap_i = taps_ref[k, real_rows, :], taps_ref[k, imag_rows, :]
            val_r = series_ref[piece + step * k, real_rows, lane]
            val_i = series_ref[piece + step * k, imag_rows, lane]
            if conjugate:
                return (
                    real + tap_r * val_r + tap_i * val_i,
                    imag + tap_r * val_i - tap_i * val_r,
                )
            return real + tap_r * val_r - tap_i * val_i, imag + tap_r * val_i + tap_i * val_r

        zero = jnp.zeros((tile, lanes), F32)
        real, imag = lax.fori_loop(0, count, add, (zero, zero))
        into_ref[real_rows, lane] = real
        into_ref[imag_rows, lane] = imag
        return carry

    lax.fori_loop(0, block // tile, part, 0)


def long_forward_kernel(
    table_ref, series_ref, taps_ref, skip_ref, ah_ref, al_ref, bh_ref, bl_ref, out_ref, spec, work
):
    blocks, rows, block, lanes = series_ref.shape
    piece_spectra(table_ref, series_ref, ah_ref, al_ref, spec)
    for piece in range(spec.shape[0]):
        for row in range(rows):
            couple(table_ref[3, row, piece], -1, taps_ref, spec, piece, row, work, False)
        result = wide_dot(bh_ref[...], bl_ref[...], work[...])
        for row in range(rows):
            at, inside = piece_mask(table_ref, row, piece, block, lanes)
            direct = skip_ref[...] * series_ref[at, row].astype(F32)
            value = result[:, row * lanes : (row + 1) * lanes] + direct
            kept = out_ref[at, row].astype(F32)
            out_ref[at, row] = jnp.where(inside, value, kept).astype(BF16)


def long_forward(table, series, taps_spec, skip, tables):
    blocks, rows, block, lanes = series.shape
    pieces = table.shape[2]
    smem = pl.BlockSpec(memory_space=pltpu.SMEM)
    vmem = pl.BlockSpec(memory_space=pltpu.VMEM)
    return pl.pallas_call(
        long_forward_kernel,
        in_specs=[smem] + [vmem] * 7,
        out_specs=vmem,
        out_shape=jax.ShapeDtypeStruct(series.shape, BF16),
        scratch_shapes=[
            pltpu.VMEM((pieces, 2 * block, rows * lanes), F32),
            pltpu.VMEM((2 * block, rows * lanes), F32),
        ],
        compiler_params=pltpu.CompilerParams(vmem_limit_bytes=VMEM_LIMIT),
        name="long_forward",
    )(table, series, taps_spec, skip, *tables)


def long_backward_kernel(
    table_ref,
    grad_ref,
    series_ref,
    taps_ref,
    skip_ref,
    ah_ref,
    al_ref,
    bh_ref,
    bl_ref,
    out_ref,
    taps_out_ref,
    skip_out_ref,
    spec,
    grad_spec,
    work,
    cross,
):
    blocks, rows, block, lanes = series_ref.shape
    pieces = spec.shape[0]
    piece_spectra(table_ref, grad_ref, ah_ref, al_ref, grad_spec)
    piece_spectra(table_ref, series_ref, ah_ref, al_ref, spec)
    for piece in range(pieces):
        for row in range(rows):
            couple(table_ref[4, row, piece], 1, taps_ref, grad_spec, piece, row, work, True)
        result = wide_dot(bh_ref[...], bl_ref[...], work[...])
        for row in range(rows):
            at, inside = piece_mask(table_ref, row, piece, block, lanes)
            direct = skip_ref[...] * grad_ref[at, row].astype(F32)
            value = result[:, row * lanes : (row + 1) * lanes] + direct
            kept = out_ref[at, row].astype(F32)
            out_ref[at, row] = jnp.where(inside, value, kept).astype(BF16)

    tile = 64
    for k in range(blocks):

        def part(index, carry, k=k):
            real_rows = pl.ds(pl.multiple_of(index * tile, tile), tile)
            imag_rows = pl.ds(pl.multiple_of(block + index * tile, tile), tile)
            total = (jnp.zeros((tile, lanes), F32), jnp.zeros((tile, lanes), F32))
            for row in range(rows):
                lane = pl.ds(row * lanes, lanes)

                def add(piece, total, row=row, lane=lane):
                    real, imag = total
                    weight = jnp.where(table_ref[3, row, piece] > k, 1.0, 0.0)
                    val_r = spec[piece - k, real_rows, lane]
                    val_i = spec[piece - k, imag_rows, lane]
                    out_r = grad_spec[piece, real_rows, lane] * weight
                    out_i = grad_spec[piece, imag_rows, lane] * weight
                    return (
                        real + val_r * out_r + val_i * out_i,
                        imag + val_r * out_i - val_i * out_r,
                    )

                total = lax.fori_loop(k, pieces, add, total)
            cross[k, real_rows, :] = total[0]
            cross[k, imag_rows, :] = total[1]
            return carry

        lax.fori_loop(0, block // tile, part, 0)
    sign = alternating(block, lanes)
    for k in range(blocks):
        if k + 1 < blocks:
            cross[k, :block] = cross[k, :block] + sign * cross[k + 1, block:]
            cross[k, block:] = cross[k, block:] - sign * cross[k + 1, :block]
        taps_out_ref[k] = wide_dot(bh_ref[...], bl_ref[...], cross[k])
    total = jnp.zeros((8, lanes), F32)
    for at in range(blocks):
        for row in range(rows):
            both = grad_ref[at, row].astype(F32) * series_ref[at, row].astype(F32)
            total = total + jnp.sum(both.reshape(block // 8, 8, lanes), axis=0)
    skip_out_ref[...] = jnp.sum(total, axis=0, keepdims=True)


def long_backward(table, grad, series, taps_spec, skip, tables):
    blocks, rows, block, lanes = series.shape
    pieces = table.shape[2]
    smem = pl.BlockSpec(memory_space=pltpu.SMEM)
    vmem = pl.BlockSpec(memory_space=pltpu.VMEM)
    return pl.pallas_call(
        long_backward_kernel,
        in_specs=[smem] + [vmem] * 8,
        out_specs=[vmem] * 3,
        out_shape=[
            jax.ShapeDtypeStruct(series.shape, BF16),
            jax.ShapeDtypeStruct((blocks, block, lanes), F32),
            jax.ShapeDtypeStruct((1, lanes), F32),
        ],
        scratch_shapes=[
            pltpu.VMEM((pieces, 2 * block, rows * lanes), F32),
            pltpu.VMEM((pieces, 2 * block, rows * lanes), F32),
            pltpu.VMEM((2 * block, rows * lanes), F32),
            pltpu.VMEM((blocks, 2 * block, lanes), F32),
        ],
        compiler_params=pltpu.CompilerParams(vmem_limit_bytes=VMEM_LIMIT),
        name="long_backward",
    )(table, grad, series, taps_spec, skip, *tables)


def document_masks(bounds, positions, length):
    lower = jnp.concatenate([jnp.zeros_like(bounds[:, :1]), bounds], axis=1)
    upper = jnp.concatenate([bounds, jnp.full_like(bounds[:, :1], length)], axis=1)
    inside = (positions[None, None, :] >= lower[:, :, None]) & (
        positions[None, None, :] < upper[:, :, None]
    )
    return inside.astype(F32)


def cos_sin(count_a, count_b, modulus):
    table = (
        jnp.arange(count_a, dtype=jnp.int32)[:, None]
        * jnp.arange(count_b, dtype=jnp.int32)[None, :]
        % modulus
    )
    angles = table.astype(F32) * (2.0 * math.pi / modulus)
    return (jnp.cos(angles), jnp.sin(angles))


def make_plan(blocks, block_len):
    outer = 2 * blocks
    cos_outer, sin_outer = cos_sin(outer, outer, outer)
    cos_twist, sin_twist = cos_sin(outer, block_len, outer * block_len)
    cos_inner, sin_inner = cos_sin(block_len, block_len, block_len)
    return (blocks, block_len, cos_outer, sin_outer, cos_twist, sin_twist, cos_inner, sin_inner)


def right_mul(left, table):
    return jnp.einsum("...km,mj->...kj", left, table, precision=HIGH)


def spectrum(series, plan):
    blocks, block_len, cos_outer, sin_outer, cos_twist, sin_twist, cos_inner, sin_inner = plan
    folded = series.reshape(series.shape[:-1] + (blocks, block_len))
    real_a = jnp.einsum("kn,...nm->...km", cos_outer[:, :blocks], folded, precision=HIGH)
    imag_a = -jnp.einsum("kn,...nm->...km", sin_outer[:, :blocks], folded, precision=HIGH)
    real_t = real_a * cos_twist + imag_a * sin_twist
    imag_t = imag_a * cos_twist - real_a * sin_twist
    real_x = right_mul(real_t, cos_inner) + right_mul(imag_t, sin_inner)
    imag_x = right_mul(imag_t, cos_inner) - right_mul(real_t, sin_inner)
    return (real_x, imag_x)


def inverse(real_x, imag_x, plan):
    blocks, block_len, cos_outer, sin_outer, cos_twist, sin_twist, cos_inner, sin_inner = plan
    real_b = right_mul(real_x, cos_inner) - right_mul(imag_x, sin_inner)
    imag_b = right_mul(imag_x, cos_inner) + right_mul(real_x, sin_inner)
    real_u = real_b * cos_twist - imag_b * sin_twist
    imag_u = imag_b * cos_twist + real_b * sin_twist
    folded = jnp.einsum("nk,...km->...nm", cos_outer[:blocks], real_u, precision=HIGH) - jnp.einsum(
        "nk,...km->...nm", sin_outer[:blocks], imag_u, precision=HIGH
    )
    folded = folded * (1.0 / (2 * blocks * block_len))
    return folded.reshape(folded.shape[:-2] + (blocks * block_len,))


def by_channel(blocked):
    blocks, rows, block, lanes = blocked.shape
    return blocked.astype(F32).transpose(1, 3, 0, 2).reshape(rows, lanes, blocks * block)


def by_block(series, blocks):
    rows, lanes, length = series.shape
    return series.reshape(rows, lanes, blocks, length // blocks).transpose(2, 0, 3, 1).astype(BF16)


class WholeSpectra:
    def __init__(self, bounds, taps, skip):
        blocks, block, lanes = taps.shape
        self.blocks, self.plan = blocks, make_plan(blocks, block)
        length = blocks * block
        everywhere = jnp.arange(length, dtype=jnp.int32)
        self.masks = document_masks(bounds, everywhere, length)[:, :, None, :]
        self.skip = skip[0][None, :, None]
        self.taps_real, self.taps_imag = spectrum(taps.reshape(length, lanes).T, self.plan)

    def forward(self, series):
        carried = by_channel(series)
        self.carried = carried
        real, imag = spectrum(self.masks * carried[:, None], self.plan)
        self.spec = real, imag
        docs = inverse(
            real * self.taps_real - imag * self.taps_imag,
            real * self.taps_imag + imag * self.taps_real,
            self.plan,
        )
        conv = jnp.sum(self.masks * docs, axis=1) + self.skip * carried
        return by_block(conv, self.blocks)

    def backward(self, grad):
        g_long = by_channel(grad)
        spec_real, spec_imag = self.spec
        g_skip = jnp.sum(g_long * self.carried, axis=(0, 2))
        real, imag = spectrum(self.masks * g_long[:, None], self.plan)
        docs = inverse(
            self.taps_real * real + self.taps_imag * imag,
            self.taps_real * imag - self.taps_imag * real,
            self.plan,
        )
        g_carried = jnp.sum(self.masks * docs, axis=1) + self.skip * g_long
        cross_real = jnp.sum(real * spec_real + imag * spec_imag, axis=(0, 1))
        cross_imag = jnp.sum(imag * spec_real - real * spec_imag, axis=(0, 1))
        g_taps = inverse(cross_real, cross_imag, self.plan)
        return by_block(g_carried, self.blocks), g_taps.T, g_skip[None, :]


class BlockSpectra:
    def __init__(self, bounds, taps, skip):
        blocks, block, lanes = taps.shape
        self.tables = transform_tables(block)
        self.table = piece_table(bounds, blocks, block)
        self.skip = skip
        self.taps = taps_spectrum(taps, self.tables)

    def forward(self, series):
        self.series = series
        return long_forward(self.table, series, self.taps, self.skip, self.tables)

    def backward(self, grad):
        g_series, g_taps, g_skip = long_backward(
            self.table, grad, self.series, self.taps, self.skip, self.tables
        )
        return g_series, g_taps.reshape(-1, g_taps.shape[2]), g_skip


def device_index():
    return lax.axis_index("rows") * lax.axis_size("seq") + lax.axis_index("seq")


def device_bits():
    return int(math.log2(lax.axis_size("rows") * lax.axis_size("seq")))


def swapped(value, mask_of):
    count = lax.axis_size("rows") * lax.axis_size("seq")
    return lax.ppermute(value, BOTH, [(one, one ^ mask_of(one)) for one in range(count)])


def pick(array, index, axis):
    return lax.dynamic_index_in_dim(array, index, axis=axis, keepdims=False)


def added(kept, arrived, kind):
    return (kept.astype(F32) + arrived.astype(F32)).astype(kind)


def halved(pieces, bit, axis, kind):
    mine = (device_index() >> bit) & 1
    arrived = swapped(pick(pieces, 1 - mine, axis), lambda one: 1 << bit)
    return added(pick(pieces, mine, axis), arrived, kind)


def quartered(pieces, axis, kind):
    index = device_index()
    core, low, high = index & 1, (index >> 1) & 1, (index >> 2) & 1

    def two(low_bit, high_bit):
        return jnp.stack(
            [
                pick(pieces, jnp.where(core == 0, 2 * j + low_bit, 2 * high_bit + j), axis)
                for j in range(2)
            ],
            axis=axis,
        )

    arrived = swapped(two(1 - low, 1 - high), lambda one: 4 if one & 1 else 2)
    pieces = added(two(low, high), arrived, kind)
    mine = jnp.where(core == 0, high, low)
    arrived = swapped(pick(pieces, 1 - mine, axis), lambda one: 2 if one & 1 else 4)
    return added(pick(pieces, mine, axis), arrived, kind)


def scattered(pieces, kind):
    rest = pieces.shape[1:]
    bits = device_bits()
    pieces = quartered(pieces.reshape((-1, 4) + rest), 1, kind)
    for bit in range(3, bits):
        last = bit == bits - 1
        pieces = halved(pieces.reshape((-1, 2) + rest), bit, 1, F32 if last else kind)
    return pieces.reshape(rest)


def weight_gradient(first, second):
    tokens, width = first.shape
    shares = 1 << device_bits()
    share = width // shares
    core = device_index() & 1
    halves = first.reshape(tokens, shares // 2, 2, share).transpose(2, 0, 1, 3)
    halves = halves.reshape(2, tokens, width // 2)

    def product(which):
        return jnp.einsum(
            "ti,tj->ij", pick(halves, which, 0), second, preferred_element_type=F32
        )

    arrived = swapped(product(1 - core).astype(BF16), lambda one: 1)
    kept = added(product(core), arrived, BF16)
    return scattered(kept.reshape(shares // 2, share, second.shape[1]), BF16)


def small_scattered(vectors):
    pieces = halved(vectors.reshape(-1, 2, vectors.shape[1]), 0, 1, F32)
    return scattered(pieces, F32)


def summed(value, bits):
    for bit in bits:
        value = value + swapped(value, lambda one, bit=bit: 1 << bit)
    return value


def back_product(grad_low, weight):
    return jnp.einsum("tj,ij->ti", grad_low, weight, preferred_element_type=F32)


def per_device(
    tokens,
    cotangent,
    bounds,
    ln1_gain,
    ln1_bias,
    in_weight,
    in_bias,
    short_weight,
    short_bias,
    f1_weight,
    f1_bias,
    f2_weight,
    f2_bias,
    f3_weight,
    filter_skip,
    out_weight,
    out_bias,
    ln2_gain,
    ln2_bias,
    up_weight,
    up_bias,
    down_weight,
    down_bias,
):
    seq_count = lax.axis_size("seq")
    row_count, tok_count, width = tokens.shape
    flat_count = row_count * tok_count
    length = tok_count * seq_count
    lanes = f3_weight.shape[1]
    first_channel = lax.axis_index("seq") * lanes
    x_in = tokens.astype(F32).reshape(flat_count, width)
    n1, ln1_pull = jax.vjp(layer_norm, x_in, ln1_gain.astype(F32), ln1_bias.astype(F32))
    n1_low = n1.astype(BF16)
    proj = jnp.dot(n1_low, in_weight, preferred_element_type=F32) + in_bias.astype(F32)
    proj_low = proj.astype(BF16).reshape(row_count, tok_count, 3 * width)
    here = lax.axis_index("seq") * tok_count + jnp.arange(tok_count, dtype=jnp.int32)
    starts = jnp.max(
        jnp.where(bounds[:, :, None] <= here[None, None, :], bounds[:, :, None], 0), axis=1
    )
    keep_one = (here[None, :] - 1 >= starts).astype(F32)[:, :, None]
    keep_two = (here[None, :] - 2 >= starts).astype(F32)[:, :, None]
    rim = passed_along(proj_low[:, tok_count - 2 :, :], "seq", 1)
    extended = jnp.concatenate([rim, proj_low], axis=1).astype(F32)
    current = extended[:, 2:, :]
    before_one = extended[:, 1:-1, :]
    before_two = extended[:, :-2, :]
    taps_short = short_weight.astype(F32)
    shorted = (
        taps_short[0] * current
        + keep_one * taps_short[1] * before_one
        + keep_two * taps_short[2] * before_two
        + short_bias.astype(F32)
    )
    gate_out = shorted[:, :, :width]
    gate_in = shorted[:, :, width : 2 * width]
    values = shorted[:, :, 2 * width :]
    carried_low = (gate_in * values).astype(BF16)

    def to_channels(array):
        array = array.reshape(row_count, tok_count, seq_count, lanes).transpose(2, 0, 1, 3)
        return lax.all_to_all(array, "seq", split_axis=0, concat_axis=0, tiled=True)

    def to_positions(array):
        array = lax.all_to_all(array, "seq", split_axis=0, concat_axis=0, tiled=True)
        return array.transpose(1, 2, 0, 3).reshape(row_count, tok_count, width)

    carried = to_channels(carried_low)

    def make_taps(w_one, b_one, w_two, b_two, w_three):
        return filter_taps(w_one, b_one, w_two, b_two, w_three, first_channel, length)

    taps, filter_pull = jax.vjp(
        make_taps,
        f1_weight.astype(F32),
        f1_bias.astype(F32),
        f2_weight.astype(F32),
        f2_bias.astype(F32),
        f3_weight.astype(F32),
    )
    long_filter = (BlockSpectra if lanes % 128 == 0 else WholeSpectra)(
        bounds, taps.reshape(seq_count, tok_count, lanes), filter_skip.astype(F32)[None, :]
    )
    long_low = long_filter.forward(carried)
    long_seq = to_positions(long_low).astype(F32)
    mixed_low = (gate_out * long_seq).astype(BF16).reshape(flat_count, width)
    branch = jnp.dot(mixed_low, out_weight, preferred_element_type=F32) + out_bias.astype(F32)
    resid = x_in + branch
    n2, ln2_pull = jax.vjp(layer_norm, resid, ln2_gain.astype(F32), ln2_bias.astype(F32))
    n2_low = n2.astype(BF16)
    pre = jnp.dot(n2_low, up_weight, preferred_element_type=F32) + up_bias.astype(F32)
    act, gelu_pull = jax.vjp(gelu_tanh, pre)
    act_low = act.astype(BF16)
    result = (
        resid
        + jnp.dot(act_low, down_weight, preferred_element_type=F32)
        + down_bias.astype(F32)
    )
    output = result.astype(BF16).reshape(row_count, tok_count, width)
    grad_low = cotangent.reshape(flat_count, width)
    grad_float = grad_low.astype(F32)
    g_down_w = weight_gradient(act_low, grad_low)
    g_down_b = jnp.sum(grad_float, axis=0)
    g_act = back_product(grad_low, down_weight)
    (g_pre,) = gelu_pull(g_act)
    g_pre_low = g_pre.astype(BF16)
    g_up_w = weight_gradient(n2_low, g_pre_low)
    g_up_b = jnp.sum(g_pre_low.astype(F32), axis=0)
    g_n2 = back_product(g_pre_low, up_weight)
    g_resid_part, g_ln2_gain, g_ln2_bias = ln2_pull(g_n2)
    g_resid = grad_float + g_resid_part
    g_branch_low = g_resid.astype(BF16)
    g_out_w = weight_gradient(mixed_low, g_branch_low)
    g_out_b = jnp.sum(g_branch_low.astype(F32), axis=0)
    g_mixed = back_product(g_branch_low, out_weight).reshape(row_count, tok_count, width)
    g_gate_out = g_mixed * long_seq
    g_long_low = (g_mixed * gate_out).astype(BF16)
    g_carried_low, g_taps, g_skip = long_filter.backward(to_channels(g_long_low))
    g_f1_w, g_f1_b, g_f2_w, g_f2_b, g_f3_w = filter_pull(g_taps)
    g_carried_seq = to_positions(g_carried_low).astype(F32)
    g_shorted = jnp.concatenate(
        [g_gate_out, g_carried_seq * values, g_carried_seq * gate_in], axis=-1
    )
    lead_one = keep_one * g_shorted
    lead_two = keep_two * g_shorted
    ahead = passed_along(
        jnp.concatenate([lead_one[:, :2], lead_two[:, :2]], axis=1).astype(BF16), "seq", -1
    ).astype(F32)
    after_one = jnp.concatenate([lead_one[:, 1:], ahead[:, :1]], axis=1)
    after_two = jnp.concatenate([lead_two[:, 2:], ahead[:, 2:4]], axis=1)
    g_proj = taps_short[0] * g_shorted + taps_short[1] * after_one + taps_short[2] * after_two
    g_short_w = jnp.stack(
        [
            jnp.sum(g_shorted * current, axis=(0, 1)),
            jnp.sum(lead_one * before_one, axis=(0, 1)),
            jnp.sum(lead_two * before_two, axis=(0, 1)),
        ],
        axis=0,
    )
    g_short_b = jnp.sum(g_shorted, axis=(0, 1))
    g_proj_low = g_proj.astype(BF16).reshape(flat_count, 3 * width)
    g_in_w = weight_gradient(n1_low, g_proj_low)
    g_in_b = jnp.sum(g_proj_low.astype(F32), axis=0)
    g_n1 = back_product(g_proj_low, in_weight)
    g_x_part, g_ln1_gain, g_ln1_bias = ln1_pull(g_n1)
    grad_tokens = (g_resid + g_x_part).reshape(row_count, tok_count, width)

    def lined(parts):
        flat = jnp.concatenate([part.reshape(-1) for part in parts])
        return jnp.pad(flat, (0, -flat.shape[0] % 128)).reshape(-1, 128)

    net = lined((g_f1_w, g_f1_b, g_f2_w, g_f2_b))
    net_rows = net.shape[0]
    own = lined((g_f3_w, g_skip))
    bits = device_bits()
    seq_bits = int(math.log2(seq_count))
    joint = summed(jnp.concatenate([net, own]), range(seq_bits, bits))
    net = summed(joint[:net_rows], range(seq_bits)).reshape(-1)
    own = joint[net_rows:].reshape(-1)
    g_f1_w, g_f1_b, g_f2_w, g_f2_b = (
        part.reshape(like.shape)
        for part, like in zip(
            jnp.split(net, np.cumsum([f1_weight.size, f1_bias.size, f2_weight.size, f2_bias.size])),
            (f1_weight, f1_bias, f2_weight, f2_bias),
        )
    )
    g_f3_w = own[: f3_weight.size].reshape(f3_weight.shape)
    g_skip = own[f3_weight.size : f3_weight.size + lanes]

    shares = 1 << bits
    vectors = (g_ln2_gain, g_ln2_bias, g_up_b, g_down_b, g_out_b)
    vectors += (g_ln1_gain, g_ln1_bias, g_in_b, g_short_b) + tuple(g_short_w)
    rows = jnp.concatenate([v.reshape(shares, -1) for v in vectors], axis=1)
    sums = small_scattered(rows)
    cuts = np.cumsum([v.shape[0] // shares for v in vectors])[:-1]
    (
        g_ln2_gain,
        g_ln2_bias,
        g_up_b,
        g_down_b,
        g_out_b,
        g_ln1_gain,
        g_ln1_bias,
        g_in_b,
        g_short_b,
        *g_short_w,
    ) = jnp.split(sums, cuts)
    return (
        output,
        grad_tokens,
        g_ln1_gain,
        g_ln1_bias,
        g_in_w,
        g_in_b,
        jnp.stack(g_short_w),
        g_short_b,
        g_f1_w,
        g_f1_b,
        g_f2_w,
        g_f2_b,
        g_f3_w,
        g_skip,
        g_out_w,
        g_out_b,
        g_ln2_gain,
        g_ln2_bias,
        g_up_w,
        g_up_b,
        g_down_w,
        g_down_b,
    )


def solution(mesh):
    return jax.shard_map(
        per_device,
        mesh=mesh,
        in_specs=(
            P("rows", "seq", None),
            P("rows", "seq", None),
            P("rows", None),
            P(),
            P(),
            P(),
            P(),
            P(),
            P(),
            P(),
            P(),
            P(),
            P(),
            P(None, "seq"),
            P("seq"),
            P(),
            P(),
            P(),
            P(),
            P(),
            P(),
            P(),
            P(),
        ),
        out_specs=(
            P("rows", "seq", None),
            P("rows", "seq", None),
            P(("rows", "seq")),
            P(("rows", "seq")),
            P(("rows", "seq"), None),
            P(("rows", "seq")),
            P(None, ("rows", "seq")),
            P(("rows", "seq")),
            P(),
            P(),
            P(),
            P(),
            P(None, "seq"),
            P("seq"),
            P(("rows", "seq"), None),
            P(("rows", "seq")),
            P(("rows", "seq")),
            P(("rows", "seq")),
            P(("rows", "seq"), None),
            P(("rows", "seq")),
            P(("rows", "seq"), None),
            P(("rows", "seq")),
        ),
        check_vma=False,
    )
```

```python
import functools
import math

import jax
import jax.numpy as jnp
import ml_dtypes
import numpy as np
from jax import lax
from jax.experimental import pallas as pl
from jax.experimental.pallas import tpu as pltpu
from jax.sharding import PartitionSpec as P

D = 1024
EMB = 33
HIGH = lax.Precision.HIGHEST
eps = 1e-05
slow_rate = math.log(100.0) / 1.5
fast_rate = math.log(100.0) / 0.3
BOTH = ("rows", "seq")
F32 = jnp.float32
BF16 = jnp.bfloat16
VMEM_MIB = 58
LITTLE = pl.CostEstimate(flops=1, bytes_accessed=1, transcendentals=0)
MUCH = pl.CostEstimate(flops=5 * 10**10, bytes_accessed=2 * 10**8, transcendentals=0)


def passed_along(value, axis, steps):
    count = lax.axis_size(axis)
    first, last = (max(0, -steps), min(count, count - steps))
    return lax.ppermute(value, axis, [(source, source + steps) for source in range(first, last)])


def layer_norm(values, gain, shift):
    center = values - jnp.mean(values, axis=-1, keepdims=True)
    spread = jnp.mean(center * center, axis=-1, keepdims=True)
    return center * lax.rsqrt(spread + eps) * gain + shift


def gelu_tanh(values):
    return jax.nn.gelu(values, approximate=True)


def features(length):
    steps = np.arange(length, dtype=np.float64)
    bands = (EMB - 1) // 2
    freqs = 0.0001 + np.arange(bands, dtype=np.float64) * ((bands - 1 - 0.0001) / (bands - 1))
    angles = (steps * (2.0 * math.pi / length))[:, None] * freqs[None, :]
    timeline = steps / (length - 1)
    table = np.concatenate([timeline[:, None], np.cos(angles), -np.sin(angles)], axis=1)
    return jnp.asarray(table.astype(np.float32)), jnp.asarray(timeline.astype(np.float32))


def filter_taps(w_one, b_one, w_two, b_two, w_three, first, length):
    feats, timeline = features(length)
    hidden = jnp.sin(jnp.dot(feats, w_one, precision=HIGH) + b_one)
    hidden = jnp.sin(jnp.dot(hidden, w_two, precision=HIGH) + b_two)
    raw_taps = jnp.dot(hidden, w_three, precision=HIGH)
    channels = (first + jnp.arange(w_three.shape[1], dtype=jnp.int32)).astype(F32)
    rates = slow_rate + channels * ((fast_rate - slow_rate) / (D - 1))
    return raw_taps * jnp.exp(-timeline[:, None] * rates[None, :])


def filter_network(w_one, b_one, w_two, b_two, w_three, first, length):
    feats, timeline = features(length)
    one = jnp.dot(feats, w_one, precision=HIGH) + b_one
    hidden_one = jnp.sin(one)
    two = jnp.dot(hidden_one, w_two, precision=HIGH) + b_two
    hidden_two = jnp.sin(two)
    raw_taps = jnp.dot(hidden_two, w_three, precision=HIGH)
    channels = (first + jnp.arange(w_three.shape[1], dtype=jnp.int32)).astype(F32)
    rates = slow_rate + channels * ((fast_rate - slow_rate) / (D - 1))
    taps = raw_taps * jnp.exp(-timeline[:, None] * rates[None, :])
    return taps, (feats, hidden_one, hidden_two, jnp.cos(one), jnp.cos(two))


def close_dot(left, right, dims):
    def one(a, b):
        return lax.dot_general(a, b, (dims, ((), ())), preferred_element_type=F32)

    (a, a_rest), (b, b_rest) = split32(left), split32(right)
    return one(a, b) + one(a, b_rest) + one(a_rest, b)


def line_up(out_ref, count, parts):
    line = 0
    for ref, lead, rows in parts:
        width = ref.shape[-1]
        share = rows * width // count // 128
        for z in range(count):
            for k in range(share):
                at = (z * share + k) * 128
                row, lane = at // width, at % width
                index = ((row,) if rows > 1 else ()) + tuple(lead)
                value = ref[index + (slice(lane, lane + 128),)]
                out_ref[z, line + k : line + k + 1] = value.reshape(1, 128)
        line += share


def filter_backward_kernel(
    first_ref,
    row_ref,
    grad_ref,
    feats_ref,
    h1_ref,
    h2_ref,
    c1_ref,
    c2_ref,
    w2_ref,
    w3_ref,
    skip_ref,
    middle_ref,
    up_ref,
    norm_ref,
    short_ref,
    outs,
    lines,
    out_ref,
):
    lines[...] = jnp.zeros_like(lines)
    parts = [(middle_ref, (k,), 1) for k in range(4)] + [(norm_ref, (k,), 1) for k in range(2)]
    parts += [(up_ref, (0,), 1)] + [(short_ref, (k,), 3) for k in range(5)]
    line_up(lines, len(outs), parts)
    length, lanes = grad_ref.shape
    units = h1_ref.shape[1]
    bands = feats_ref.shape[1]
    spot = lax.broadcasted_iota(jnp.int32, (length, lanes), 0).astype(F32) * (1.0 / (length - 1))
    channel = (lax.broadcasted_iota(jnp.int32, (1, lanes), 1) + first_ref[0]).astype(F32)
    rates = slow_rate + channel * ((fast_rate - slow_rate) / (D - 1))
    inner = grad_ref[...] * jnp.exp(-spot * rates)
    over_time, over_last = ((0,), (0,)), ((1,), (1,))
    out_ref[...] = jnp.zeros_like(out_ref)
    out_ref[:units] = close_dot(h2_ref[...], inner, over_time)
    out_ref[units : units + 1] = skip_ref[...]
    two = close_dot(inner, w3_ref[...].astype(F32), over_last) * c2_ref[...]
    one = close_dot(two, w2_ref[...].astype(F32), over_last) * c1_ref[...]
    below = units + 8
    out_ref[below : below + units, :units] = close_dot(h1_ref[...], two, over_time)
    out_ref[below : below + bands, units:] = close_dot(feats_ref[...], one, over_time)
    out_ref[below + bands : below + bands + 1, units:] = jnp.sum(one, axis=0, keepdims=True)
    out_ref[below + bands + 1 : below + bands + 2, units:] = jnp.sum(two, axis=0, keepdims=True)
    for k, payload in enumerate(outs):
        payload[: 2 * units + 8] = out_ref[...]
        payload[2 * units + 8 :] = lines[row_ref[0] ^ k]


LINES = 56


def filter_backward(first, row, count, g_taps, kept, w_two, w_three, g_skip, sums, ready):
    feats, h1, h2, c1, c2 = kept
    units, lanes = w_three.shape
    vmem = pl.BlockSpec(memory_space=pltpu.VMEM)
    height = 2 * units + 8

    def kernel(*refs):
        outs, scratch = refs[15 + len(ready) : -2], refs[-2:]
        filter_backward_kernel(*refs[:15], outs, *scratch)

    return pl.pallas_call(
        kernel,
        in_specs=[smem()] * 2 + [vmem] * 13 + [pl.BlockSpec(memory_space=pl.ANY)] * len(ready),
        out_specs=[vmem] * count,
        out_shape=[jax.ShapeDtypeStruct((height + LINES, lanes), F32)] * count,
        scratch_shapes=[
            pltpu.VMEM((count, LINES, lanes), F32),
            pltpu.VMEM((height, lanes), F32),
        ],
        compiler_params=pltpu.CompilerParams(vmem_limit_bytes=VMEM_MIB * 2**20),
        cost_estimate=MUCH,
        name="filter_backward",
    )(first, row, g_taps, feats, h1, h2, c1, c2, w_two, w_three, g_skip, *sums, *ready)


def split16(values):
    high = values.astype(ml_dtypes.bfloat16)
    return high, (values - high.astype(np.float64)).astype(ml_dtypes.bfloat16)


def transform_tables(block):
    freq = np.arange(block)[:, None]
    time = np.arange(block)[None, :]
    angles = ((2 * freq + 1) * time % (4 * block)) * (math.pi / (2 * block))
    ahead = np.concatenate([np.cos(angles), -np.sin(angles)], axis=0)
    ahead_high, ahead_low = split16(ahead)
    back_high, back_low = split16(ahead.T / block)
    return tuple(jnp.asarray(t) for t in (ahead_high, ahead_low, back_high, back_low))


def piece_table(bounds, blocks, block):
    length = blocks * block
    edges = jnp.broadcast_to(jnp.arange(blocks, dtype=jnp.int32) * block, (bounds.shape[0], blocks))
    for cut in range(bounds.shape[1]):
        one = bounds[:, cut : cut + 1]
        low = jnp.concatenate([jnp.full_like(one, -1), edges], axis=1)
        high = jnp.concatenate([edges, jnp.full_like(one, length)], axis=1)
        edges = jnp.maximum(low, jnp.minimum(one, high))
    ends = jnp.concatenate([edges[:, 1:], jnp.full_like(edges[:, :1], length)], axis=1)
    index = jnp.minimum(edges // block, blocks - 1)
    start = jnp.max(
        jnp.where(bounds[:, :, None] <= edges[:, None, :], bounds[:, :, None], 0), axis=1
    )
    stop = jnp.min(
        jnp.where(bounds[:, :, None] > edges[:, None, :], bounds[:, :, None], length), axis=1
    )
    empty = ends <= edges
    earlier = jnp.where(empty, 0, index - start // block + 1)
    later = jnp.where(empty, 0, (stop - 1) // block - index + 1)
    return jnp.stack([edges, ends, index, earlier, later]).astype(jnp.int32)


def dot32(left, right):
    return jnp.dot(left, right, preferred_element_type=F32)


def split32(values):
    high = values.astype(BF16)
    return high, (values - high.astype(F32)).astype(BF16)


def wide_dot(high, low, values):
    top, rest = split32(values)
    return dot32(high, top) + dot32(high, rest) + dot32(low, top)


def alternating(rows, lanes):
    odd = lax.broadcasted_iota(jnp.int32, (rows, lanes), 0) % 2
    return 1.0 - 2.0 * odd.astype(F32)


def taps_spectrum_kernel(taps_ref, high_ref, low_ref, out_ref, own):
    blocks, block, lanes = taps_ref.shape
    for k in range(blocks):
        own[k] = wide_dot(high_ref[...], low_ref[...], taps_ref[k])
    sign = alternating(block, lanes)
    out_ref[0] = own[0]
    for k in range(1, blocks):
        out_ref[k, :block] = own[k, :block] - sign * own[k - 1, block:]
        out_ref[k, block:] = own[k, block:] + sign * own[k - 1, :block]


def taps_spectrum(taps, tables):
    blocks, block, lanes = taps.shape
    return pl.pallas_call(
        taps_spectrum_kernel,
        out_shape=jax.ShapeDtypeStruct((blocks, 2 * block, lanes), F32),
        scratch_shapes=[pltpu.VMEM((blocks, 2 * block, lanes), F32)],
        compiler_params=pltpu.CompilerParams(vmem_limit_bytes=VMEM_MIB * 2**20),
        cost_estimate=LITTLE,
        name="taps_spectrum",
    )(taps, tables[0], tables[1])


def piece_mask(table_ref, row, piece, block, lanes):
    at = table_ref[2, row, piece]
    spot = lax.broadcasted_iota(jnp.int32, (block, lanes), 0) + at * block
    return at, (spot >= table_ref[0, row, piece]) & (spot < table_ref[1, row, piece])


def piece_spectra(table_ref, series_ref, ahead_ref, out_ref):
    blocks, rows, block, lanes = series_ref.shape
    for piece in range(out_ref.shape[0]):
        parts = []
        for row in range(rows):
            at, inside = piece_mask(table_ref, row, piece, block, lanes)
            values = series_ref[at, row].astype(F32)
            parts.append(jnp.where(inside, values, 0.0).astype(BF16))
        out_ref[piece] = dot32(ahead_ref[...], jnp.concatenate(parts, axis=1))


def each_piece(table_ref, which, pieces, rows, lanes, blocks, visit):
    def body(index, carry):
        piece, row = index // rows, index % rows
        lane = pl.ds(pl.multiple_of(row * lanes, lanes), lanes)
        found = table_ref[which, row, piece]
        for count in range(blocks + 1):

            @pl.when(found == count)
            def _(count=count):
                visit(piece, lane, count)

        return carry

    lax.fori_loop(0, pieces * rows, body, 0)


def halves_of(block, tile):
    for begin in range(0, block, tile):
        yield pl.ds(begin, tile), pl.ds(block + begin, tile)


def couple(table_ref, step, taps_ref, series_ref, into_ref):
    blocks, double, lanes = taps_ref.shape
    block = double // 2
    pieces, _, both = series_ref.shape

    def visit(piece, lane, count):
        for real_rows, imag_rows in halves_of(block, 32):
            real = imag = jnp.zeros((32, lanes), F32)
            for k in range(count):
                tap_r, tap_i = taps_ref[k, real_rows, :], taps_ref[k, imag_rows, :]
                val_r = series_ref[piece + step * k, real_rows, lane]
                val_i = series_ref[piece + step * k, imag_rows, lane]
                if step > 0:
                    real = real + (tap_r * val_r + tap_i * val_i)
                    imag = imag + (tap_r * val_i - tap_i * val_r)
                else:
                    real = real + (tap_r * val_r - tap_i * val_i)
                    imag = imag + (tap_r * val_i + tap_i * val_r)
            into_ref[piece, real_rows, lane] = real
            into_ref[piece, imag_rows, lane] = imag

    each_piece(table_ref, 3 if step < 0 else 4, pieces, both // lanes, lanes, blocks, visit)


def correlate(table_ref, series_ref, grad_ref, into_ref):
    blocks, double, lanes = into_ref.shape
    block = double // 2
    pieces, _, both = series_ref.shape
    into_ref[...] = jnp.zeros_like(into_ref)

    def visit(piece, lane, count):
        for real_rows, imag_rows in halves_of(block, 32):
            if count:
                out_r, out_i = grad_ref[piece, real_rows, lane], grad_ref[piece, imag_rows, lane]
            for k in range(count):
                val_r = series_ref[piece - k, real_rows, lane]
                val_i = series_ref[piece - k, imag_rows, lane]
                into_ref[k, real_rows, :] += val_r * out_r + val_i * out_i
                into_ref[k, imag_rows, :] += val_r * out_i - val_i * out_r

    each_piece(table_ref, 3, pieces, both // lanes, lanes, blocks, visit)


def write_pieces(table_ref, work, back_ref, series_ref, skip_ref, out_ref):
    blocks, rows, block, lanes = series_ref.shape
    for piece in range(work.shape[0]):
        result = dot32(back_ref[...], work[piece].astype(BF16))
        for row in range(rows):
            at, inside = piece_mask(table_ref, row, piece, block, lanes)
            direct = skip_ref[...].astype(F32).reshape(1, -1) * series_ref[at, row].astype(F32)
            value = result[:, row * lanes : (row + 1) * lanes] + direct
            kept = out_ref[at, row, :block].astype(F32)
            out_ref[at, row, :block] = jnp.where(inside, value, kept).astype(BF16)


def long_forward_kernel(
    table_ref, series_ref, taps_ref, skip_ref, ahead_ref, back_ref, out_ref, spec, work
):
    piece_spectra(table_ref, series_ref, ahead_ref, spec)
    couple(table_ref, -1, taps_ref, spec, work)
    write_pieces(table_ref, work, back_ref, series_ref, skip_ref, out_ref)


def long_forward(table, series, taps_spec, skip, tables):
    blocks, rows, block, lanes = series.shape
    pieces = table.shape[2]
    vmem = pl.BlockSpec(memory_space=pltpu.VMEM)
    return pl.pallas_call(
        long_forward_kernel,
        in_specs=[smem()] + [vmem] * 5,
        out_specs=vmem,
        out_shape=jax.ShapeDtypeStruct(series.shape, BF16),
        scratch_shapes=[pltpu.VMEM((pieces, 2 * block, rows * lanes), F32)] * 2,
        compiler_params=pltpu.CompilerParams(vmem_limit_bytes=VMEM_MIB * 2**20),
        cost_estimate=MUCH,
        name="long_forward",
    )(table, series, taps_spec, skip, tables[0], tables[2])


def long_backward_kernel(
    table_ref, grad_ref, series_ref, taps_ref, skip_ref, ahead_ref, back_ref, *others
):
    out_ref, taps_out_ref, skip_out_ref, token_out, spec, grad_spec, work, cross = others[-8:]
    token_out[0] = 0
    blocks, rows, block, lanes = series_ref.shape
    piece_spectra(table_ref, grad_ref, ahead_ref, grad_spec)
    couple(table_ref, 1, taps_ref, grad_spec, work)
    write_pieces(table_ref, work, back_ref, grad_ref, skip_ref, out_ref)
    for at in range(blocks):
        for row in range(rows):
            if at + 1 < blocks:
                out_ref[at, row, block:] = out_ref[at + 1, row, : out_ref.shape[2] - block]
            else:
                out_ref[at, row, block:] = jnp.zeros_like(out_ref[at, row, block:])
    piece_spectra(table_ref, series_ref, ahead_ref, spec)
    correlate(table_ref, spec, grad_spec, cross)
    sign = alternating(block, lanes)
    for k in range(blocks):
        if k + 1 < blocks:
            cross[k, :block] = cross[k, :block] + sign * cross[k + 1, block:]
            cross[k, block:] = cross[k, block:] - sign * cross[k + 1, :block]
        taps_out_ref[k] = dot32(back_ref[...], cross[k].astype(BF16))
    total = jnp.zeros((8, lanes), F32)
    for at in range(blocks):
        for row in range(rows):
            both = grad_ref[at, row].astype(F32) * series_ref[at, row].astype(F32)
            total = total + jnp.sum(both.reshape(block // 8, 8, lanes), axis=0)
    skip_out_ref[...] = jnp.sum(total, axis=0, keepdims=True)


def long_backward(table, grad, series, taps_spec, skip, tables, ready):
    blocks, rows, block, lanes = series.shape
    pieces = table.shape[2]
    vmem = pl.BlockSpec(memory_space=pltpu.VMEM)
    return pl.pallas_call(
        long_backward_kernel,
        in_specs=[smem()] + [vmem] * 6 + [pl.BlockSpec(memory_space=pl.ANY)] * len(ready),
        out_specs=[vmem] * 3 + [smem()],
        out_shape=[
            jax.ShapeDtypeStruct((blocks, rows, block + HALO, lanes), BF16),
            jax.ShapeDtypeStruct((blocks, block, lanes), F32),
            jax.ShapeDtypeStruct((1, lanes), F32),
            jax.ShapeDtypeStruct((1,), jnp.int32),
        ],
        scratch_shapes=[pltpu.VMEM((pieces, 2 * block, rows * lanes), F32)] * 3
        + [pltpu.VMEM((blocks, 2 * block, lanes), F32)],
        compiler_params=pltpu.CompilerParams(vmem_limit_bytes=VMEM_MIB * 2**20),
        cost_estimate=MUCH,
        name="long_backward",
    )(table, grad, series, taps_spec, skip, tables[0], tables[2], *ready)


def document_masks(bounds, positions, length):
    lower = jnp.concatenate([jnp.zeros_like(bounds[:, :1]), bounds], axis=1)
    upper = jnp.concatenate([bounds, jnp.full_like(bounds[:, :1], length)], axis=1)
    inside = (positions[None, None, :] >= lower[:, :, None]) & (
        positions[None, None, :] < upper[:, :, None]
    )
    return inside.astype(F32)


def cos_sin(count_a, count_b, modulus):
    table = (
        jnp.arange(count_a, dtype=jnp.int32)[:, None]
        * jnp.arange(count_b, dtype=jnp.int32)[None, :]
        % modulus
    )
    angles = table.astype(F32) * (2.0 * math.pi / modulus)
    return (jnp.cos(angles), jnp.sin(angles))


def make_plan(blocks, block_len):
    outer = 2 * blocks
    cos_outer, sin_outer = cos_sin(outer, outer, outer)
    cos_twist, sin_twist = cos_sin(outer, block_len, outer * block_len)
    cos_inner, sin_inner = cos_sin(block_len, block_len, block_len)
    return (blocks, block_len, cos_outer, sin_outer, cos_twist, sin_twist, cos_inner, sin_inner)


def right_mul(left, table):
    return jnp.einsum("...km,mj->...kj", left, table, precision=HIGH)


def spectrum(series, plan):
    blocks, block_len, cos_outer, sin_outer, cos_twist, sin_twist, cos_inner, sin_inner = plan
    folded = series.reshape(series.shape[:-1] + (blocks, block_len))
    real_a = jnp.einsum("kn,...nm->...km", cos_outer[:, :blocks], folded, precision=HIGH)
    imag_a = -jnp.einsum("kn,...nm->...km", sin_outer[:, :blocks], folded, precision=HIGH)
    real_t = real_a * cos_twist + imag_a * sin_twist
    imag_t = imag_a * cos_twist - real_a * sin_twist
    real_x = right_mul(real_t, cos_inner) + right_mul(imag_t, sin_inner)
    imag_x = right_mul(imag_t, cos_inner) - right_mul(real_t, sin_inner)
    return (real_x, imag_x)


def inverse(real_x, imag_x, plan):
    blocks, block_len, cos_outer, sin_outer, cos_twist, sin_twist, cos_inner, sin_inner = plan
    real_b = right_mul(real_x, cos_inner) - right_mul(imag_x, sin_inner)
    imag_b = right_mul(imag_x, cos_inner) + right_mul(real_x, sin_inner)
    real_u = real_b * cos_twist - imag_b * sin_twist
    imag_u = imag_b * cos_twist + real_b * sin_twist
    folded = jnp.einsum("nk,...km->...nm", cos_outer[:blocks], real_u, precision=HIGH) - jnp.einsum(
        "nk,...km->...nm", sin_outer[:blocks], imag_u, precision=HIGH
    )
    folded = folded * (1.0 / (2 * blocks * block_len))
    return folded.reshape(folded.shape[:-2] + (blocks * block_len,))


def by_channel(blocked):
    blocks, rows, block, lanes = blocked.shape
    return blocked.astype(F32).transpose(1, 3, 0, 2).reshape(rows, lanes, blocks * block)


def by_block(series, blocks):
    rows, lanes, length = series.shape
    return series.reshape(rows, lanes, blocks, length // blocks).transpose(2, 0, 3, 1).astype(BF16)


class WholeSpectra:
    def __init__(self, bounds, taps, skip):
        blocks, block, lanes = taps.shape
        self.blocks, self.plan = blocks, make_plan(blocks, block)
        length = blocks * block
        everywhere = jnp.arange(length, dtype=jnp.int32)
        self.masks = document_masks(bounds, everywhere, length)[:, :, None, :]
        self.skip = skip[0][None, :, None]
        self.taps_real, self.taps_imag = spectrum(taps.reshape(length, lanes).T, self.plan)

    def forward(self, series):
        carried = by_channel(series)
        self.carried = carried
        real, imag = spectrum(self.masks * carried[:, None], self.plan)
        self.spec = real, imag
        docs = inverse(
            real * self.taps_real - imag * self.taps_imag,
            real * self.taps_imag + imag * self.taps_real,
            self.plan,
        )
        conv = jnp.sum(self.masks * docs, axis=1) + self.skip * carried
        return by_block(conv, self.blocks)

    def backward(self, grad):
        g_long = by_channel(grad)
        spec_real, spec_imag = self.spec
        g_skip = jnp.sum(g_long * self.carried, axis=(0, 2))
        real, imag = spectrum(self.masks * g_long[:, None], self.plan)
        docs = inverse(
            self.taps_real * real + self.taps_imag * imag,
            self.taps_real * imag - self.taps_imag * real,
            self.plan,
        )
        g_carried = jnp.sum(self.masks * docs, axis=1) + self.skip * g_long
        cross_real = jnp.sum(real * spec_real + imag * spec_imag, axis=(0, 1))
        cross_imag = jnp.sum(imag * spec_real - real * spec_imag, axis=(0, 1))
        g_taps = inverse(cross_real, cross_imag, self.plan)
        return by_block(g_carried, self.blocks), g_taps.T, g_skip[None, :]


def device_index():
    return lax.axis_index("rows") * lax.axis_size("seq") + lax.axis_index("seq")


def device_bits():
    return int(math.log2(lax.axis_size("rows") * lax.axis_size("seq")))


def swapped(value, mask_of):
    count = lax.axis_size("rows") * lax.axis_size("seq")
    return lax.ppermute(value, BOTH, [(one, one ^ mask_of(one)) for one in range(count)])


def pick(array, index, axis):
    return lax.dynamic_index_in_dim(array, index, axis=axis, keepdims=False)


def added(kept, arrived, kind):
    return (kept.astype(F32) + arrived.astype(F32)).astype(kind)


def halved(pieces, bit, axis, kind):
    mine = (device_index() >> bit) & 1
    arrived = swapped(pick(pieces, 1 - mine, axis), lambda one: 1 << bit)
    return added(pick(pieces, mine, axis), arrived, kind)


def quartered(pieces, axis, kind):
    index = device_index()
    core, low, high = index & 1, (index >> 1) & 1, (index >> 2) & 1

    def two(low_bit, high_bit):
        return jnp.stack(
            [
                pick(pieces, jnp.where(core == 0, 2 * j + low_bit, 2 * high_bit + j), axis)
                for j in range(2)
            ],
            axis=axis,
        )

    arrived = swapped(two(1 - low, 1 - high), lambda one: 4 if one & 1 else 2)
    pieces = added(two(low, high), arrived, kind)
    mine = jnp.where(core == 0, high, low)
    arrived = swapped(pick(pieces, 1 - mine, axis), lambda one: 2 if one & 1 else 4)
    return added(pick(pieces, mine, axis), arrived, kind)


def scattered(pieces, kind):
    rest = pieces.shape[1:]
    bits = device_bits()
    pieces = quartered(pieces.reshape((-1, 4) + rest), 1, kind)
    for bit in range(3, bits):
        last = bit == bits - 1
        pieces = halved(pieces.reshape((-1, 2) + rest), bit, 1, F32 if last else kind)
    return pieces.reshape(rest)


def weight_gradient(first, second):
    tokens, width = first.shape
    shares = 1 << device_bits()
    share = width // shares
    core = device_index() & 1
    halves = first.reshape(tokens, shares // 2, 2, share).transpose(2, 0, 1, 3)
    halves = halves.reshape(2, tokens, width // 2)

    def product(which):
        return jnp.einsum(
            "ti,tj->ij", pick(halves, which, 0), second, preferred_element_type=F32
        )

    arrived = swapped(product(1 - core).astype(BF16), lambda one: 1)
    kept = added(product(core), arrived, BF16)
    return scattered(kept.reshape(shares // 2, share, second.shape[1]), BF16)


def small_scattered(vectors):
    pieces = halved(vectors.reshape(-1, 2, vectors.shape[1]), 0, 1, F32)
    return scattered(pieces, F32)


def summed(value, bits):
    for bit in bits:
        value = value + swapped(value, lambda one, bit=bit: 1 << bit)
    return value


def back_product(grad_low, weight):
    return jnp.einsum("tj,ij->ti", grad_low, weight, preferred_element_type=F32)


def plain_device(
    tokens,
    cotangent,
    bounds,
    ln1_gain,
    ln1_bias,
    in_weight,
    in_bias,
    short_weight,
    short_bias,
    f1_weight,
    f1_bias,
    f2_weight,
    f2_bias,
    f3_weight,
    filter_skip,
    out_weight,
    out_bias,
    ln2_gain,
    ln2_bias,
    up_weight,
    up_bias,
    down_weight,
    down_bias,
):
    seq_count = lax.axis_size("seq")
    row_count, tok_count, width = tokens.shape
    flat_count = row_count * tok_count
    length = tok_count * seq_count
    lanes = f3_weight.shape[1]
    first_channel = lax.axis_index("seq") * lanes
    x_in = tokens.astype(F32).reshape(flat_count, width)
    n1, ln1_pull = jax.vjp(layer_norm, x_in, ln1_gain.astype(F32), ln1_bias.astype(F32))
    n1_low = n1.astype(BF16)
    proj = jnp.dot(n1_low, in_weight, preferred_element_type=F32) + in_bias.astype(F32)
    proj_low = proj.astype(BF16).reshape(row_count, tok_count, 3 * width)
    here = lax.axis_index("seq") * tok_count + jnp.arange(tok_count, dtype=jnp.int32)
    starts = jnp.max(
        jnp.where(bounds[:, :, None] <= here[None, None, :], bounds[:, :, None], 0), axis=1
    )
    keep_one = (here[None, :] - 1 >= starts).astype(F32)[:, :, None]
    keep_two = (here[None, :] - 2 >= starts).astype(F32)[:, :, None]
    rim = passed_along(proj_low[:, tok_count - 2 :, :], "seq", 1)
    extended = jnp.concatenate([rim, proj_low], axis=1).astype(F32)
    current = extended[:, 2:, :]
    before_one = extended[:, 1:-1, :]
    before_two = extended[:, :-2, :]
    taps_short = short_weight.astype(F32)
    shorted = (
        taps_short[0] * current
        + keep_one * taps_short[1] * before_one
        + keep_two * taps_short[2] * before_two
        + short_bias.astype(F32)
    )
    gate_out = shorted[:, :, :width]
    gate_in = shorted[:, :, width : 2 * width]
    values = shorted[:, :, 2 * width :]
    carried_low = (gate_in * values).astype(BF16)

    def to_channels(array):
        array = array.reshape(row_count, tok_count, seq_count, lanes).transpose(2, 0, 1, 3)
        return lax.all_to_all(array, "seq", split_axis=0, concat_axis=0, tiled=True)

    def to_positions(array):
        array = lax.all_to_all(array, "seq", split_axis=0, concat_axis=0, tiled=True)
        return array.transpose(1, 2, 0, 3).reshape(row_count, tok_count, width)

    carried = to_channels(carried_low)

    def make_taps(w_one, b_one, w_two, b_two, w_three):
        return filter_taps(w_one, b_one, w_two, b_two, w_three, first_channel, length)

    taps, filter_pull = jax.vjp(
        make_taps,
        f1_weight.astype(F32),
        f1_bias.astype(F32),
        f2_weight.astype(F32),
        f2_bias.astype(F32),
        f3_weight.astype(F32),
    )
    long_filter = WholeSpectra(
        bounds, taps.reshape(seq_count, tok_count, lanes), filter_skip.astype(F32)[None, :]
    )
    long_low = long_filter.forward(carried)
    long_seq = to_positions(long_low).astype(F32)
    mixed_low = (gate_out * long_seq).astype(BF16).reshape(flat_count, width)
    branch = jnp.dot(mixed_low, out_weight, preferred_element_type=F32) + out_bias.astype(F32)
    resid = x_in + branch
    n2, ln2_pull = jax.vjp(layer_norm, resid, ln2_gain.astype(F32), ln2_bias.astype(F32))
    n2_low = n2.astype(BF16)
    pre = jnp.dot(n2_low, up_weight, preferred_element_type=F32) + up_bias.astype(F32)
    act, gelu_pull = jax.vjp(gelu_tanh, pre)
    act_low = act.astype(BF16)
    result = (
        resid
        + jnp.dot(act_low, down_weight, preferred_element_type=F32)
        + down_bias.astype(F32)
    )
    output = result.astype(BF16).reshape(row_count, tok_count, width)
    grad_low = cotangent.reshape(flat_count, width)
    grad_float = grad_low.astype(F32)
    g_down_w = weight_gradient(act_low, grad_low)
    g_down_b = jnp.sum(grad_float, axis=0)
    g_act = back_product(grad_low, down_weight)
    (g_pre,) = gelu_pull(g_act)
    g_pre_low = g_pre.astype(BF16)
    g_up_w = weight_gradient(n2_low, g_pre_low)
    g_up_b = jnp.sum(g_pre_low.astype(F32), axis=0)
    g_n2 = back_product(g_pre_low, up_weight)
    g_resid_part, g_ln2_gain, g_ln2_bias = ln2_pull(g_n2)
    g_resid = grad_float + g_resid_part
    g_branch_low = g_resid.astype(BF16)
    g_out_w = weight_gradient(mixed_low, g_branch_low)
    g_out_b = jnp.sum(g_branch_low.astype(F32), axis=0)
    g_mixed = back_product(g_branch_low, out_weight).reshape(row_count, tok_count, width)
    g_gate_out = g_mixed * long_seq
    g_long_low = (g_mixed * gate_out).astype(BF16)
    g_carried_low, g_taps, g_skip = long_filter.backward(to_channels(g_long_low))
    g_f1_w, g_f1_b, g_f2_w, g_f2_b, g_f3_w = filter_pull(g_taps)
    g_carried_seq = to_positions(g_carried_low).astype(F32)
    g_shorted = jnp.concatenate(
        [g_gate_out, g_carried_seq * values, g_carried_seq * gate_in], axis=-1
    )
    lead_one = keep_one * g_shorted
    lead_two = keep_two * g_shorted
    ahead = passed_along(
        jnp.concatenate([lead_one[:, :2], lead_two[:, :2]], axis=1).astype(BF16), "seq", -1
    ).astype(F32)
    after_one = jnp.concatenate([lead_one[:, 1:], ahead[:, :1]], axis=1)
    after_two = jnp.concatenate([lead_two[:, 2:], ahead[:, 2:4]], axis=1)
    g_proj = taps_short[0] * g_shorted + taps_short[1] * after_one + taps_short[2] * after_two
    g_short_w = jnp.stack(
        [
            jnp.sum(g_shorted * current, axis=(0, 1)),
            jnp.sum(lead_one * before_one, axis=(0, 1)),
            jnp.sum(lead_two * before_two, axis=(0, 1)),
        ],
        axis=0,
    )
    g_short_b = jnp.sum(g_shorted, axis=(0, 1))
    g_proj_low = g_proj.astype(BF16).reshape(flat_count, 3 * width)
    g_in_w = weight_gradient(n1_low, g_proj_low)
    g_in_b = jnp.sum(g_proj_low.astype(F32), axis=0)
    g_n1 = back_product(g_proj_low, in_weight)
    g_x_part, g_ln1_gain, g_ln1_bias = ln1_pull(g_n1)
    grad_tokens = (g_resid + g_x_part).reshape(row_count, tok_count, width)

    def lined(parts):
        flat = jnp.concatenate([part.reshape(-1) for part in parts])
        return jnp.pad(flat, (0, -flat.shape[0] % 128)).reshape(-1, 128)

    net = lined((g_f1_w, g_f1_b, g_f2_w, g_f2_b))
    net_rows = net.shape[0]
    own = lined((g_f3_w, g_skip))
    bits = device_bits()
    seq_bits = int(math.log2(seq_count))
    joint = summed(jnp.concatenate([net, own]), range(seq_bits, bits))
    net = summed(joint[:net_rows], range(seq_bits)).reshape(-1)
    own = joint[net_rows:].reshape(-1)
    g_f1_w, g_f1_b, g_f2_w, g_f2_b = (
        part.reshape(like.shape)
        for part, like in zip(
            jnp.split(net, np.cumsum([f1_weight.size, f1_bias.size, f2_weight.size, f2_bias.size])),
            (f1_weight, f1_bias, f2_weight, f2_bias),
        )
    )
    g_f3_w = own[: f3_weight.size].reshape(f3_weight.shape)
    g_skip = own[f3_weight.size : f3_weight.size + lanes]

    shares = 1 << bits
    vectors = (g_ln2_gain, g_ln2_bias, g_up_b, g_down_b, g_out_b)
    vectors += (g_ln1_gain, g_ln1_bias, g_in_b, g_short_b) + tuple(g_short_w)
    rows = jnp.concatenate([v.reshape(shares, -1) for v in vectors], axis=1)
    sums = small_scattered(rows)
    cuts = np.cumsum([v.shape[0] // shares for v in vectors])[:-1]
    (
        g_ln2_gain,
        g_ln2_bias,
        g_up_b,
        g_down_b,
        g_out_b,
        g_ln1_gain,
        g_ln1_bias,
        g_in_b,
        g_short_b,
        *g_short_w,
    ) = jnp.split(sums, cuts)
    return (
        output,
        grad_tokens,
        g_ln1_gain,
        g_ln1_bias,
        g_in_w,
        g_in_b,
        jnp.stack(g_short_w),
        g_short_b,
        g_f1_w,
        g_f1_b,
        g_f2_w,
        g_f2_b,
        g_f3_w,
        g_skip,
        g_out_w,
        g_out_b,
        g_ln2_gain,
        g_ln2_bias,
        g_up_w,
        g_up_b,
        g_down_w,
        g_down_b,
    )


HALO = 16


def turned_halves(values, share, out_ref, at):
    turned = values.T.astype(BF16)
    for run in range(turned.shape[0] // share):
        into = pl.ds(run // 2 * share, share)
        out_ref[run % 2, into, at] = turned[run * share : (run + 1) * share]


def row_of(ref):
    return ref[...].astype(F32).reshape(1, -1)


def keeps(cuts_ref, first_ref, row, count, lanes):
    spot = lax.broadcasted_iota(jnp.int32, (count, lanes), 0) + first_ref[0]

    def begins(at):
        found = at == 0
        for cut in range(cuts_ref.shape[1]):
            found = found | (at == cuts_ref[row, cut])
        return found

    here, before = begins(spot), begins(spot - 1)
    return jnp.where(here, 0.0, 1.0), jnp.where(here | before, 0.0, 1.0)


def short_filter(values, weight, shift, keep_one, keep_two, begin, count):
    one = pltpu.roll(values, 1, 0)[begin : begin + count]
    two = pltpu.roll(values, 2, 0)[begin : begin + count]
    here = values[begin : begin + count]
    return weight[0:1] * here + keep_one * (weight[1:2] * one) + keep_two * (weight[2:3] * two) + shift


def normed(values):
    center = values - jnp.mean(values, axis=-1, keepdims=True)
    spread = jnp.mean(center * center, axis=-1, keepdims=True)
    scale = lax.rsqrt(spread + eps)
    return center * scale, scale


def in_forward_kernel(
    cuts_ref,
    first_ref,
    before_ref,
    x_ref,
    beyond_ref,
    gain_ref,
    bias_ref,
    w0,
    w1,
    w2,
    b0,
    b1,
    b2,
    s1,
    s2,
    c1,
    c2,
    norm_out,
    proj_out,
    carried_out,
    norm,
):
    rows, count, width = x_ref.shape
    extent = count + 2 * HALO
    group = carried_out.shape[3]

    @pl.when(pl.program_id(0) == 0)
    def _():
        for row in range(rows):
            around = [ref[row].astype(F32) for ref in (before_ref, x_ref, beyond_ref)]
            hat, _ = normed(jnp.concatenate(around, axis=0))
            value = hat * row_of(gain_ref) + row_of(bias_ref)
            norm[row * extent : (row + 1) * extent] = value.astype(BF16)
            turned_halves(
                value[HALO : HALO + count], 32, norm_out, pl.ds(row * count, count)
            )

    parts = []
    for third, (w, b) in enumerate(((w0, b0), (w1, b1), (w2, b2))):
        part = dot32(norm[...], w[...]) + row_of(b)
        low = part.astype(BF16)
        for row in range(rows):
            proj_out[third, row] = low[row * extent : (row + 1) * extent]
        parts.append(low.astype(F32))
    lanes = parts[0].shape[1]
    for row in range(rows):
        keep_one, keep_two = keeps(cuts_ref, first_ref, row, count, lanes)
        sides = [
            short_filter(
                parts[third][row * extent : (row + 1) * extent],
                s[...].astype(F32),
                row_of(c),
                keep_one,
                keep_two,
                HALO,
                count,
            )
            for third, s, c in ((1, s1, c1), (2, s2, c2))
        ]
        carried = (sides[0] * sides[1]).astype(BF16)
        for index in range(lanes // group):
            carried_out[index, row] = carried[:, index * group : (index + 1) * group]


def smem():
    return pl.BlockSpec(memory_space=pltpu.SMEM)


def whole(shape):
    return pl.BlockSpec(shape, lambda i: (0,) * len(shape), pipeline_mode=pl.Buffered(1))


def params():
    return pltpu.CompilerParams(
        vmem_limit_bytes=VMEM_MIB * 2**20, dimension_semantics=("arbitrary",)
    )


def third_block(shape, which, steps):
    lead = (0,) * (len(shape) - 1)
    return pl.BlockSpec(shape, lambda i: lead + (which * steps + i,))


def in_forward(
    cuts, first, before, x, beyond, gain, bias, in_weight, in_bias, short_weight, short_bias, group
):
    rows, count, width = x.shape
    extent = count + 2 * HALO
    lanes = 256
    steps = width // lanes
    return pl.pallas_call(
        in_forward_kernel,
        grid=(steps,),
        in_specs=[smem(), smem(), whole(before.shape), whole(x.shape), whole(beyond.shape)]
        + [whole(gain.shape), whole(bias.shape)]
        + [third_block((width, lanes), t, steps) for t in range(3)]
        + [third_block((lanes,), t, steps) for t in range(3)]
        + [third_block((3, lanes), t, steps) for t in (1, 2)]
        + [third_block((lanes,), t, steps) for t in (1, 2)],
        out_specs=[
            whole((2, width // 2, rows * count)),
            pl.BlockSpec((3, rows, extent, lanes), lambda i: (0, 0, 0, i)),
            pl.BlockSpec((lanes // group, rows, count, group), lambda i: (i, 0, 0, 0)),
        ],
        out_shape=[
            jax.ShapeDtypeStruct((2, width // 2, rows * count), BF16),
            jax.ShapeDtypeStruct((3, rows, extent, width), BF16),
            jax.ShapeDtypeStruct((width // group, rows, count, group), BF16),
        ],
        scratch_shapes=[pltpu.VMEM((rows * extent, width), BF16)],
        compiler_params=params(),
        cost_estimate=MUCH,
        name="in_forward",
    )(
        cuts,
        first,
        before,
        x,
        beyond,
        gain,
        bias,
        *[in_weight] * 3,
        *[in_bias] * 3,
        *[short_weight] * 2,
        *[short_bias] * 2,
    )


def gates(cuts_ref, first_ref, proj_ref, weight_ref, shift_ref, row, index, group):
    at = pl.ds(index * group, group)
    extent = proj_ref.shape[2]
    count = extent - 2 * HALO
    keep_one, keep_two = keeps(cuts_ref, first_ref, row, count, group)
    return short_filter(
        proj_ref[0, row, :, at].astype(F32),
        weight_ref[:, at].astype(F32),
        shift_ref[at].astype(F32).reshape(1, -1),
        keep_one,
        keep_two,
        HALO,
        count,
    )


def middle_forward_kernel(
    cuts_ref,
    first_ref,
    long_ref,
    proj_ref,
    weight_ref,
    shift_ref,
    x_ref,
    out_w_ref,
    out_b_ref,
    gain_ref,
    bias_ref,
    up_ref,
    up_b_ref,
    g_act_ref,
    mixed_out,
    resid_out,
    norm_out,
    act_out,
    split_out,
    g_pre_out,
    g_up_b_out,
    mixed,
    norm,
):
    groups, rows, count, group = long_ref.shape

    @pl.when(pl.program_id(0) == 0)
    def _():
        for row in range(rows):
            own = pl.ds(row * count, count)
            for index in range(groups):
                gate = gates(cuts_ref, first_ref, proj_ref, weight_ref, shift_ref, row, index, group)
                value = gate * long_ref[index, row].astype(F32)
                mixed[own, pl.ds(index * group, group)] = value.astype(BF16)
        for row in range(rows):
            own = pl.ds(row * count, count)
            turned_halves(mixed[own, :].astype(F32), 32, mixed_out, own)
            branch = dot32(mixed[own, :], out_w_ref[...]) + row_of(out_b_ref)
            resid = x_ref[own, :].astype(F32) + branch
            resid_out[own, :] = resid
            hat, _ = normed(resid)
            value = hat * row_of(gain_ref) + row_of(bias_ref)
            norm[own, :] = value.astype(BF16)
            turned_halves(value, 32, norm_out, own)

    pre = dot32(norm[...], up_ref[...]) + row_of(up_b_ref)
    scale = math.sqrt(2.0 / math.pi)
    square = pre * pre
    inner = pre * (scale + (scale * 0.044715) * square)
    half = 0.5 + 0.5 * jnp.tanh(inner)
    act = pre * half
    act_out[...] = act.astype(BF16)
    turned_halves(act, 128, split_out, pl.ds(0, act.shape[0]))
    slope = pre * (2.0 * scale + (6.0 * scale * 0.044715) * square)
    slope = half + slope * (half * (1.0 - half))
    g_pre = (g_act_ref[...].astype(F32) * slope).astype(BF16)
    g_pre_out[...] = g_pre
    g_up_b_out[...] = jnp.sum(g_pre.astype(F32), axis=0, keepdims=True)


def middle_forward(
    cuts, first, long, proj, short_weight, short_bias, x, out_w, out_b, gain, bias, up, up_b, g_act
):
    groups, rows, count, group = long.shape
    extent = proj.shape[2]
    tokens, width = x.shape
    hidden = up.shape[1]
    lanes = width
    steps = hidden // lanes

    def part(height):
        return pl.BlockSpec((height, lanes), lambda i: (0, i))

    return pl.pallas_call(
        middle_forward_kernel,
        grid=(steps,),
        in_specs=[
            smem(),
            smem(),
            whole(long.shape),
            whole((1, rows, extent, width)),
            whole((3, width)),
            whole((width,)),
            whole((tokens, width)),
            whole((width, width)),
            whole((width,)),
            whole((width,)),
            whole((width,)),
            part(width),
            pl.BlockSpec((lanes,), lambda i: (i,)),
            part(tokens),
        ],
        out_specs=[
            whole((2, width // 2, tokens)),
            whole((tokens, width)),
            whole((2, width // 2, tokens)),
            part(tokens),
            pl.BlockSpec((2, lanes // 2, tokens), lambda i: (0, i, 0)),
            part(tokens),
            part(1),
        ],
        out_shape=[
            jax.ShapeDtypeStruct((2, width // 2, tokens), BF16),
            jax.ShapeDtypeStruct((tokens, width), F32),
            jax.ShapeDtypeStruct((2, width // 2, tokens), BF16),
            jax.ShapeDtypeStruct((tokens, hidden), BF16),
            jax.ShapeDtypeStruct((2, hidden // 2, tokens), BF16),
            jax.ShapeDtypeStruct((tokens, hidden), BF16),
            jax.ShapeDtypeStruct((1, hidden), F32),
        ],
        scratch_shapes=[pltpu.VMEM((tokens, width), BF16), pltpu.VMEM((tokens, width), BF16)],
        compiler_params=params(),
        cost_estimate=MUCH,
        name="middle_forward",
    )(
        cuts,
        first,
        long,
        proj,
        short_weight,
        short_bias,
        x,
        out_w,
        out_b,
        gain,
        bias,
        up,
        up_b,
        g_act,
    )


def turned_dot(left, right):
    return lax.dot_general(left, right, (((1,), (1,)), ((), ())), preferred_element_type=F32)


def normed_back(values, grad, gain):
    hat, scale = normed(values)
    inward = grad * gain
    mean = jnp.mean(inward, axis=-1, keepdims=True)
    along = jnp.mean(inward * hat, axis=-1, keepdims=True)
    g_gain = jnp.sum(grad * hat, axis=0, keepdims=True)
    return scale * (inward - mean - hat * along), g_gain, jnp.sum(grad, axis=0, keepdims=True)


def middle_backward_kernel(
    cuts_ref,
    first_ref,
    long_ref,
    proj_ref,
    weight_ref,
    shift_ref,
    resid_ref,
    grad_ref,
    gain_ref,
    out_w_ref,
    g_pre_ref,
    up_ref,
    _,
    g_long_out,
    g_gate_out,
    g_resid_out,
    g_branch_out,
    sums_out,
    token_out,
    total,
):
    groups, rows, count, group = long_ref.shape
    step = pl.program_id(0)
    token_out[0] = 0

    @pl.when(step == 0)
    def _():
        total[...] = turned_dot(g_pre_ref[...], up_ref[...])

    @pl.when(step > 0)
    def _():
        total[...] += turned_dot(g_pre_ref[...], up_ref[...])

    @pl.when(step == pl.num_programs(0) - 1)
    def _():
        sums = [0.0] * 4
        for row in range(rows):
            own = pl.ds(row * count, count)
            grad = grad_ref[own, :].astype(F32)
            back, g_gain, g_bias = normed_back(
                resid_ref[own, :], total[own, :], row_of(gain_ref)
            )
            g_resid = grad + back
            g_resid_out[own, :] = g_resid
            low = g_resid.astype(BF16)
            g_branch_out[own, :] = low
            g_out_b = jnp.sum(low.astype(F32), axis=0, keepdims=True)
            g_down_b = jnp.sum(grad, axis=0, keepdims=True)
            sums = [a + b for a, b in zip(sums, (g_gain, g_bias, g_out_b, g_down_b))]
            total[own, :] = turned_dot(low, out_w_ref[...])
        sums_out[...] = jnp.concatenate(sums + [jnp.zeros_like(sums[0])] * 4, axis=0)
        for row in range(rows):
            own = pl.ds(row * count, count)
            for index in range(groups):
                at = pl.ds(index * group, group)
                g_mixed = total[own, at]
                gate = gates(cuts_ref, first_ref, proj_ref, weight_ref, shift_ref, row, index, group)
                g_gate_out[row, :, at] = g_mixed * long_ref[index, row].astype(F32)
                g_long_out[index, row] = (g_mixed * gate).astype(BF16)


def middle_backward(
    cuts, first, long, proj, short_weight, short_bias, resid, grad, gain, out_w, g_pre, up, ready
):
    groups, rows, count, group = long.shape
    extent = proj.shape[2]
    tokens, width = resid.shape
    hidden = up.shape[1]
    lanes = 1024
    steps = hidden // lanes

    def part(height):
        return pl.BlockSpec((height, lanes), lambda i: (0, i))

    return pl.pallas_call(
        middle_backward_kernel,
        grid=(steps,),
        in_specs=[
            smem(),
            smem(),
            whole(long.shape),
            whole((1, rows, extent, width)),
            whole((3, width)),
            whole((width,)),
            whole((tokens, width)),
            whole((tokens, width)),
            whole((width,)),
            whole((width, width)),
            part(tokens),
            part(width),
            pl.BlockSpec(memory_space=pl.ANY),
        ],
        out_specs=[
            whole(long.shape),
            whole((rows, count, width)),
            whole((tokens, width)),
            whole((tokens, width)),
            whole((8, width)),
            smem(),
        ],
        out_shape=[
            jax.ShapeDtypeStruct(long.shape, BF16),
            jax.ShapeDtypeStruct((rows, count, width), F32),
            jax.ShapeDtypeStruct((tokens, width), F32),
            jax.ShapeDtypeStruct((tokens, width), BF16),
            jax.ShapeDtypeStruct((8, width), F32),
            jax.ShapeDtypeStruct((1,), jnp.int32),
        ],
        scratch_shapes=[pltpu.VMEM((tokens, width), F32)],
        compiler_params=params(),
        cost_estimate=MUCH,
        name="middle_backward",
    )(
        cuts,
        first,
        long,
        proj,
        short_weight,
        short_bias,
        resid,
        grad,
        gain,
        out_w,
        g_pre,
        up,
        ready,
    )


def in_backward_kernel(
    cuts_ref,
    first_ref,
    g_carried_ref,
    g_gate_ref,
    g_next_ref,
    proj_ref,
    s0,
    s1,
    s2,
    c1,
    c2,
    w0,
    w1,
    w2,
    x_ref,
    gain_ref,
    g_resid_ref,
    *others,
):
    g_proj_out, sums_out, g_tokens_out, norm_sums_out, token_out, total = others[-6:]
    token_out[0] = 0
    weights = [s[...].astype(F32) for s in (s0, s1, s2)]
    shifts = [None, row_of(c1), row_of(c2)]
    _, rows, extent, lanes = proj_ref.shape
    count = extent - 2 * HALO
    reach = count + HALO
    group = g_carried_ref.shape[3]
    step = pl.program_id(0)
    sums = [[0.0] * 5 for _ in range(3)]
    for row in range(rows):
        keep_one, keep_two = keeps(cuts_ref, first_ref, row, reach, lanes)
        values = [proj_ref[third, row].astype(F32) for third in range(3)]
        sides = [
            short_filter(
                values[t], weights[t], shifts[t], keep_one, keep_two, HALO, reach
            )
            for t in (1, 2)
        ]
        g_carried = jnp.concatenate(
            [g_carried_ref[index, row] for index in range(lanes // group)], axis=1
        ).astype(F32)
        g_gate = jnp.concatenate([g_gate_ref[row], g_next_ref[row].astype(F32)], axis=0)
        grads = (g_gate, g_carried * sides[1], g_carried * sides[0])
        for third, grad in enumerate(grads):
            weight = weights[third]
            lead_one, lead_two = keep_one * grad, keep_two * grad
            g_proj = (
                weight[0:1] * grad
                + weight[1:2] * pltpu.roll(lead_one, reach - 1, 0)
                + weight[2:3] * pltpu.roll(lead_two, reach - 2, 0)
            )[:count]
            low = g_proj.astype(BF16)
            g_proj_out[third, row * count : (row + 1) * count] = low
            before_one = pltpu.roll(values[third], 1, 0)[HALO : HALO + count]
            before_two = pltpu.roll(values[third], 2, 0)[HALO : HALO + count]
            here = values[third][HALO : HALO + count]
            parts = (
                grad[:count] * here,
                lead_one[:count] * before_one,
                lead_two[:count] * before_two,
                grad[:count],
                low.astype(F32),
            )
            sums[third] = [
                a + jnp.sum(b, axis=0, keepdims=True) for a, b in zip(sums[third], parts)
            ]
    for third in range(3):
        sums_out[third] = jnp.concatenate(
            sums[third] + [jnp.zeros((3, lanes), F32)], axis=0
        )
    product = sum(
        turned_dot(g_proj_out[third], w[...]) for third, w in enumerate((w0, w1, w2))
    )

    @pl.when(step == 0)
    def _():
        total[...] = product

    @pl.when(step > 0)
    def _():
        total[...] += product

    @pl.when(step == pl.num_programs(0) - 1)
    def _():
        norm_sums = [0.0, 0.0]
        for row in range(rows):
            own = pl.ds(row * count, count)
            back, g_gain, g_shift = normed_back(
                x_ref[own, :].astype(F32), total[own, :], row_of(gain_ref)
            )
            g_tokens_out[own, :] = g_resid_ref[own, :] + back
            norm_sums = [norm_sums[0] + g_gain, norm_sums[1] + g_shift]
        norm_sums_out[...] = jnp.concatenate(
            norm_sums + [jnp.zeros((6, x_ref.shape[1]), F32)], axis=0
        )


def in_backward(
    cuts,
    first,
    g_carried,
    g_gate,
    g_next,
    proj,
    short_weight,
    short_bias,
    in_w,
    x,
    gain,
    g_resid,
    ready,
):
    _, rows, extent, width = proj.shape
    count = extent - 2 * HALO
    tokens = rows * count
    group = g_carried.shape[3]
    lanes = 256
    steps = width // lanes

    return pl.pallas_call(
        in_backward_kernel,
        grid=(steps,),
        in_specs=[
            smem(),
            smem(),
            pl.BlockSpec((lanes // group, rows, count + HALO, group), lambda i: (i, 0, 0, 0)),
            pl.BlockSpec((rows, count, lanes), lambda i: (0, 0, i)),
            pl.BlockSpec((rows, HALO, lanes), lambda i: (0, 0, i)),
            pl.BlockSpec((3, rows, extent, lanes), lambda i: (0, 0, 0, i)),
        ]
        + [third_block((3, lanes), t, steps) for t in range(3)]
        + [third_block((lanes,), t, steps) for t in (1, 2)]
        + [third_block((width, lanes), t, steps) for t in range(3)]
        + [whole((tokens, width)), whole((width,)), whole((tokens, width))]
        + [pl.BlockSpec(memory_space=pl.ANY)] * len(ready),
        out_specs=[
            pl.BlockSpec((3, tokens, lanes), lambda i: (0, 0, i)),
            pl.BlockSpec((3, 8, lanes), lambda i: (0, 0, i)),
            whole((tokens, width)),
            whole((8, width)),
            smem(),
        ],
        out_shape=[
            jax.ShapeDtypeStruct((3, tokens, width), BF16),
            jax.ShapeDtypeStruct((3, 8, width), F32),
            jax.ShapeDtypeStruct((tokens, width), F32),
            jax.ShapeDtypeStruct((8, width), F32),
            jax.ShapeDtypeStruct((1,), jnp.int32),
        ],
        scratch_shapes=[pltpu.VMEM((tokens, width), F32)],
        compiler_params=params(),
        cost_estimate=MUCH,
        name="in_backward",
    )(
        cuts,
        first,
        g_carried,
        g_gate,
        g_next,
        proj,
        *[short_weight] * 3,
        *[short_bias] * 2,
        *[in_w] * 3,
        x,
        gain,
        g_resid,
        *ready,
    )


def mark(*others):
    def kernel(*refs):
        refs[-1][0] = 0

    return pl.pallas_call(
        kernel,
        in_specs=[pl.BlockSpec(memory_space=pl.ANY)] * len(others),
        out_specs=smem(),
        out_shape=jax.ShapeDtypeStruct((1,), jnp.int32),
        cost_estimate=LITTLE,
        name="mark",
    )(*others)


def matmul_turned(left, right, columns, ready):
    def kernel(left_ref, right_ref, _, out_ref):
        out_ref[...] = turned_dot(left_ref[...], right_ref[...]).astype(BF16)

    height, depth = left.shape
    width = right.shape[0]
    return pl.pallas_call(
        kernel,
        grid=(width // columns,),
        in_specs=[
            whole((height, depth)),
            pl.BlockSpec((columns, depth), lambda i: (i, 0)),
            pl.BlockSpec(memory_space=pl.ANY),
        ],
        out_specs=pl.BlockSpec((height, columns), lambda i: (0, i)),
        out_shape=jax.ShapeDtypeStruct((height, width), BF16),
        compiler_params=params(),
        cost_estimate=LITTLE,
        name="matmul_turned",
    )(left, right, ready)


def down_forward(resid, act, down, bias, ready):
    tokens, width = resid.shape
    depth = 1024
    steps = act.shape[1] // depth

    def kernel(resid_ref, act_ref, down_ref, bias_ref, *refs):
        out_ref, token_out, total = refs[-3:]
        step = pl.program_id(0)
        token_out[0] = 0
        product = dot32(act_ref[...], down_ref[...])

        @pl.when(step == 0)
        def _():
            total[...] = resid_ref[...] + row_of(bias_ref) + product

        @pl.when(step > 0)
        def _():
            total[...] += product

        @pl.when(step == steps - 1)
        def _():
            out_ref[...] = total[...].astype(BF16)

    return pl.pallas_call(
        kernel,
        grid=(steps,),
        in_specs=[
            whole((tokens, width)),
            pl.BlockSpec((tokens, depth), lambda i: (0, i)),
            pl.BlockSpec((depth, width), lambda i: (i, 0)),
            whole((width,)),
        ]
        + [pl.BlockSpec(memory_space=pl.ANY)] * len(ready),
        out_specs=[whole((tokens, width)), smem()],
        out_shape=[
            jax.ShapeDtypeStruct((tokens, width), BF16),
            jax.ShapeDtypeStruct((1,), jnp.int32),
        ],
        scratch_shapes=[pltpu.VMEM((tokens, width), F32)],
        compiler_params=params(),
        cost_estimate=LITTLE,
        name="down_forward",
    )(resid, act, down, bias, *ready)


def after(value, *others):
    return lax.optimization_barrier((value, others))[0]


def gradient_kernel(counts, order_ref, firsts, seconds, arrived, sent, kept, token, total):
    step = pl.program_id(0)
    token[0] = 0

    def write(values, place):
        if not kept:
            sent[place][...] = values.astype(BF16)
            return
        (send,), (keep,), (total_ref,) = sent, kept, total
        total_ref[...] = values
        share = total_ref.shape[0] // 16
        for spot in range(16):
            piece = pl.ds(pl.multiple_of(order_ref[1 + spot] * share, share), share)
            into = (send, keep)[spot // 8]
            into[pl.ds(spot % 8 * share, share)] = (
                total_ref[piece] + arrived[place][piece].astype(F32)
            ).astype(BF16)

    place = 0
    for steps, first, second in zip(counts, firsts, seconds):
        for _ in range(steps):

            @pl.when(step == place)
            def _(first=first, second=second, place=place):
                write(dot32(first[0], second[...]), place)

            place += 1


def gradient(order, pairs, arrived, ready, columns, cost=LITTLE):
    height, tokens = pairs[0][0].shape[1:]
    counts, first_specs, second_specs, begin = [], [], [], 0
    for first, second in pairs:
        parts = second.shape[-1] // columns
        steps = parts * (second.shape[0] if second.ndim == 3 else 1)
        first_specs.append(pl.BlockSpec((1, height, tokens), lambda i, o: (o[0], 0, 0)))

        def place(i, o, begin=begin, steps=steps, parts=parts, deep=second.ndim == 3):
            at = jnp.clip(i - begin, 0, steps - 1)
            return (at // parts, 0, at % parts) if deep else (0, at)

        shape = (None, tokens, columns) if second.ndim == 3 else (tokens, columns)
        second_specs.append(pl.BlockSpec(shape, place))
        counts.append(steps)
        begin += steps
    single = pl.BlockSpec((height, columns), lambda i, o: (0, 0), pipeline_mode=pl.Buffered(1))
    anywhere = pl.BlockSpec(memory_space=pl.ANY)
    if arrived is None:
        arrived = ()
        sent = [jax.ShapeDtypeStruct((height, columns), BF16)] * begin
        kept, scratch = [], []
        out_specs = [single] * begin
    else:
        sent = [jax.ShapeDtypeStruct((height // 2, begin * columns), BF16)]
        kept, scratch = sent, [pltpu.VMEM((height, columns), F32)]
        out_specs = [pl.BlockSpec((height // 2, columns), lambda i, o: (0, i))] * 2

    def kernel(order_ref, *refs):
        refs = list(refs)

        def take(count):
            taken, refs[:] = refs[:count], refs[count:]
            return taken

        firsts, seconds, arrived_refs = take(len(pairs)), take(len(pairs)), take(len(arrived))
        take(len(ready))
        sent_refs, kept_refs, (token,) = take(len(sent)), take(len(kept)), take(1)
        gradient_kernel(
            counts, order_ref, firsts, seconds, arrived_refs, sent_refs, kept_refs, token, refs
        )

    inputs = [p[0] for p in pairs] + [p[1] for p in pairs] + list(arrived) + list(ready)
    outputs = sent + kept + [jax.ShapeDtypeStruct((1,), jnp.int32)]
    return pl.pallas_call(
        kernel,
        grid_spec=pltpu.PrefetchScalarGridSpec(
            num_scalar_prefetch=1,
            grid=(begin,),
            in_specs=first_specs
            + second_specs
            + [single] * len(arrived)
            + [anywhere] * len(ready),
            out_specs=out_specs + [smem()],
            scratch_shapes=scratch,
        ),
        out_shape=outputs,
        compiler_params=params(),
        cost_estimate=cost,
        name="gradient",
    )(order, *inputs)


def to_sibling(blocks):
    return [swapped(block, lambda one: 1) for block in blocks]


def bit_of(index, bit):
    return (index >> bit) & 1


def choose_bit(index, bit, axis):
    def choose(array, mine):
        own = bit_of(index, bit)
        return pick(array, own if mine else 1 - own, axis)

    return choose


def choose_second(index, axis):
    def choose(array, mine):
        own = jnp.where(bit_of(index, 0) == 0, bit_of(index, 2), bit_of(index, 1))
        return pick(array, own if mine else 1 - own, axis)

    return choose


def choose_first(index, axis):
    def choose(array, mine):
        low, high = bit_of(index, 1), bit_of(index, 2)
        if not mine:
            low, high = 1 - low, 1 - high
        core = bit_of(index, 0)
        return jnp.stack(
            [
                pick(array, jnp.where(core == 0, 2 * j + low, 2 * high + j), axis)
                for j in range(2)
            ],
            axis=axis,
        )

    return choose


def swap_bit(bit):
    return lambda value: swapped(value, lambda one: 1 << bit)


def swap_first(value):
    return swapped(value, lambda one: 4 if one & 1 else 2)


def swap_second(value):
    return swapped(value, lambda one: 2 if one & 1 else 4)


def order_first(index):
    core, low, high = bit_of(index, 0), bit_of(index, 1), bit_of(index, 2)

    def some(low, high):
        return [
            4 * z + jnp.where(core == 0, 2 * j + low, 2 * high + j) for z in range(4) for j in range(2)
        ]

    return jnp.stack([core] + some(1 - low, 1 - high) + some(low, high)).astype(jnp.int32)


def stage_sent(kept, arrived, choose):
    return added(choose(kept, False), choose(arrived, False), BF16)


def stage(kept, arrived, choose):
    sent = stage_sent(kept, arrived, choose)
    return sent, added(choose(kept, True), choose(arrived, True), BF16)


def finished(kept, arrived, own, last, cuts, ready):
    rows, width = last.shape[-2:]
    last = last.reshape(rows, width)

    def kernel(own_ref, kept_ref, arrived_ref, last_ref, *refs):
        outs = refs[len(ready) : len(ready) + len(cuts)]
        refs[-1][0] = 0
        begin = 0
        for out, size in zip(outs, cuts):
            at = slice(begin, begin + size)
            first = kept_ref[:, at].astype(F32) + arrived_ref[:, at].astype(F32)
            out[...] = first + last_ref[:, at].astype(F32)
            begin += size

    half = pl.BlockSpec((None, rows, width), lambda i, o: (o[0], 0, 0))

    def flat(columns):
        return pl.BlockSpec((rows, columns), lambda i, o: (0, 0))

    *outs, token = pl.pallas_call(
        kernel,
        grid_spec=pltpu.PrefetchScalarGridSpec(
            num_scalar_prefetch=1,
            grid=(1,),
            in_specs=[half, half, flat(width)]
            + [pl.BlockSpec(memory_space=pl.ANY)] * len(ready),
            out_specs=[flat(size) for size in cuts] + [smem()],
        ),
        out_shape=[jax.ShapeDtypeStruct((rows, size), F32) for size in cuts]
        + [jax.ShapeDtypeStruct((1,), jnp.int32)],
        compiler_params=params(),
        cost_estimate=LITTLE,
        name="finished",
    )(
        own.astype(jnp.int32).reshape(1),
        kept.reshape(2, rows, width),
        arrived.reshape(2, rows, width),
        last,
        *ready,
    )
    return outs, token


def paired(values):
    while len(values) > 1:
        values = [values[k] + values[k + 1] for k in range(0, len(values), 2)]
    return values[0]


def summed_lines(values, top, ready, cut=True):
    rows, lanes = values[0].shape
    rest = top if cut else 0
    count = len(values)

    def kernel(*refs):
        total = paired([ref[...] for ref in refs[:count]])
        refs[-3][...] = total[:top]
        refs[-2][...] = total[rest:]
        refs[-1][0] = 0

    return pl.pallas_call(
        kernel,
        grid=(1,),
        in_specs=[whole((rows, lanes))] * count + [pl.BlockSpec(memory_space=pl.ANY)] * len(ready),
        out_specs=[whole((top, lanes)), whole((rows - rest, lanes)), smem()],
        out_shape=[
            jax.ShapeDtypeStruct((top, lanes), F32),
            jax.ShapeDtypeStruct((rows - rest, lanes), F32),
            jax.ShapeDtypeStruct((1,), jnp.int32),
        ],
        compiler_params=params(),
        cost_estimate=LITTLE,
        name="summed_lines",
    )(*values, *ready)


def unpacked(seq, seq_count, top, values, units, bands, sizes, ready):
    lanes = top.shape[1]
    count = len(values)

    def kernel(seq_ref, top_ref, *refs):
        outs, below, token = refs[count + len(ready) : -2], refs[-1], refs[-2]
        token[0] = 0
        below[...] = paired([ref[...] for ref in refs[:count]])
        f1_w, f1_b, f2_w, f2_b, f3_w, skip = outs[:6]
        f3_w[...] = top_ref[:units]
        skip[...] = top_ref[units]
        f2_w[...] = below[:units, :units]
        f1_w[...] = below[:bands, units:]
        f1_b[...] = below[bands, units:]
        f2_b[...] = below[bands + 1, units:]
        line, seq = units, seq_ref[0]
        for out, (kinds, size) in zip(outs[6:], sizes):
            begin = seq * size
            for kind in range(kinds):
                at = line + begin // lanes
                two = jnp.concatenate([below[pl.ds(at, 1)], below[pl.ds(at + 1, 1)]], axis=1)
                shift = lax.rem(2 * lanes - begin % lanes, 2 * lanes)
                out[kind : kind + 1] = pltpu.roll(two, shift, 1)[:, :size]
                line += size * seq_count // lanes

    shapes = [(bands, units), (units,), (units, units), (units,), (units, lanes), (lanes,)]
    shapes += [(kinds, size) for kinds, size in sizes]
    return pl.pallas_call(
        kernel,
        grid=(1,),
        in_specs=[smem(), whole(top.shape)]
        + [whole(values[0].shape)] * count
        + [pl.BlockSpec(memory_space=pl.ANY)] * len(ready),
        out_specs=[whole(shape) for shape in shapes] + [smem()],
        out_shape=[jax.ShapeDtypeStruct(shape, F32) for shape in shapes]
        + [jax.ShapeDtypeStruct((1,), jnp.int32)],
        scratch_shapes=[pltpu.VMEM(values[0].shape, F32)],
        compiler_params=params(),
        cost_estimate=LITTLE,
        name="unpacked",
    )(seq, top, *values, *ready)


def block_device(
    tokens,
    cotangent,
    bounds,
    ln1_gain,
    ln1_bias,
    in_weight,
    in_bias,
    short_weight,
    short_bias,
    f1_weight,
    f1_bias,
    f2_weight,
    f2_bias,
    f3_weight,
    filter_skip,
    out_weight,
    out_bias,
    ln2_gain,
    ln2_bias,
    up_weight,
    up_bias,
    down_weight,
    down_bias,
):
    seq_count = lax.axis_size("seq")
    rows, count, width = tokens.shape
    flat = rows * count
    length = count * seq_count
    lanes = f3_weight.shape[1]
    first_channel = (lax.axis_index("seq") * lanes).astype(jnp.int32)
    first = (lax.axis_index("seq") * count).astype(jnp.int32).reshape(1)

    def exchanged(array):
        return lax.all_to_all(array, "seq", split_axis=0, concat_axis=0, tiled=True)

    index = device_index()
    before = passed_along(tokens[:, count - HALO :], "seq", 1)
    beyond = passed_along(tokens[:, :HALO], "seq", -1)
    norm_halves, proj, carried_own = in_forward(
        bounds,
        first,
        before,
        tokens,
        beyond,
        ln1_gain,
        ln1_bias,
        in_weight,
        in_bias,
        short_weight,
        short_bias,
        lanes,
    )
    carried = exchanged(carried_own)

    taps, kept = filter_network(
        after(f1_weight, carried_own).astype(F32),
        f1_bias.astype(F32),
        f2_weight.astype(F32),
        f2_bias.astype(F32),
        f3_weight.astype(F32),
        first_channel,
        length,
    )
    tables = transform_tables(count)
    table = piece_table(bounds, seq_count, count)
    skip = filter_skip
    taps_spec = taps_spectrum(taps.reshape(seq_count, count, lanes), tables)
    long_own = long_forward(table, carried, taps_spec, skip, tables)
    long = exchanged(long_own)
    x = tokens.reshape(flat, width)
    grad = cotangent.reshape(flat, width)
    g_act = matmul_turned(grad, down_weight, 1024, long_own)
    mixed_halves, resid, norm2_halves, act, act_halves, g_pre, g_up_b = middle_forward(
        bounds,
        first,
        long,
        proj,
        short_weight,
        short_bias,
        x,
        out_weight,
        out_bias,
        ln2_gain,
        ln2_bias,
        up_weight,
        up_bias,
        g_act,
    )
    first_order = order_first(index)
    send_order = (1 - bit_of(index, 0)).astype(jnp.int32).reshape(1)
    down_pairs = [(act_halves, grad)]
    *down_sent, _ = gradient(send_order, down_pairs, None, (), 512)
    down_arrived = to_sibling(down_sent)
    *up_sent, _ = gradient(send_order, [(norm2_halves, g_pre)], None, down_sent, 1024)
    up_arrived = to_sibling(up_sent)
    down_send, down_keep, _ = gradient(first_order, down_pairs, down_arrived, up_sent, 512)
    down_arrived = swap_first(down_send)
    g_long, g_gate, g_resid, g_branch, middle_sums, token = middle_backward(
        bounds,
        first,
        long,
        proj,
        short_weight,
        short_bias,
        resid,
        grad,
        ln2_gain,
        out_weight,
        g_pre,
        up_weight,
        down_send,
    )
    g_long_all = exchanged(g_long)
    g_next = passed_along(g_gate[:, :HALO].astype(BF16), "seq", -1)

    def shaped(array, lead):
        return array.reshape(lead + (-1, array.shape[-1]))

    *out_sent, _ = gradient(send_order, [(mixed_halves, g_branch)], None, (), 1024)
    up_send, up_keep, token = gradient(
        first_order,
        [(norm2_halves, g_pre), (mixed_halves, g_branch)],
        up_arrived + to_sibling(out_sent),
        (),
        1024,
    )
    up_arrived = swap_first(up_send)
    down_send, down_keep = stage(
        shaped(down_keep, (2, 2, 2)),
        shaped(down_arrived, (2, 2, 2)),
        choose_bit(index + token[0], 3, 1),
    )
    down_arrived = swap_bit(3)(down_send)
    g_series, g_taps, g_skip, token = long_backward(
        table, g_long_all, carried, taps_spec, skip, tables, (up_send, down_send)
    )
    g_carried = exchanged(g_series)
    output, token = down_forward(resid, act, down_weight, down_bias, (g_series,))
    output = output.reshape(rows, count, width)
    later = index + token[0]
    down_send, down_keep = stage(down_keep, down_arrived, choose_bit(later, 4, 0))
    down_arrived = swap_bit(4)(down_send)
    up_send, up_keep = stage(
        shaped(up_keep, (4, 2)), shaped(up_arrived, (4, 2)), choose_second(later, 1)
    )
    up_arrived = swap_second(up_send)
    g_proj, short_sums, g_tokens, norm_sums, token = in_backward(
        bounds,
        first,
        g_carried,
        g_gate,
        g_next,
        proj,
        short_weight,
        short_bias,
        in_weight,
        x,
        ln1_gain,
        g_resid,
        (down_send, up_send),
    )
    later = index + token[0]
    down_send = stage_sent(down_keep, down_arrived, choose_second(later, 0))
    down_last = swap_second(down_send)
    up_send, up_keep = stage(
        shaped(up_keep, (2, 2)), shaped(up_arrived, (2, 2)), choose_bit(later, 3, 1)
    )
    up_arrived = swap_bit(3)(up_send)
    in_pairs = [(norm_halves, g_proj)]
    *in_sent, _ = gradient(send_order, in_pairs, None, (down_send, up_send), 1024, MUCH)
    in_send, in_keep, token = gradient(first_order, in_pairs, to_sibling(in_sent), (), 1024)
    in_arrived = swap_first(in_send)
    row_count = lax.axis_size("rows")
    seq_bits = seq_count.bit_length() - 1
    payloads = filter_backward(
        first_channel.reshape(1),
        lax.axis_index("rows").astype(jnp.int32).reshape(1),
        row_count,
        g_taps.reshape(length, lanes),
        kept,
        f2_weight,
        f3_weight,
        g_skip,
        (middle_sums, g_up_b, norm_sums, short_sums),
        (in_send,),
    )
    arrived = [payloads[0]] + [
        swapped(payloads[k], lambda one, k=k: k << seq_bits) for k in range(1, row_count)
    ]
    later = index + mark(*payloads)[0]
    up_send = stage_sent(up_keep, up_arrived, choose_bit(later, 4, 0))
    up_last = swap_bit(4)(up_send)
    left = jnp.where(bit_of(index, 0) == 0, bit_of(index, 2), bit_of(index, 1))
    (g_down_w,), token = finished(
        down_keep, down_arrived, left, down_last, (width,), (up_send,)
    )
    units, bands = f3_weight.shape[0], f1_weight.shape[0]
    top, mine, token = summed_lines(arrived, units + 8, (token,))
    in_send, in_keep = stage(
        shaped(in_keep, (4, 2)),
        shaped(in_arrived, (4, 2)),
        choose_second(index + token[0], 1),
    )
    in_arrived = swap_second(in_send)
    arrived = swapped(mine, lambda one: 1)
    _, mine, token = summed_lines([mine, arrived], 8, (in_send,), False)
    in_send, in_keep = stage(
        shaped(in_keep, (2, 2)), shaped(in_arrived, (2, 2)), choose_bit(index + token[0], 3, 1)
    )
    in_arrived = swap_bit(3)(in_send)
    arrived = swapped(mine, lambda one: 2)
    _, mine, token = summed_lines([mine, arrived], 8, (in_send,), False)
    (g_up_w, g_out_w), token = finished(
        up_keep, up_arrived, bit_of(index, 4), up_last, (up_weight.shape[1], width), (token,)
    )
    in_send = stage_sent(in_keep, in_arrived, choose_bit(index + token[0], 4, 0))
    in_last = swap_bit(4)(in_send)
    arrived = swapped(mine, lambda one: 4)
    shares = 1 << device_bits()
    sizes = ((6, width // shares), (1, up_weight.shape[1] // shares), (5, 3 * width // shares))
    seq = lax.axis_index("seq").astype(jnp.int32).reshape(1)
    *small, token = unpacked(
        seq, seq_count, top, [mine, arrived], units, bands, sizes, (in_send,)
    )
    (g_in_w,), _ = finished(
        in_keep, in_arrived, bit_of(index, 4), in_last, (3 * width,), (token,)
    )
    g_f1_w, g_f1_b, g_f2_w, g_f2_b, g_f3_w, g_skip, narrow, g_up_b, broad = small
    g_ln2_gain, g_ln2_bias, g_out_b, g_down_b, g_ln1_gain, g_ln1_bias = narrow
    g_up_b = g_up_b.reshape(-1)
    g_short_w, g_short_b, g_in_b = broad[:3], broad[3], broad[4]
    grad_tokens = g_tokens.reshape(rows, count, width)
    return (
        output,
        grad_tokens,
        g_ln1_gain,
        g_ln1_bias,
        g_in_w,
        g_in_b,
        g_short_w,
        g_short_b,
        g_f1_w,
        g_f1_b,
        g_f2_w,
        g_f2_b,
        g_f3_w,
        g_skip,
        g_out_w,
        g_out_b,
        g_ln2_gain,
        g_ln2_bias,
        g_up_w,
        g_up_b,
        g_down_w,
        g_down_b,
    )


def per_device(tokens, *others):
    shares = lax.axis_size("rows") * lax.axis_size("seq")
    count, width = tokens.shape[1:]
    hidden = others[20].shape[0]
    lanes = width // lax.axis_size("seq")
    fits = shares == 32 and width == 1024 and hidden == 4096 and lanes == 128 and count % 128 == 0
    return (block_device if fits else plain_device)(tokens, *others)


def solution(mesh):
    return jax.shard_map(
        per_device,
        mesh=mesh,
        in_specs=(
            P("rows", "seq", None),
            P("rows", "seq", None),
            P("rows", None),
            P(),
            P(),
            P(),
            P(),
            P(),
            P(),
            P(),
            P(),
            P(),
            P(),
            P(None, "seq"),
            P("seq"),
            P(),
            P(),
            P(),
            P(),
            P(),
            P(),
            P(),
            P(),
        ),
        out_specs=(
            P("rows", "seq", None),
            P("rows", "seq", None),
            P(("rows", "seq")),
            P(("rows", "seq")),
            P(("rows", "seq"), None),
            P(("rows", "seq")),
            P(None, ("rows", "seq")),
            P(("rows", "seq")),
            P(),
            P(),
            P(),
            P(),
            P(None, "seq"),
            P("seq"),
            P(("rows", "seq"), None),
            P(("rows", "seq")),
            P(("rows", "seq")),
            P(("rows", "seq")),
            P(("rows", "seq"), None),
            P(("rows", "seq")),
            P(("rows", "seq"), None),
            P(("rows", "seq")),
        ),
        check_vma=False,
    )
```

```python
import functools
import math

import jax
import jax.numpy as jnp
import ml_dtypes
import numpy as np
from jax import lax
from jax.experimental import pallas as pl
from jax.experimental.pallas import tpu as pltpu
from jax.sharding import PartitionSpec as P

D = 1024
EMB = 33
HIGH = lax.Precision.HIGHEST
eps = 1e-05
slow_rate = math.log(100.0) / 1.5
fast_rate = math.log(100.0) / 0.3
BOTH = ("rows", "seq")
F32 = jnp.float32
BF16 = jnp.bfloat16
VMEM_MIB = 58
LITTLE = pl.CostEstimate(flops=1, bytes_accessed=1, transcendentals=0)
MUCH = pl.CostEstimate(flops=5 * 10**10, bytes_accessed=2 * 10**8, transcendentals=0)


def passed_along(value, axis, steps):
    count = lax.axis_size(axis)
    first, last = (max(0, -steps), min(count, count - steps))
    return lax.ppermute(value, axis, [(source, source + steps) for source in range(first, last)])


def layer_norm(values, gain, shift):
    center = values - jnp.mean(values, axis=-1, keepdims=True)
    spread = jnp.mean(center * center, axis=-1, keepdims=True)
    return center * lax.rsqrt(spread + eps) * gain + shift


def gelu_tanh(values):
    return jax.nn.gelu(values, approximate=True)


def features(length):
    steps = np.arange(length, dtype=np.float64)
    bands = (EMB - 1) // 2
    freqs = 0.0001 + np.arange(bands, dtype=np.float64) * ((bands - 1 - 0.0001) / (bands - 1))
    angles = (steps * (2.0 * math.pi / length))[:, None] * freqs[None, :]
    timeline = steps / (length - 1)
    table = np.concatenate([timeline[:, None], np.cos(angles), -np.sin(angles)], axis=1)
    return jnp.asarray(table.astype(np.float32)), jnp.asarray(timeline.astype(np.float32))


def filter_taps(w_one, b_one, w_two, b_two, w_three, first, length):
    feats, timeline = features(length)
    hidden = jnp.sin(jnp.dot(feats, w_one, precision=HIGH) + b_one)
    hidden = jnp.sin(jnp.dot(hidden, w_two, precision=HIGH) + b_two)
    raw_taps = jnp.dot(hidden, w_three, precision=HIGH)
    channels = (first + jnp.arange(w_three.shape[1], dtype=jnp.int32)).astype(F32)
    rates = slow_rate + channels * ((fast_rate - slow_rate) / (D - 1))
    return raw_taps * jnp.exp(-timeline[:, None] * rates[None, :])


def close_dot(left, right, dims):
    def one(a, b):
        return lax.dot_general(a, b, (dims, ((), ())), preferred_element_type=F32)

    (a, a_rest), (b, b_rest) = split32(left), split32(right)
    return one(a, b) + one(a, b_rest) + one(a_rest, b)


def line_up(out_ref, count, parts):
    line = 0
    for ref, lead, rows in parts:
        width = ref.shape[-1]
        share = rows * width // count // 128
        for z in range(count):
            for k in range(share):
                at = (z * share + k) * 128
                row, lane = at // width, at % width
                index = ((row,) if rows > 1 else ()) + tuple(lead)
                value = ref[index + (slice(lane, lane + 128),)]
                out_ref[z, line + k : line + k + 1] = value.reshape(1, 128)
        line += share


def filter_backward_kernel(
    first_ref,
    row_ref,
    grad_ref,
    feats_ref,
    one_ref,
    two_ref,
    w2_ref,
    w3_ref,
    skip_ref,
    middle_ref,
    up_ref,
    norm_ref,
    short_ref,
    outs,
    lines,
    out_ref,
):
    lines[...] = jnp.zeros_like(lines)
    parts = [(middle_ref, (k,), 1) for k in range(4)] + [(norm_ref, (k,), 1) for k in range(2)]
    parts += [(up_ref, (0,), 1)] + [(short_ref, (k,), 3) for k in range(5)]
    line_up(lines, len(outs), parts)
    length, lanes = grad_ref.shape
    units = one_ref.shape[1] // 2
    bands = feats_ref.shape[1]
    inner = grad_ref[...] * decay(first_ref, 0, length, lanes, length)
    over_time, over_last = ((0,), (0,)), ((1,), (1,))
    out_ref[...] = jnp.zeros_like(out_ref)
    out_ref[:units] = close_dot(two_ref[:, :units], inner, over_time)
    out_ref[units : units + 1] = skip_ref[...]
    two = close_dot(inner, w3_ref[...].astype(F32), over_last) * two_ref[:, units:]
    one = close_dot(two, w2_ref[...].astype(F32), over_last) * one_ref[:, units:]
    below = units + 8
    out_ref[below : below + units, :units] = close_dot(one_ref[:, :units], two, over_time)
    out_ref[below : below + bands, units:] = close_dot(feats_ref[...], one, over_time)
    out_ref[below + bands : below + bands + 1, units:] = jnp.sum(one, axis=0, keepdims=True)
    out_ref[below + bands + 1 : below + bands + 2, units:] = jnp.sum(two, axis=0, keepdims=True)
    for k, payload in enumerate(outs):
        payload[: 2 * units + 8] = out_ref[...]
        payload[2 * units + 8 :] = lines[row_ref[0] ^ k]


LINES = 56


def filter_backward(first, row, count, g_taps, kept, w_two, w_three, g_skip, sums, ready):
    feats, one, two = kept
    units, lanes = w_three.shape
    vmem = pl.BlockSpec(memory_space=pltpu.VMEM)
    height = 2 * units + 8

    def kernel(*refs):
        outs, scratch = refs[13 + len(ready) : -2], refs[-2:]
        filter_backward_kernel(*refs[:13], outs, *scratch)

    return pl.pallas_call(
        kernel,
        in_specs=[smem()] * 2 + [vmem] * 11 + [pl.BlockSpec(memory_space=pl.ANY)] * len(ready),
        out_specs=[vmem] * count,
        out_shape=[jax.ShapeDtypeStruct((height + LINES, lanes), F32)] * count,
        scratch_shapes=[
            pltpu.VMEM((count, LINES, lanes), F32),
            pltpu.VMEM((height, lanes), F32),
        ],
        compiler_params=pltpu.CompilerParams(vmem_limit_bytes=VMEM_MIB * 2**20),
        cost_estimate=MUCH,
        name="filter_backward",
    )(first, row, g_taps, feats, one, two, w_two, w_three, g_skip, *sums, *ready)


def split16(values):
    high = values.astype(ml_dtypes.bfloat16)
    return high, (values - high.astype(np.float64)).astype(ml_dtypes.bfloat16)


def transform_tables(block):
    freq = np.arange(block)[:, None]
    time = np.arange(block)[None, :]
    angles = ((2 * freq + 1) * time % (4 * block)) * (math.pi / (2 * block))
    ahead = np.concatenate([np.cos(angles), -np.sin(angles)], axis=0)
    ahead_high, ahead_low = split16(ahead)
    back_high, back_low = split16(ahead.T / block)
    return tuple(jnp.asarray(t) for t in (ahead_high, ahead_low, back_high, back_low))


def piece_table(bounds, blocks, block):
    length = blocks * block
    edges = jnp.broadcast_to(jnp.arange(blocks, dtype=jnp.int32) * block, (bounds.shape[0], blocks))
    for cut in range(bounds.shape[1]):
        one = bounds[:, cut : cut + 1]
        low = jnp.concatenate([jnp.full_like(one, -1), edges], axis=1)
        high = jnp.concatenate([edges, jnp.full_like(one, length)], axis=1)
        edges = jnp.maximum(low, jnp.minimum(one, high))
    ends = jnp.concatenate([edges[:, 1:], jnp.full_like(edges[:, :1], length)], axis=1)
    index = jnp.minimum(edges // block, blocks - 1)
    start = jnp.max(
        jnp.where(bounds[:, :, None] <= edges[:, None, :], bounds[:, :, None], 0), axis=1
    )
    stop = jnp.min(
        jnp.where(bounds[:, :, None] > edges[:, None, :], bounds[:, :, None], length), axis=1
    )
    empty = ends <= edges
    earlier = jnp.where(empty, 0, index - start // block + 1)
    later = jnp.where(empty, 0, (stop - 1) // block - index + 1)
    return jnp.stack([edges, ends, index, earlier, later]).astype(jnp.int32)


def dot32(left, right):
    return jnp.dot(left, right, preferred_element_type=F32)


def split32(values):
    high = values.astype(BF16)
    return high, (values - high.astype(F32)).astype(BF16)


def wide_dot(high, low, values):
    top, rest = split32(values)
    return dot32(high, top) + dot32(high, rest) + dot32(low, top)


def alternating(rows, lanes):
    odd = lax.broadcasted_iota(jnp.int32, (rows, lanes), 0) % 2
    return 1.0 - 2.0 * odd.astype(F32)


def sine_cosine(angle):
    turns = jnp.floor(angle * (2.0 / math.pi) + 0.5)
    rest = angle - turns * 1.5703125
    rest = rest - turns * 4.837512969970703125e-4
    rest = rest - turns * 7.549789948768648e-8
    square = rest * rest
    sine = ((-1.9515295891e-4 * square + 8.3321608736e-3) * square - 1.6666654611e-1) * square
    sine = sine * rest + rest
    cosine = (2.443315711809948e-5 * square - 1.388731625493765e-3) * square
    cosine = (cosine + 4.166664568298827e-2) * square * square - 0.5 * square + 1.0
    quarter = turns.astype(jnp.int32)
    swap = (quarter & 1) == 1
    sine, cosine = jnp.where(swap, cosine, sine), jnp.where(swap, sine, cosine)
    return (
        jnp.where((quarter & 2) == 2, -sine, sine),
        jnp.where(((quarter + 1) & 2) == 2, -cosine, cosine),
    )


def near_dot(left, right):
    top, rest = split32(left)
    return dot32(top, right) + dot32(rest, right)


def decay(first_ref, begin, count, lanes, length):
    spot = (lax.broadcasted_iota(jnp.int32, (count, lanes), 0) + begin).astype(F32)
    channel = (lax.broadcasted_iota(jnp.int32, (1, lanes), 1) + first_ref[0]).astype(F32)
    rates = slow_rate + channel * ((fast_rate - slow_rate) / (D - 1))
    return jnp.exp(-(spot * (1.0 / (length - 1))) * rates)


def taps_kernel(
    first_ref, feats_ref, w1, b1, w2, b2, w3, high_ref, low_ref, _, out_ref, one_ref, two_ref, own
):
    blocks, double, lanes = out_ref.shape
    block = double // 2
    for k in range(blocks):
        at = slice(k * block, (k + 1) * block)
        sine, cosine = sine_cosine(near_dot(feats_ref[at], w1[...]) + row_of(b1))
        one_ref[at] = jnp.concatenate([sine, cosine], axis=1)
        sine, cosine = sine_cosine(near_dot(sine, w2[...]) + row_of(b2))
        two_ref[at] = jnp.concatenate([sine, cosine], axis=1)
        taps = near_dot(sine, w3[...]) * decay(first_ref, k * block, block, lanes, blocks * block)
        own[k] = wide_dot(high_ref[...], low_ref[...], taps)
    sign = alternating(block, lanes)
    out_ref[0] = own[0]
    for k in range(1, blocks):
        out_ref[k, :block] = own[k, :block] - sign * own[k - 1, block:]
        out_ref[k, block:] = own[k, block:] + sign * own[k - 1, :block]


def taps_and_spectrum(first, blocks, block, w1, b1, w2, b2, w3, tables, ready):
    lanes, units = w3.shape[1], w2.shape[0]
    length = blocks * block
    feats, _ = features(length)
    vmem = pl.BlockSpec(memory_space=pltpu.VMEM)
    spectra, one, two = pl.pallas_call(
        taps_kernel,
        in_specs=[smem()] + [vmem] * 8 + [pl.BlockSpec(memory_space=pl.ANY)],
        out_specs=[vmem] * 3,
        out_shape=[jax.ShapeDtypeStruct((blocks, 2 * block, lanes), F32)]
        + [jax.ShapeDtypeStruct((length, 2 * units), F32)] * 2,
        scratch_shapes=[pltpu.VMEM((blocks, 2 * block, lanes), F32)],
        compiler_params=pltpu.CompilerParams(vmem_limit_bytes=VMEM_MIB * 2**20),
        cost_estimate=LITTLE,
        name="taps_and_spectrum",
    )(first, feats, w1, b1, w2, b2, w3, tables[0], tables[1], ready)
    return spectra, (feats, one, two)


def piece_mask(table_ref, row, piece, block, lanes):
    at = table_ref[2, row, piece]
    spot = lax.broadcasted_iota(jnp.int32, (block, lanes), 0) + at * block
    return at, (spot >= table_ref[0, row, piece]) & (spot < table_ref[1, row, piece])


def piece_spectra(table_ref, series_ref, ahead_ref, out_ref):
    blocks, rows, block, lanes = series_ref.shape
    for piece in range(out_ref.shape[0]):
        parts = []
        for row in range(rows):
            at, inside = piece_mask(table_ref, row, piece, block, lanes)
            values = series_ref[at, row].astype(F32)
            parts.append(jnp.where(inside, values, 0.0).astype(BF16))
        out_ref[piece] = dot32(ahead_ref[...], jnp.concatenate(parts, axis=1))


def each_piece(table_ref, which, pieces, rows, lanes, blocks, visit):
    def body(index, carry):
        piece, row = index // rows, index % rows
        lane = pl.ds(pl.multiple_of(row * lanes, lanes), lanes)
        found = table_ref[which, row, piece]
        for count in range(blocks + 1):

            @pl.when(found == count)
            def _(count=count):
                visit(piece, lane, count)

        return carry

    lax.fori_loop(0, pieces * rows, body, 0)


def halves_of(block, tile):
    for begin in range(0, block, tile):
        yield pl.ds(begin, tile), pl.ds(block + begin, tile)


def couple(table_ref, step, taps_ref, series_ref, into_ref):
    blocks, double, lanes = taps_ref.shape
    block = double // 2
    pieces, _, both = series_ref.shape

    def visit(piece, lane, count):
        for real_rows, imag_rows in halves_of(block, 32):
            real = imag = jnp.zeros((32, lanes), F32)
            for k in range(count):
                tap_r, tap_i = taps_ref[k, real_rows, :], taps_ref[k, imag_rows, :]
                val_r = series_ref[piece + step * k, real_rows, lane]
                val_i = series_ref[piece + step * k, imag_rows, lane]
                if step > 0:
                    real = real + (tap_r * val_r + tap_i * val_i)
                    imag = imag + (tap_r * val_i - tap_i * val_r)
                else:
                    real = real + (tap_r * val_r - tap_i * val_i)
                    imag = imag + (tap_r * val_i + tap_i * val_r)
            into_ref[piece, real_rows, lane] = real
            into_ref[piece, imag_rows, lane] = imag

    each_piece(table_ref, 3 if step < 0 else 4, pieces, both // lanes, lanes, blocks, visit)


def correlate(table_ref, series_ref, grad_ref, into_ref):
    blocks, double, lanes = into_ref.shape
    block = double // 2
    pieces, _, both = series_ref.shape
    into_ref[...] = jnp.zeros_like(into_ref)

    def visit(piece, lane, count):
        for real_rows, imag_rows in halves_of(block, 32):
            if count:
                out_r, out_i = grad_ref[piece, real_rows, lane], grad_ref[piece, imag_rows, lane]
            for k in range(count):
                val_r = series_ref[piece - k, real_rows, lane]
                val_i = series_ref[piece - k, imag_rows, lane]
                into_ref[k, real_rows, :] += val_r * out_r + val_i * out_i
                into_ref[k, imag_rows, :] += val_r * out_i - val_i * out_r

    each_piece(table_ref, 3, pieces, both // lanes, lanes, blocks, visit)


def write_pieces(table_ref, work, back_ref, series_ref, skip_ref, out_ref):
    blocks, rows, block, lanes = series_ref.shape
    for piece in range(work.shape[0]):
        result = dot32(back_ref[...], work[piece].astype(BF16))
        for row in range(rows):
            at, inside = piece_mask(table_ref, row, piece, block, lanes)
            direct = skip_ref[...].astype(F32).reshape(1, -1) * series_ref[at, row].astype(F32)
            value = result[:, row * lanes : (row + 1) * lanes] + direct
            kept = out_ref[at, row, :block].astype(F32)
            out_ref[at, row, :block] = jnp.where(inside, value, kept).astype(BF16)


def long_forward_kernel(
    table_ref, series_ref, taps_ref, skip_ref, ahead_ref, back_ref, out_ref, spec, work
):
    piece_spectra(table_ref, series_ref, ahead_ref, spec)
    couple(table_ref, -1, taps_ref, spec, work)
    write_pieces(table_ref, work, back_ref, series_ref, skip_ref, out_ref)


def long_forward(table, series, taps_spec, skip, tables):
    blocks, rows, block, lanes = series.shape
    pieces = table.shape[2]
    vmem = pl.BlockSpec(memory_space=pltpu.VMEM)
    return pl.pallas_call(
        long_forward_kernel,
        in_specs=[smem()] + [vmem] * 5,
        out_specs=vmem,
        out_shape=jax.ShapeDtypeStruct(series.shape, BF16),
        scratch_shapes=[pltpu.VMEM((pieces, 2 * block, rows * lanes), F32)] * 2,
        compiler_params=pltpu.CompilerParams(vmem_limit_bytes=VMEM_MIB * 2**20),
        cost_estimate=MUCH,
        name="long_forward",
    )(table, series, taps_spec, skip, tables[0], tables[2])


def long_backward_kernel(
    table_ref, grad_ref, series_ref, taps_ref, skip_ref, ahead_ref, back_ref, *others
):
    out_ref, taps_out_ref, skip_out_ref, token_out, spec, grad_spec, work, cross = others[-8:]
    token_out[0] = 0
    blocks, rows, block, lanes = series_ref.shape
    piece_spectra(table_ref, grad_ref, ahead_ref, grad_spec)
    couple(table_ref, 1, taps_ref, grad_spec, work)
    write_pieces(table_ref, work, back_ref, grad_ref, skip_ref, out_ref)
    for at in range(blocks):
        for row in range(rows):
            if at + 1 < blocks:
                out_ref[at, row, block:] = out_ref[at + 1, row, : out_ref.shape[2] - block]
            else:
                out_ref[at, row, block:] = jnp.zeros_like(out_ref[at, row, block:])
    piece_spectra(table_ref, series_ref, ahead_ref, spec)
    correlate(table_ref, spec, grad_spec, cross)
    sign = alternating(block, lanes)
    for k in range(blocks):
        if k + 1 < blocks:
            cross[k, :block] = cross[k, :block] + sign * cross[k + 1, block:]
            cross[k, block:] = cross[k, block:] - sign * cross[k + 1, :block]
        taps_out_ref[k] = dot32(back_ref[...], cross[k].astype(BF16))
    total = jnp.zeros((8, lanes), F32)
    for at in range(blocks):
        for row in range(rows):
            both = grad_ref[at, row].astype(F32) * series_ref[at, row].astype(F32)
            total = total + jnp.sum(both.reshape(block // 8, 8, lanes), axis=0)
    skip_out_ref[...] = jnp.sum(total, axis=0, keepdims=True)


def long_backward(table, grad, series, taps_spec, skip, tables, ready):
    blocks, rows, block, lanes = series.shape
    pieces = table.shape[2]
    vmem = pl.BlockSpec(memory_space=pltpu.VMEM)
    return pl.pallas_call(
        long_backward_kernel,
        in_specs=[smem()] + [vmem] * 6 + [pl.BlockSpec(memory_space=pl.ANY)] * len(ready),
        out_specs=[vmem] * 3 + [smem()],
        out_shape=[
            jax.ShapeDtypeStruct((blocks, rows, block + HALO, lanes), BF16),
            jax.ShapeDtypeStruct((blocks, block, lanes), F32),
            jax.ShapeDtypeStruct((1, lanes), F32),
            jax.ShapeDtypeStruct((1,), jnp.int32),
        ],
        scratch_shapes=[pltpu.VMEM((pieces, 2 * block, rows * lanes), F32)] * 3
        + [pltpu.VMEM((blocks, 2 * block, lanes), F32)],
        compiler_params=pltpu.CompilerParams(vmem_limit_bytes=VMEM_MIB * 2**20),
        cost_estimate=MUCH,
        name="long_backward",
    )(table, grad, series, taps_spec, skip, tables[0], tables[2], *ready)


def document_masks(bounds, positions, length):
    lower = jnp.concatenate([jnp.zeros_like(bounds[:, :1]), bounds], axis=1)
    upper = jnp.concatenate([bounds, jnp.full_like(bounds[:, :1], length)], axis=1)
    inside = (positions[None, None, :] >= lower[:, :, None]) & (
        positions[None, None, :] < upper[:, :, None]
    )
    return inside.astype(F32)


def cos_sin(count_a, count_b, modulus):
    table = (
        jnp.arange(count_a, dtype=jnp.int32)[:, None]
        * jnp.arange(count_b, dtype=jnp.int32)[None, :]
        % modulus
    )
    angles = table.astype(F32) * (2.0 * math.pi / modulus)
    return (jnp.cos(angles), jnp.sin(angles))


def make_plan(blocks, block_len):
    outer = 2 * blocks
    cos_outer, sin_outer = cos_sin(outer, outer, outer)
    cos_twist, sin_twist = cos_sin(outer, block_len, outer * block_len)
    cos_inner, sin_inner = cos_sin(block_len, block_len, block_len)
    return (blocks, block_len, cos_outer, sin_outer, cos_twist, sin_twist, cos_inner, sin_inner)


def right_mul(left, table):
    return jnp.einsum("...km,mj->...kj", left, table, precision=HIGH)


def spectrum(series, plan):
    blocks, block_len, cos_outer, sin_outer, cos_twist, sin_twist, cos_inner, sin_inner = plan
    folded = series.reshape(series.shape[:-1] + (blocks, block_len))
    real_a = jnp.einsum("kn,...nm->...km", cos_outer[:, :blocks], folded, precision=HIGH)
    imag_a = -jnp.einsum("kn,...nm->...km", sin_outer[:, :blocks], folded, precision=HIGH)
    real_t = real_a * cos_twist + imag_a * sin_twist
    imag_t = imag_a * cos_twist - real_a * sin_twist
    real_x = right_mul(real_t, cos_inner) + right_mul(imag_t, sin_inner)
    imag_x = right_mul(imag_t, cos_inner) - right_mul(real_t, sin_inner)
    return (real_x, imag_x)


def inverse(real_x, imag_x, plan):
    blocks, block_len, cos_outer, sin_outer, cos_twist, sin_twist, cos_inner, sin_inner = plan
    real_b = right_mul(real_x, cos_inner) - right_mul(imag_x, sin_inner)
    imag_b = right_mul(imag_x, cos_inner) + right_mul(real_x, sin_inner)
    real_u = real_b * cos_twist - imag_b * sin_twist
    imag_u = imag_b * cos_twist + real_b * sin_twist
    folded = jnp.einsum("nk,...km->...nm", cos_outer[:blocks], real_u, precision=HIGH) - jnp.einsum(
        "nk,...km->...nm", sin_outer[:blocks], imag_u, precision=HIGH
    )
    folded = folded * (1.0 / (2 * blocks * block_len))
    return folded.reshape(folded.shape[:-2] + (blocks * block_len,))


def by_channel(blocked):
    blocks, rows, block, lanes = blocked.shape
    return blocked.astype(F32).transpose(1, 3, 0, 2).reshape(rows, lanes, blocks * block)


def by_block(series, blocks):
    rows, lanes, length = series.shape
    return series.reshape(rows, lanes, blocks, length // blocks).transpose(2, 0, 3, 1).astype(BF16)


class WholeSpectra:
    def __init__(self, bounds, taps, skip):
        blocks, block, lanes = taps.shape
        self.blocks, self.plan = blocks, make_plan(blocks, block)
        length = blocks * block
        everywhere = jnp.arange(length, dtype=jnp.int32)
        self.masks = document_masks(bounds, everywhere, length)[:, :, None, :]
        self.skip = skip[0][None, :, None]
        self.taps_real, self.taps_imag = spectrum(taps.reshape(length, lanes).T, self.plan)

    def forward(self, series):
        carried = by_channel(series)
        self.carried = carried
        real, imag = spectrum(self.masks * carried[:, None], self.plan)
        self.spec = real, imag
        docs = inverse(
            real * self.taps_real - imag * self.taps_imag,
            real * self.taps_imag + imag * self.taps_real,
            self.plan,
        )
        conv = jnp.sum(self.masks * docs, axis=1) + self.skip * carried
        return by_block(conv, self.blocks)

    def backward(self, grad):
        g_long = by_channel(grad)
        spec_real, spec_imag = self.spec
        g_skip = jnp.sum(g_long * self.carried, axis=(0, 2))
        real, imag = spectrum(self.masks * g_long[:, None], self.plan)
        docs = inverse(
            self.taps_real * real + self.taps_imag * imag,
            self.taps_real * imag - self.taps_imag * real,
            self.plan,
        )
        g_carried = jnp.sum(self.masks * docs, axis=1) + self.skip * g_long
        cross_real = jnp.sum(real * spec_real + imag * spec_imag, axis=(0, 1))
        cross_imag = jnp.sum(imag * spec_real - real * spec_imag, axis=(0, 1))
        g_taps = inverse(cross_real, cross_imag, self.plan)
        return by_block(g_carried, self.blocks), g_taps.T, g_skip[None, :]


def device_index():
    return lax.axis_index("rows") * lax.axis_size("seq") + lax.axis_index("seq")


def device_bits():
    return int(math.log2(lax.axis_size("rows") * lax.axis_size("seq")))


def swapped(value, mask_of):
    count = lax.axis_size("rows") * lax.axis_size("seq")
    return lax.ppermute(value, BOTH, [(one, one ^ mask_of(one)) for one in range(count)])


def pick(array, index, axis):
    return lax.dynamic_index_in_dim(array, index, axis=axis, keepdims=False)


def added(kept, arrived, kind):
    return (kept.astype(F32) + arrived.astype(F32)).astype(kind)


def halved(pieces, bit, axis, kind):
    mine = (device_index() >> bit) & 1
    arrived = swapped(pick(pieces, 1 - mine, axis), lambda one: 1 << bit)
    return added(pick(pieces, mine, axis), arrived, kind)


def quartered(pieces, axis, kind):
    index = device_index()
    core, low, high = index & 1, (index >> 1) & 1, (index >> 2) & 1

    def two(low_bit, high_bit):
        return jnp.stack(
            [
                pick(pieces, jnp.where(core == 0, 2 * j + low_bit, 2 * high_bit + j), axis)
                for j in range(2)
            ],
            axis=axis,
        )

    arrived = swapped(two(1 - low, 1 - high), lambda one: 4 if one & 1 else 2)
    pieces = added(two(low, high), arrived, kind)
    mine = jnp.where(core == 0, high, low)
    arrived = swapped(pick(pieces, 1 - mine, axis), lambda one: 2 if one & 1 else 4)
    return added(pick(pieces, mine, axis), arrived, kind)


def scattered(pieces, kind):
    rest = pieces.shape[1:]
    bits = device_bits()
    pieces = quartered(pieces.reshape((-1, 4) + rest), 1, kind)
    for bit in range(3, bits):
        last = bit == bits - 1
        pieces = halved(pieces.reshape((-1, 2) + rest), bit, 1, F32 if last else kind)
    return pieces.reshape(rest)


def weight_gradient(first, second):
    tokens, width = first.shape
    shares = 1 << device_bits()
    share = width // shares
    core = device_index() & 1
    halves = first.reshape(tokens, shares // 2, 2, share).transpose(2, 0, 1, 3)
    halves = halves.reshape(2, tokens, width // 2)

    def product(which):
        return jnp.einsum(
            "ti,tj->ij", pick(halves, which, 0), second, preferred_element_type=F32
        )

    arrived = swapped(product(1 - core).astype(BF16), lambda one: 1)
    kept = added(product(core), arrived, BF16)
    return scattered(kept.reshape(shares // 2, share, second.shape[1]), BF16)


def small_scattered(vectors):
    pieces = halved(vectors.reshape(-1, 2, vectors.shape[1]), 0, 1, F32)
    return scattered(pieces, F32)


def summed(value, bits):
    for bit in bits:
        value = value + swapped(value, lambda one, bit=bit: 1 << bit)
    return value


def back_product(grad_low, weight):
    return jnp.einsum("tj,ij->ti", grad_low, weight, preferred_element_type=F32)


def plain_device(
    tokens,
    cotangent,
    bounds,
    ln1_gain,
    ln1_bias,
    in_weight,
    in_bias,
    short_weight,
    short_bias,
    f1_weight,
    f1_bias,
    f2_weight,
    f2_bias,
    f3_weight,
    filter_skip,
    out_weight,
    out_bias,
    ln2_gain,
    ln2_bias,
    up_weight,
    up_bias,
    down_weight,
    down_bias,
):
    seq_count = lax.axis_size("seq")
    row_count, tok_count, width = tokens.shape
    flat_count = row_count * tok_count
    length = tok_count * seq_count
    lanes = f3_weight.shape[1]
    first_channel = lax.axis_index("seq") * lanes
    x_in = tokens.astype(F32).reshape(flat_count, width)
    n1, ln1_pull = jax.vjp(layer_norm, x_in, ln1_gain.astype(F32), ln1_bias.astype(F32))
    n1_low = n1.astype(BF16)
    proj = jnp.dot(n1_low, in_weight, preferred_element_type=F32) + in_bias.astype(F32)
    proj_low = proj.astype(BF16).reshape(row_count, tok_count, 3 * width)
    here = lax.axis_index("seq") * tok_count + jnp.arange(tok_count, dtype=jnp.int32)
    starts = jnp.max(
        jnp.where(bounds[:, :, None] <= here[None, None, :], bounds[:, :, None], 0), axis=1
    )
    keep_one = (here[None, :] - 1 >= starts).astype(F32)[:, :, None]
    keep_two = (here[None, :] - 2 >= starts).astype(F32)[:, :, None]
    rim = passed_along(proj_low[:, tok_count - 2 :, :], "seq", 1)
    extended = jnp.concatenate([rim, proj_low], axis=1).astype(F32)
    current = extended[:, 2:, :]
    before_one = extended[:, 1:-1, :]
    before_two = extended[:, :-2, :]
    taps_short = short_weight.astype(F32)
    shorted = (
        taps_short[0] * current
        + keep_one * taps_short[1] * before_one
        + keep_two * taps_short[2] * before_two
        + short_bias.astype(F32)
    )
    gate_out = shorted[:, :, :width]
    gate_in = shorted[:, :, width : 2 * width]
    values = shorted[:, :, 2 * width :]
    carried_low = (gate_in * values).astype(BF16)

    def to_channels(array):
        array = array.reshape(row_count, tok_count, seq_count, lanes).transpose(2, 0, 1, 3)
        return lax.all_to_all(array, "seq", split_axis=0, concat_axis=0, tiled=True)

    def to_positions(array):
        array = lax.all_to_all(array, "seq", split_axis=0, concat_axis=0, tiled=True)
        return array.transpose(1, 2, 0, 3).reshape(row_count, tok_count, width)

    carried = to_channels(carried_low)

    def make_taps(w_one, b_one, w_two, b_two, w_three):
        return filter_taps(w_one, b_one, w_two, b_two, w_three, first_channel, length)

    taps, filter_pull = jax.vjp(
        make_taps,
        f1_weight.astype(F32),
        f1_bias.astype(F32),
        f2_weight.astype(F32),
        f2_bias.astype(F32),
        f3_weight.astype(F32),
    )
    long_filter = WholeSpectra(
        bounds, taps.reshape(seq_count, tok_count, lanes), filter_skip.astype(F32)[None, :]
    )
    long_low = long_filter.forward(carried)
    long_seq = to_positions(long_low).astype(F32)
    mixed_low = (gate_out * long_seq).astype(BF16).reshape(flat_count, width)
    branch = jnp.dot(mixed_low, out_weight, preferred_element_type=F32) + out_bias.astype(F32)
    resid = x_in + branch
    n2, ln2_pull = jax.vjp(layer_norm, resid, ln2_gain.astype(F32), ln2_bias.astype(F32))
    n2_low = n2.astype(BF16)
    pre = jnp.dot(n2_low, up_weight, preferred_element_type=F32) + up_bias.astype(F32)
    act, gelu_pull = jax.vjp(gelu_tanh, pre)
    act_low = act.astype(BF16)
    result = (
        resid
        + jnp.dot(act_low, down_weight, preferred_element_type=F32)
        + down_bias.astype(F32)
    )
    output = result.astype(BF16).reshape(row_count, tok_count, width)
    grad_low = cotangent.reshape(flat_count, width)
    grad_float = grad_low.astype(F32)
    g_down_w = weight_gradient(act_low, grad_low)
    g_down_b = jnp.sum(grad_float, axis=0)
    g_act = back_product(grad_low, down_weight)
    (g_pre,) = gelu_pull(g_act)
    g_pre_low = g_pre.astype(BF16)
    g_up_w = weight_gradient(n2_low, g_pre_low)
    g_up_b = jnp.sum(g_pre_low.astype(F32), axis=0)
    g_n2 = back_product(g_pre_low, up_weight)
    g_resid_part, g_ln2_gain, g_ln2_bias = ln2_pull(g_n2)
    g_resid = grad_float + g_resid_part
    g_branch_low = g_resid.astype(BF16)
    g_out_w = weight_gradient(mixed_low, g_branch_low)
    g_out_b = jnp.sum(g_branch_low.astype(F32), axis=0)
    g_mixed = back_product(g_branch_low, out_weight).reshape(row_count, tok_count, width)
    g_gate_out = g_mixed * long_seq
    g_long_low = (g_mixed * gate_out).astype(BF16)
    g_carried_low, g_taps, g_skip = long_filter.backward(to_channels(g_long_low))
    g_f1_w, g_f1_b, g_f2_w, g_f2_b, g_f3_w = filter_pull(g_taps)
    g_carried_seq = to_positions(g_carried_low).astype(F32)
    g_shorted = jnp.concatenate(
        [g_gate_out, g_carried_seq * values, g_carried_seq * gate_in], axis=-1
    )
    lead_one = keep_one * g_shorted
    lead_two = keep_two * g_shorted
    ahead = passed_along(
        jnp.concatenate([lead_one[:, :2], lead_two[:, :2]], axis=1).astype(BF16), "seq", -1
    ).astype(F32)
    after_one = jnp.concatenate([lead_one[:, 1:], ahead[:, :1]], axis=1)
    after_two = jnp.concatenate([lead_two[:, 2:], ahead[:, 2:4]], axis=1)
    g_proj = taps_short[0] * g_shorted + taps_short[1] * after_one + taps_short[2] * after_two
    g_short_w = jnp.stack(
        [
            jnp.sum(g_shorted * current, axis=(0, 1)),
            jnp.sum(lead_one * before_one, axis=(0, 1)),
            jnp.sum(lead_two * before_two, axis=(0, 1)),
        ],
        axis=0,
    )
    g_short_b = jnp.sum(g_shorted, axis=(0, 1))
    g_proj_low = g_proj.astype(BF16).reshape(flat_count, 3 * width)
    g_in_w = weight_gradient(n1_low, g_proj_low)
    g_in_b = jnp.sum(g_proj_low.astype(F32), axis=0)
    g_n1 = back_product(g_proj_low, in_weight)
    g_x_part, g_ln1_gain, g_ln1_bias = ln1_pull(g_n1)
    grad_tokens = (g_resid + g_x_part).reshape(row_count, tok_count, width)

    def lined(parts):
        flat = jnp.concatenate([part.reshape(-1) for part in parts])
        return jnp.pad(flat, (0, -flat.shape[0] % 128)).reshape(-1, 128)

    net = lined((g_f1_w, g_f1_b, g_f2_w, g_f2_b))
    net_rows = net.shape[0]
    own = lined((g_f3_w, g_skip))
    bits = device_bits()
    seq_bits = int(math.log2(seq_count))
    joint = summed(jnp.concatenate([net, own]), range(seq_bits, bits))
    net = summed(joint[:net_rows], range(seq_bits)).reshape(-1)
    own = joint[net_rows:].reshape(-1)
    g_f1_w, g_f1_b, g_f2_w, g_f2_b = (
        part.reshape(like.shape)
        for part, like in zip(
            jnp.split(net, np.cumsum([f1_weight.size, f1_bias.size, f2_weight.size, f2_bias.size])),
            (f1_weight, f1_bias, f2_weight, f2_bias),
        )
    )
    g_f3_w = own[: f3_weight.size].reshape(f3_weight.shape)
    g_skip = own[f3_weight.size : f3_weight.size + lanes]

    shares = 1 << bits
    vectors = (g_ln2_gain, g_ln2_bias, g_up_b, g_down_b, g_out_b)
    vectors += (g_ln1_gain, g_ln1_bias, g_in_b, g_short_b) + tuple(g_short_w)
    rows = jnp.concatenate([v.reshape(shares, -1) for v in vectors], axis=1)
    sums = small_scattered(rows)
    cuts = np.cumsum([v.shape[0] // shares for v in vectors])[:-1]
    (
        g_ln2_gain,
        g_ln2_bias,
        g_up_b,
        g_down_b,
        g_out_b,
        g_ln1_gain,
        g_ln1_bias,
        g_in_b,
        g_short_b,
        *g_short_w,
    ) = jnp.split(sums, cuts)
    return (
        output,
        grad_tokens,
        g_ln1_gain,
        g_ln1_bias,
        g_in_w,
        g_in_b,
        jnp.stack(g_short_w),
        g_short_b,
        g_f1_w,
        g_f1_b,
        g_f2_w,
        g_f2_b,
        g_f3_w,
        g_skip,
        g_out_w,
        g_out_b,
        g_ln2_gain,
        g_ln2_bias,
        g_up_w,
        g_up_b,
        g_down_w,
        g_down_b,
    )


HALO = 16


def turned_halves(values, share, out_ref, at):
    turned = values.T.astype(BF16)
    for run in range(turned.shape[0] // share):
        into = pl.ds(run // 2 * share, share)
        out_ref[run % 2, into, at] = turned[run * share : (run + 1) * share]


def row_of(ref):
    return ref[...].astype(F32).reshape(1, -1)


def keeps(cuts_ref, first_ref, row, count, lanes):
    spot = lax.broadcasted_iota(jnp.int32, (count, lanes), 0) + first_ref[0]

    def begins(at):
        found = at == 0
        for cut in range(cuts_ref.shape[1]):
            found = found | (at == cuts_ref[row, cut])
        return found

    here, before = begins(spot), begins(spot - 1)
    return jnp.where(here, 0.0, 1.0), jnp.where(here | before, 0.0, 1.0)


def short_filter(values, weight, shift, keep_one, keep_two, begin, count):
    one = pltpu.roll(values, 1, 0)[begin : begin + count]
    two = pltpu.roll(values, 2, 0)[begin : begin + count]
    here = values[begin : begin + count]
    return weight[0:1] * here + keep_one * (weight[1:2] * one) + keep_two * (weight[2:3] * two) + shift


def normed(values):
    center = values - jnp.mean(values, axis=-1, keepdims=True)
    spread = jnp.mean(center * center, axis=-1, keepdims=True)
    scale = lax.rsqrt(spread + eps)
    return center * scale, scale


def in_forward_kernel(
    cuts_ref,
    first_ref,
    before_ref,
    x_ref,
    beyond_ref,
    gain_ref,
    bias_ref,
    w0,
    w1,
    w2,
    b0,
    b1,
    b2,
    s1,
    s2,
    c1,
    c2,
    norm_out,
    proj_out,
    carried_out,
    norm,
):
    rows, count, width = x_ref.shape
    extent = count + 2 * HALO
    group = carried_out.shape[3]

    @pl.when(pl.program_id(0) == 0)
    def _():
        for row in range(rows):
            around = [ref[row].astype(F32) for ref in (before_ref, x_ref, beyond_ref)]
            hat, _ = normed(jnp.concatenate(around, axis=0))
            value = hat * row_of(gain_ref) + row_of(bias_ref)
            norm[row * extent : (row + 1) * extent] = value.astype(BF16)
            turned_halves(
                value[HALO : HALO + count], 32, norm_out, pl.ds(row * count, count)
            )

    parts = []
    for third, (w, b) in enumerate(((w0, b0), (w1, b1), (w2, b2))):
        part = dot32(norm[...], w[...]) + row_of(b)
        low = part.astype(BF16)
        for row in range(rows):
            proj_out[third, row] = low[row * extent : (row + 1) * extent]
        parts.append(low.astype(F32))
    lanes = parts[0].shape[1]
    for row in range(rows):
        keep_one, keep_two = keeps(cuts_ref, first_ref, row, count, lanes)
        sides = [
            short_filter(
                parts[third][row * extent : (row + 1) * extent],
                s[...].astype(F32),
                row_of(c),
                keep_one,
                keep_two,
                HALO,
                count,
            )
            for third, s, c in ((1, s1, c1), (2, s2, c2))
        ]
        carried = (sides[0] * sides[1]).astype(BF16)
        for index in range(lanes // group):
            carried_out[index, row] = carried[:, index * group : (index + 1) * group]


def smem():
    return pl.BlockSpec(memory_space=pltpu.SMEM)


def whole(shape):
    return pl.BlockSpec(shape, lambda i: (0,) * len(shape), pipeline_mode=pl.Buffered(1))


def params():
    return pltpu.CompilerParams(
        vmem_limit_bytes=VMEM_MIB * 2**20, dimension_semantics=("arbitrary",)
    )


def third_block(shape, which, steps):
    lead = (0,) * (len(shape) - 1)
    return pl.BlockSpec(shape, lambda i: lead + (which * steps + i,))


def in_forward(
    cuts, first, before, x, beyond, gain, bias, in_weight, in_bias, short_weight, short_bias, group
):
    rows, count, width = x.shape
    extent = count + 2 * HALO
    lanes = 256
    steps = width // lanes
    return pl.pallas_call(
        in_forward_kernel,
        grid=(steps,),
        in_specs=[smem(), smem(), whole(before.shape), whole(x.shape), whole(beyond.shape)]
        + [whole(gain.shape), whole(bias.shape)]
        + [third_block((width, lanes), t, steps) for t in range(3)]
        + [third_block((lanes,), t, steps) for t in range(3)]
        + [third_block((3, lanes), t, steps) for t in (1, 2)]
        + [third_block((lanes,), t, steps) for t in (1, 2)],
        out_specs=[
            whole((2, width // 2, rows * count)),
            pl.BlockSpec((3, rows, extent, lanes), lambda i: (0, 0, 0, i)),
            pl.BlockSpec((lanes // group, rows, count, group), lambda i: (i, 0, 0, 0)),
        ],
        out_shape=[
            jax.ShapeDtypeStruct((2, width // 2, rows * count), BF16),
            jax.ShapeDtypeStruct((3, rows, extent, width), BF16),
            jax.ShapeDtypeStruct((width // group, rows, count, group), BF16),
        ],
        scratch_shapes=[pltpu.VMEM((rows * extent, width), BF16)],
        compiler_params=params(),
        cost_estimate=MUCH,
        name="in_forward",
    )(
        cuts,
        first,
        before,
        x,
        beyond,
        gain,
        bias,
        *[in_weight] * 3,
        *[in_bias] * 3,
        *[short_weight] * 2,
        *[short_bias] * 2,
    )


def gates(cuts_ref, first_ref, proj_ref, weight_ref, shift_ref, row, index, group):
    at = pl.ds(index * group, group)
    extent = proj_ref.shape[2]
    count = extent - 2 * HALO
    keep_one, keep_two = keeps(cuts_ref, first_ref, row, count, group)
    return short_filter(
        proj_ref[0, row, :, at].astype(F32),
        weight_ref[:, at].astype(F32),
        shift_ref[at].astype(F32).reshape(1, -1),
        keep_one,
        keep_two,
        HALO,
        count,
    )


def middle_forward_kernel(
    cuts_ref,
    first_ref,
    long_ref,
    proj_ref,
    weight_ref,
    shift_ref,
    x_ref,
    out_w_ref,
    out_b_ref,
    gain_ref,
    bias_ref,
    up_ref,
    up_b_ref,
    g_act_ref,
    mixed_out,
    resid_out,
    norm_out,
    act_out,
    split_out,
    g_pre_out,
    g_up_b_out,
    mixed,
    norm,
):
    groups, rows, count, group = long_ref.shape

    @pl.when(pl.program_id(0) == 0)
    def _():
        for row in range(rows):
            own = pl.ds(row * count, count)
            for index in range(groups):
                gate = gates(cuts_ref, first_ref, proj_ref, weight_ref, shift_ref, row, index, group)
                value = gate * long_ref[index, row].astype(F32)
                mixed[own, pl.ds(index * group, group)] = value.astype(BF16)
        for row in range(rows):
            own = pl.ds(row * count, count)
            turned_halves(mixed[own, :].astype(F32), 32, mixed_out, own)
            branch = dot32(mixed[own, :], out_w_ref[...]) + row_of(out_b_ref)
            resid = x_ref[own, :].astype(F32) + branch
            resid_out[own, :] = resid
            hat, _ = normed(resid)
            value = hat * row_of(gain_ref) + row_of(bias_ref)
            norm[own, :] = value.astype(BF16)
            turned_halves(value, 32, norm_out, own)

    pre = dot32(norm[...], up_ref[...]) + row_of(up_b_ref)
    scale = math.sqrt(2.0 / math.pi)
    square = pre * pre
    inner = pre * (scale + (scale * 0.044715) * square)
    half = 0.5 + 0.5 * jnp.tanh(inner)
    act = pre * half
    act_out[...] = act.astype(BF16)
    turned_halves(act, 128, split_out, pl.ds(0, act.shape[0]))
    slope = pre * (2.0 * scale + (6.0 * scale * 0.044715) * square)
    slope = half + slope * (half * (1.0 - half))
    g_pre = (g_act_ref[...].astype(F32) * slope).astype(BF16)
    g_pre_out[...] = g_pre
    g_up_b_out[...] = jnp.sum(g_pre.astype(F32), axis=0, keepdims=True)


def middle_forward(
    cuts, first, long, proj, short_weight, short_bias, x, out_w, out_b, gain, bias, up, up_b, g_act
):
    groups, rows, count, group = long.shape
    extent = proj.shape[2]
    tokens, width = x.shape
    hidden = up.shape[1]
    lanes = width
    steps = hidden // lanes

    def part(height):
        return pl.BlockSpec((height, lanes), lambda i: (0, i))

    return pl.pallas_call(
        middle_forward_kernel,
        grid=(steps,),
        in_specs=[
            smem(),
            smem(),
            whole(long.shape),
            whole((1, rows, extent, width)),
            whole((3, width)),
            whole((width,)),
            whole((tokens, width)),
            whole((width, width)),
            whole((width,)),
            whole((width,)),
            whole((width,)),
            part(width),
            pl.BlockSpec((lanes,), lambda i: (i,)),
            part(tokens),
        ],
        out_specs=[
            whole((2, width // 2, tokens)),
            whole((tokens, width)),
            whole((2, width // 2, tokens)),
            part(tokens),
            pl.BlockSpec((2, lanes // 2, tokens), lambda i: (0, i, 0)),
            part(tokens),
            part(1),
        ],
        out_shape=[
            jax.ShapeDtypeStruct((2, width // 2, tokens), BF16),
            jax.ShapeDtypeStruct((tokens, width), F32),
            jax.ShapeDtypeStruct((2, width // 2, tokens), BF16),
            jax.ShapeDtypeStruct((tokens, hidden), BF16),
            jax.ShapeDtypeStruct((2, hidden // 2, tokens), BF16),
            jax.ShapeDtypeStruct((tokens, hidden), BF16),
            jax.ShapeDtypeStruct((1, hidden), F32),
        ],
        scratch_shapes=[pltpu.VMEM((tokens, width), BF16), pltpu.VMEM((tokens, width), BF16)],
        compiler_params=params(),
        cost_estimate=MUCH,
        name="middle_forward",
    )(
        cuts,
        first,
        long,
        proj,
        short_weight,
        short_bias,
        x,
        out_w,
        out_b,
        gain,
        bias,
        up,
        up_b,
        g_act,
    )


def turned_dot(left, right):
    return lax.dot_general(left, right, (((1,), (1,)), ((), ())), preferred_element_type=F32)


def normed_back(values, grad, gain):
    hat, scale = normed(values)
    inward = grad * gain
    mean = jnp.mean(inward, axis=-1, keepdims=True)
    along = jnp.mean(inward * hat, axis=-1, keepdims=True)
    g_gain = jnp.sum(grad * hat, axis=0, keepdims=True)
    return scale * (inward - mean - hat * along), g_gain, jnp.sum(grad, axis=0, keepdims=True)


def fetched(step, last, sources, targets, sems):
    @pl.when(step == 0)
    def _():
        for k, (source, target) in enumerate(zip(sources, targets)):
            pltpu.make_async_copy(source, target, sems.at[k]).start()

    @pl.when(step == last)
    def _():
        for k, (source, target) in enumerate(zip(sources, targets)):
            pltpu.make_async_copy(source, target, sems.at[k]).wait()


def middle_backward_kernel(
    cuts_ref,
    first_ref,
    long_at,
    proj_at,
    weight_ref,
    shift_ref,
    resid_at,
    grad_at,
    gain_ref,
    out_w_at,
    g_pre_ref,
    up_ref,
    _,
    g_long_out,
    g_gate_out,
    g_resid_out,
    g_branch_out,
    sums_out,
    token_out,
    total,
    long_ref,
    proj_ref,
    resid_ref,
    grad_ref,
    out_w_ref,
    sems,
):
    groups, rows, count, group = long_ref.shape
    step = pl.program_id(0)
    token_out[0] = 0
    fetched(
        step,
        pl.num_programs(0) - 1,
        (long_at, proj_at.at[pl.ds(0, 1)], resid_at, grad_at, out_w_at),
        (long_ref, proj_ref, resid_ref, grad_ref, out_w_ref),
        sems,
    )

    @pl.when(step == 0)
    def _():
        total[...] = turned_dot(g_pre_ref[...], up_ref[...])

    @pl.when(step > 0)
    def _():
        total[...] += turned_dot(g_pre_ref[...], up_ref[...])

    @pl.when(step == pl.num_programs(0) - 1)
    def _():
        sums = [0.0] * 4
        for row in range(rows):
            own = pl.ds(row * count, count)
            grad = grad_ref[own, :].astype(F32)
            back, g_gain, g_bias = normed_back(
                resid_ref[own, :], total[own, :], row_of(gain_ref)
            )
            g_resid = grad + back
            g_resid_out[own, :] = g_resid
            low = g_resid.astype(BF16)
            g_branch_out[own, :] = low
            g_out_b = jnp.sum(low.astype(F32), axis=0, keepdims=True)
            g_down_b = jnp.sum(grad, axis=0, keepdims=True)
            sums = [a + b for a, b in zip(sums, (g_gain, g_bias, g_out_b, g_down_b))]
            total[own, :] = turned_dot(low, out_w_ref[...])
        sums_out[...] = jnp.concatenate(sums + [jnp.zeros_like(sums[0])] * 4, axis=0)
        for row in range(rows):
            own = pl.ds(row * count, count)
            for index in range(groups):
                at = pl.ds(index * group, group)
                g_mixed = total[own, at]
                gate = gates(cuts_ref, first_ref, proj_ref, weight_ref, shift_ref, row, index, group)
                g_gate_out[row, :, at] = g_mixed * long_ref[index, row].astype(F32)
                g_long_out[index, row] = (g_mixed * gate).astype(BF16)


def middle_backward(
    cuts, first, long, proj, short_weight, short_bias, resid, grad, gain, out_w, g_pre, up, ready
):
    groups, rows, count, group = long.shape
    extent = proj.shape[2]
    tokens, width = resid.shape
    hidden = up.shape[1]
    lanes = 1024
    steps = hidden // lanes

    def part(height):
        return pl.BlockSpec((height, lanes), lambda i: (0, i))

    anywhere = pl.BlockSpec(memory_space=pl.ANY)
    return pl.pallas_call(
        middle_backward_kernel,
        grid=(steps,),
        in_specs=[
            smem(),
            smem(),
            anywhere,
            anywhere,
            whole((3, width)),
            whole((width,)),
            anywhere,
            anywhere,
            whole((width,)),
            anywhere,
            part(tokens),
            part(width),
            pl.BlockSpec(memory_space=pl.ANY),
        ],
        out_specs=[
            whole(long.shape),
            whole((rows, count, width)),
            whole((tokens, width)),
            whole((tokens, width)),
            whole((8, width)),
            smem(),
        ],
        out_shape=[
            jax.ShapeDtypeStruct(long.shape, BF16),
            jax.ShapeDtypeStruct((rows, count, width), F32),
            jax.ShapeDtypeStruct((tokens, width), F32),
            jax.ShapeDtypeStruct((tokens, width), BF16),
            jax.ShapeDtypeStruct((8, width), F32),
            jax.ShapeDtypeStruct((1,), jnp.int32),
        ],
        scratch_shapes=[
            pltpu.VMEM((tokens, width), F32),
            pltpu.VMEM(long.shape, BF16),
            pltpu.VMEM((1, rows, extent, width), BF16),
            pltpu.VMEM((tokens, width), F32),
            pltpu.VMEM((tokens, width), BF16),
            pltpu.VMEM((width, width), BF16),
            pltpu.SemaphoreType.DMA((5,)),
        ],
        compiler_params=params(),
        cost_estimate=MUCH,
        name="middle_backward",
    )(
        cuts,
        first,
        long,
        proj,
        short_weight,
        short_bias,
        resid,
        grad,
        gain,
        out_w,
        g_pre,
        up,
        ready,
    )


def in_backward_kernel(
    cuts_ref,
    first_ref,
    g_carried_ref,
    g_gate_ref,
    g_next_ref,
    proj_ref,
    s0,
    s1,
    s2,
    c1,
    c2,
    w0,
    w1,
    w2,
    x_at,
    gain_ref,
    g_resid_at,
    *others,
):
    g_proj_out, sums_out, g_tokens_out, norm_sums_out, token_out = others[-9:-4]
    total, x_ref, g_resid_ref, sems = others[-4:]
    token_out[0] = 0
    fetched(
        pl.program_id(0),
        pl.num_programs(0) - 1,
        (x_at, g_resid_at),
        (x_ref, g_resid_ref),
        sems,
    )
    weights = [s[...].astype(F32) for s in (s0, s1, s2)]
    shifts = [None, row_of(c1), row_of(c2)]
    _, rows, extent, lanes = proj_ref.shape
    count = extent - 2 * HALO
    reach = count + HALO
    group = g_carried_ref.shape[3]
    step = pl.program_id(0)
    sums = [[0.0] * 5 for _ in range(3)]
    for row in range(rows):
        keep_one, keep_two = keeps(cuts_ref, first_ref, row, reach, lanes)
        values = [proj_ref[third, row].astype(F32) for third in range(3)]
        sides = [
            short_filter(
                values[t], weights[t], shifts[t], keep_one, keep_two, HALO, reach
            )
            for t in (1, 2)
        ]
        g_carried = jnp.concatenate(
            [g_carried_ref[index, row] for index in range(lanes // group)], axis=1
        ).astype(F32)
        g_gate = jnp.concatenate([g_gate_ref[row], g_next_ref[row].astype(F32)], axis=0)
        grads = (g_gate, g_carried * sides[1], g_carried * sides[0])
        for third, grad in enumerate(grads):
            weight = weights[third]
            lead_one, lead_two = keep_one * grad, keep_two * grad
            g_proj = (
                weight[0:1] * grad
                + weight[1:2] * pltpu.roll(lead_one, reach - 1, 0)
                + weight[2:3] * pltpu.roll(lead_two, reach - 2, 0)
            )[:count]
            low = g_proj.astype(BF16)
            g_proj_out[third, row * count : (row + 1) * count] = low
            before_one = pltpu.roll(values[third], 1, 0)[HALO : HALO + count]
            before_two = pltpu.roll(values[third], 2, 0)[HALO : HALO + count]
            here = values[third][HALO : HALO + count]
            parts = (
                grad[:count] * here,
                lead_one[:count] * before_one,
                lead_two[:count] * before_two,
                grad[:count],
                low.astype(F32),
            )
            sums[third] = [
                a + jnp.sum(b, axis=0, keepdims=True) for a, b in zip(sums[third], parts)
            ]
    for third in range(3):
        sums_out[third] = jnp.concatenate(
            sums[third] + [jnp.zeros((3, lanes), F32)], axis=0
        )
    product = sum(
        turned_dot(g_proj_out[third], w[...]) for third, w in enumerate((w0, w1, w2))
    )

    @pl.when(step == 0)
    def _():
        total[...] = product

    @pl.when(step > 0)
    def _():
        total[...] += product

    @pl.when(step == pl.num_programs(0) - 1)
    def _():
        norm_sums = [0.0, 0.0]
        for row in range(rows):
            own = pl.ds(row * count, count)
            back, g_gain, g_shift = normed_back(
                x_ref[own, :].astype(F32), total[own, :], row_of(gain_ref)
            )
            g_tokens_out[own, :] = g_resid_ref[own, :] + back
            norm_sums = [norm_sums[0] + g_gain, norm_sums[1] + g_shift]
        norm_sums_out[...] = jnp.concatenate(
            norm_sums + [jnp.zeros((6, x_ref.shape[1]), F32)], axis=0
        )


def in_backward(
    cuts,
    first,
    g_carried,
    g_gate,
    g_next,
    proj,
    short_weight,
    short_bias,
    in_w,
    x,
    gain,
    g_resid,
    ready,
):
    _, rows, extent, width = proj.shape
    count = extent - 2 * HALO
    tokens = rows * count
    group = g_carried.shape[3]
    lanes = 256
    steps = width // lanes

    anywhere = pl.BlockSpec(memory_space=pl.ANY)
    return pl.pallas_call(
        in_backward_kernel,
        grid=(steps,),
        in_specs=[
            smem(),
            smem(),
            pl.BlockSpec((lanes // group, rows, count + HALO, group), lambda i: (i, 0, 0, 0)),
            pl.BlockSpec((rows, count, lanes), lambda i: (0, 0, i)),
            pl.BlockSpec((rows, HALO, lanes), lambda i: (0, 0, i)),
            pl.BlockSpec((3, rows, extent, lanes), lambda i: (0, 0, 0, i)),
        ]
        + [third_block((3, lanes), t, steps) for t in range(3)]
        + [third_block((lanes,), t, steps) for t in (1, 2)]
        + [third_block((width, lanes), t, steps) for t in range(3)]
        + [anywhere, whole((width,)), anywhere]
        + [pl.BlockSpec(memory_space=pl.ANY)] * len(ready),
        out_specs=[
            pl.BlockSpec((3, tokens, lanes), lambda i: (0, 0, i)),
            pl.BlockSpec((3, 8, lanes), lambda i: (0, 0, i)),
            whole((tokens, width)),
            whole((8, width)),
            smem(),
        ],
        out_shape=[
            jax.ShapeDtypeStruct((3, tokens, width), BF16),
            jax.ShapeDtypeStruct((3, 8, width), F32),
            jax.ShapeDtypeStruct((tokens, width), F32),
            jax.ShapeDtypeStruct((8, width), F32),
            jax.ShapeDtypeStruct((1,), jnp.int32),
        ],
        scratch_shapes=[
            pltpu.VMEM((tokens, width), F32),
            pltpu.VMEM((tokens, width), BF16),
            pltpu.VMEM((tokens, width), F32),
            pltpu.SemaphoreType.DMA((2,)),
        ],
        compiler_params=params(),
        cost_estimate=MUCH,
        name="in_backward",
    )(
        cuts,
        first,
        g_carried,
        g_gate,
        g_next,
        proj,
        *[short_weight] * 3,
        *[short_bias] * 2,
        *[in_w] * 3,
        x,
        gain,
        g_resid,
        *ready,
    )


def mark(*others):
    def kernel(*refs):
        refs[-1][0] = 0

    return pl.pallas_call(
        kernel,
        in_specs=[pl.BlockSpec(memory_space=pl.ANY)] * len(others),
        out_specs=smem(),
        out_shape=jax.ShapeDtypeStruct((1,), jnp.int32),
        cost_estimate=LITTLE,
        name="mark",
    )(*others)


def matmul_turned(left, right, columns, ready):
    def kernel(left_ref, right_ref, _, out_ref):
        out_ref[...] = turned_dot(left_ref[...], right_ref[...]).astype(BF16)

    height, depth = left.shape
    width = right.shape[0]
    return pl.pallas_call(
        kernel,
        grid=(width // columns,),
        in_specs=[
            whole((height, depth)),
            pl.BlockSpec((columns, depth), lambda i: (i, 0)),
            pl.BlockSpec(memory_space=pl.ANY),
        ],
        out_specs=pl.BlockSpec((height, columns), lambda i: (0, i)),
        out_shape=jax.ShapeDtypeStruct((height, width), BF16),
        compiler_params=params(),
        cost_estimate=LITTLE,
        name="matmul_turned",
    )(left, right, ready)


def down_forward(resid, act, down, bias, ready):
    tokens, width = resid.shape
    depth = 1024
    steps = act.shape[1] // depth

    def kernel(resid_ref, act_ref, down_ref, bias_ref, *refs):
        out_ref, token_out, total = refs[-3:]
        step = pl.program_id(0)
        token_out[0] = 0
        product = dot32(act_ref[...], down_ref[...])

        @pl.when(step == 0)
        def _():
            total[...] = resid_ref[...] + row_of(bias_ref) + product

        @pl.when(step > 0)
        def _():
            total[...] += product

        @pl.when(step == steps - 1)
        def _():
            out_ref[...] = total[...].astype(BF16)

    return pl.pallas_call(
        kernel,
        grid=(steps,),
        in_specs=[
            whole((tokens, width)),
            pl.BlockSpec((tokens, depth), lambda i: (0, i)),
            pl.BlockSpec((depth, width), lambda i: (i, 0)),
            whole((width,)),
        ]
        + [pl.BlockSpec(memory_space=pl.ANY)] * len(ready),
        out_specs=[whole((tokens, width)), smem()],
        out_shape=[
            jax.ShapeDtypeStruct((tokens, width), BF16),
            jax.ShapeDtypeStruct((1,), jnp.int32),
        ],
        scratch_shapes=[pltpu.VMEM((tokens, width), F32)],
        compiler_params=params(),
        cost_estimate=LITTLE,
        name="down_forward",
    )(resid, act, down, bias, *ready)


def after(value, *others):
    return lax.optimization_barrier((value, others))[0]


def gradient_kernel(counts, order_ref, firsts, seconds, arrived, sent, kept, token, total):
    step = pl.program_id(0)
    token[0] = 0

    def write(values, place):
        if not kept:
            sent[place][...] = values.astype(BF16)
            return
        (send,), (keep,), (total_ref,) = sent, kept, total
        total_ref[...] = values
        share = total_ref.shape[0] // 16
        for spot in range(16):
            piece = pl.ds(pl.multiple_of(order_ref[1 + spot] * share, share), share)
            into = (send, keep)[spot // 8]
            into[pl.ds(spot % 8 * share, share)] = (
                total_ref[piece] + arrived[place][piece].astype(F32)
            ).astype(BF16)

    place = 0
    for steps, first, second in zip(counts, firsts, seconds):
        for _ in range(steps):

            @pl.when(step == place)
            def _(first=first, second=second, place=place):
                write(dot32(first[0], second[...]), place)

            place += 1


def gradient(order, pairs, arrived, ready, columns, cost=LITTLE):
    height, tokens = pairs[0][0].shape[1:]
    counts, first_specs, second_specs, begin = [], [], [], 0
    for first, second in pairs:
        parts = second.shape[-1] // columns
        steps = parts * (second.shape[0] if second.ndim == 3 else 1)
        first_specs.append(pl.BlockSpec((1, height, tokens), lambda i, o: (o[0], 0, 0)))

        def place(i, o, begin=begin, steps=steps, parts=parts, deep=second.ndim == 3):
            at = jnp.clip(i - begin, 0, steps - 1)
            return (at // parts, 0, at % parts) if deep else (0, at)

        shape = (None, tokens, columns) if second.ndim == 3 else (tokens, columns)
        second_specs.append(pl.BlockSpec(shape, place))
        counts.append(steps)
        begin += steps
    single = pl.BlockSpec((height, columns), lambda i, o: (0, 0), pipeline_mode=pl.Buffered(1))
    anywhere = pl.BlockSpec(memory_space=pl.ANY)
    if arrived is None:
        arrived = ()
        sent = [jax.ShapeDtypeStruct((height, columns), BF16)] * begin
        kept, scratch = [], []
        out_specs = [single] * begin
    else:
        sent = [jax.ShapeDtypeStruct((height // 2, begin * columns), BF16)]
        kept, scratch = sent, [pltpu.VMEM((height, columns), F32)]
        out_specs = [pl.BlockSpec((height // 2, columns), lambda i, o: (0, i))] * 2

    def kernel(order_ref, *refs):
        refs = list(refs)

        def take(count):
            taken, refs[:] = refs[:count], refs[count:]
            return taken

        firsts, seconds, arrived_refs = take(len(pairs)), take(len(pairs)), take(len(arrived))
        take(len(ready))
        sent_refs, kept_refs, (token,) = take(len(sent)), take(len(kept)), take(1)
        gradient_kernel(
            counts, order_ref, firsts, seconds, arrived_refs, sent_refs, kept_refs, token, refs
        )

    inputs = [p[0] for p in pairs] + [p[1] for p in pairs] + list(arrived) + list(ready)
    outputs = sent + kept + [jax.ShapeDtypeStruct((1,), jnp.int32)]
    return pl.pallas_call(
        kernel,
        grid_spec=pltpu.PrefetchScalarGridSpec(
            num_scalar_prefetch=1,
            grid=(begin,),
            in_specs=first_specs
            + second_specs
            + [single] * len(arrived)
            + [anywhere] * len(ready),
            out_specs=out_specs + [smem()],
            scratch_shapes=scratch,
        ),
        out_shape=outputs,
        compiler_params=params(),
        cost_estimate=cost,
        name="gradient",
    )(order, *inputs)


def to_sibling(blocks):
    return [swapped(block, lambda one: 1) for block in blocks]


def bit_of(index, bit):
    return (index >> bit) & 1


def choose_bit(index, bit, axis):
    def choose(array, mine):
        own = bit_of(index, bit)
        return pick(array, own if mine else 1 - own, axis)

    return choose


def choose_second(index, axis):
    def choose(array, mine):
        own = jnp.where(bit_of(index, 0) == 0, bit_of(index, 2), bit_of(index, 1))
        return pick(array, own if mine else 1 - own, axis)

    return choose


def choose_first(index, axis):
    def choose(array, mine):
        low, high = bit_of(index, 1), bit_of(index, 2)
        if not mine:
            low, high = 1 - low, 1 - high
        core = bit_of(index, 0)
        return jnp.stack(
            [
                pick(array, jnp.where(core == 0, 2 * j + low, 2 * high + j), axis)
                for j in range(2)
            ],
            axis=axis,
        )

    return choose


def swap_bit(bit):
    return lambda value: swapped(value, lambda one: 1 << bit)


def swap_first(value):
    return swapped(value, lambda one: 4 if one & 1 else 2)


def swap_second(value):
    return swapped(value, lambda one: 2 if one & 1 else 4)


def order_first(index):
    core, low, high = bit_of(index, 0), bit_of(index, 1), bit_of(index, 2)

    def some(low, high):
        return [
            4 * z + jnp.where(core == 0, 2 * j + low, 2 * high + j) for z in range(4) for j in range(2)
        ]

    return jnp.stack([core] + some(1 - low, 1 - high) + some(low, high)).astype(jnp.int32)


def stage_sent(kept, arrived, choose):
    return added(choose(kept, False), choose(arrived, False), BF16)


def stage(kept, arrived, choose):
    sent = stage_sent(kept, arrived, choose)
    return sent, added(choose(kept, True), choose(arrived, True), BF16)


def finished(kept, arrived, own, last, cuts, ready):
    rows, width = last.shape[-2:]
    last = last.reshape(rows, width)

    def kernel(own_ref, kept_ref, arrived_ref, last_ref, *refs):
        outs = refs[len(ready) : len(ready) + len(cuts)]
        refs[-1][0] = 0
        begin = 0
        for out, size in zip(outs, cuts):
            at = slice(begin, begin + size)
            first = kept_ref[:, at].astype(F32) + arrived_ref[:, at].astype(F32)
            out[...] = first + last_ref[:, at].astype(F32)
            begin += size

    half = pl.BlockSpec((None, rows, width), lambda i, o: (o[0], 0, 0))

    def flat(columns):
        return pl.BlockSpec((rows, columns), lambda i, o: (0, 0))

    *outs, token = pl.pallas_call(
        kernel,
        grid_spec=pltpu.PrefetchScalarGridSpec(
            num_scalar_prefetch=1,
            grid=(1,),
            in_specs=[half, half, flat(width)]
            + [pl.BlockSpec(memory_space=pl.ANY)] * len(ready),
            out_specs=[flat(size) for size in cuts] + [smem()],
        ),
        out_shape=[jax.ShapeDtypeStruct((rows, size), F32) for size in cuts]
        + [jax.ShapeDtypeStruct((1,), jnp.int32)],
        compiler_params=params(),
        cost_estimate=LITTLE,
        name="finished",
    )(
        own.astype(jnp.int32).reshape(1),
        kept.reshape(2, rows, width),
        arrived.reshape(2, rows, width),
        last,
        *ready,
    )
    return outs, token


def paired(values):
    while len(values) > 1:
        values = [values[k] + values[k + 1] for k in range(0, len(values), 2)]
    return values[0]


def summed_lines(values, top, ready, cut=True):
    rows, lanes = values[0].shape
    rest = top if cut else 0
    count = len(values)

    def kernel(*refs):
        total = paired([ref[...] for ref in refs[:count]])
        refs[-3][...] = total[:top]
        refs[-2][...] = total[rest:]
        refs[-1][0] = 0

    return pl.pallas_call(
        kernel,
        grid=(1,),
        in_specs=[whole((rows, lanes))] * count + [pl.BlockSpec(memory_space=pl.ANY)] * len(ready),
        out_specs=[whole((top, lanes)), whole((rows - rest, lanes)), smem()],
        out_shape=[
            jax.ShapeDtypeStruct((top, lanes), F32),
            jax.ShapeDtypeStruct((rows - rest, lanes), F32),
            jax.ShapeDtypeStruct((1,), jnp.int32),
        ],
        compiler_params=params(),
        cost_estimate=LITTLE,
        name="summed_lines",
    )(*values, *ready)


def unpacked(seq, seq_count, top, values, units, bands, sizes, ready):
    lanes = top.shape[1]
    count = len(values)

    def kernel(seq_ref, top_ref, *refs):
        outs, below, token = refs[count + len(ready) : -2], refs[-1], refs[-2]
        token[0] = 0
        below[...] = paired([ref[...] for ref in refs[:count]])
        f1_w, f1_b, f2_w, f2_b, f3_w, skip = outs[:6]
        f3_w[...] = top_ref[:units]
        skip[...] = top_ref[units]
        f2_w[...] = below[:units, :units]
        f1_w[...] = below[:bands, units:]
        f1_b[...] = below[bands, units:]
        f2_b[...] = below[bands + 1, units:]
        line, seq = units, seq_ref[0]
        outs = list(outs[6:])
        for kinds, size in sizes:
            begin = seq * size
            for kind in range(kinds):
                at = line + begin // lanes
                two = jnp.concatenate([below[pl.ds(at, 1)], below[pl.ds(at + 1, 1)]], axis=1)
                shift = lax.rem(2 * lanes - begin % lanes, 2 * lanes)
                outs.pop(0)[...] = pltpu.roll(two, shift, 1)[0, :size]
                line += size * seq_count // lanes

    shapes = [(bands, units), (units,), (units, units), (units,), (units, lanes), (lanes,)]
    shapes += [(size,) for kinds, size in sizes for _ in range(kinds)]
    return pl.pallas_call(
        kernel,
        grid=(1,),
        in_specs=[smem(), whole(top.shape)]
        + [whole(values[0].shape)] * count
        + [pl.BlockSpec(memory_space=pl.ANY)] * len(ready),
        out_specs=[whole(shape) for shape in shapes] + [smem()],
        out_shape=[jax.ShapeDtypeStruct(shape, F32) for shape in shapes]
        + [jax.ShapeDtypeStruct((1,), jnp.int32)],
        scratch_shapes=[pltpu.VMEM(values[0].shape, F32)],
        compiler_params=params(),
        cost_estimate=LITTLE,
        name="unpacked",
    )(seq, top, *values, *ready)


def block_device(
    tokens,
    cotangent,
    bounds,
    ln1_gain,
    ln1_bias,
    in_weight,
    in_bias,
    short_weight,
    short_bias,
    f1_weight,
    f1_bias,
    f2_weight,
    f2_bias,
    f3_weight,
    filter_skip,
    out_weight,
    out_bias,
    ln2_gain,
    ln2_bias,
    up_weight,
    up_bias,
    down_weight,
    down_bias,
):
    seq_count = lax.axis_size("seq")
    rows, count, width = tokens.shape
    flat = rows * count
    length = count * seq_count
    lanes = f3_weight.shape[1]
    first_channel = (lax.axis_index("seq") * lanes).astype(jnp.int32)
    first = (lax.axis_index("seq") * count).astype(jnp.int32).reshape(1)

    def exchanged(array):
        return lax.all_to_all(array, "seq", split_axis=0, concat_axis=0, tiled=True)

    index = device_index()
    before = passed_along(tokens[:, count - HALO :], "seq", 1)
    beyond = passed_along(tokens[:, :HALO], "seq", -1)
    norm_halves, proj, carried_own = in_forward(
        bounds,
        first,
        before,
        tokens,
        beyond,
        ln1_gain,
        ln1_bias,
        in_weight,
        in_bias,
        short_weight,
        short_bias,
        lanes,
    )
    carried = exchanged(carried_own)

    tables = transform_tables(count)
    table = piece_table(bounds, seq_count, count)
    skip = filter_skip
    taps_spec, kept = taps_and_spectrum(
        first_channel.reshape(1),
        seq_count,
        count,
        f1_weight,
        f1_bias,
        f2_weight,
        f2_bias,
        f3_weight,
        tables,
        carried_own,
    )
    long_own = long_forward(table, carried, taps_spec, skip, tables)
    long = exchanged(long_own)
    x = tokens.reshape(flat, width)
    grad = cotangent.reshape(flat, width)
    g_act = matmul_turned(grad, down_weight, 1024, long_own)
    mixed_halves, resid, norm2_halves, act, act_halves, g_pre, g_up_b = middle_forward(
        bounds,
        first,
        long,
        proj,
        short_weight,
        short_bias,
        x,
        out_weight,
        out_bias,
        ln2_gain,
        ln2_bias,
        up_weight,
        up_bias,
        g_act,
    )
    first_order = order_first(index)
    send_order = (1 - bit_of(index, 0)).astype(jnp.int32).reshape(1)
    down_pairs = [(act_halves, grad)]
    *down_sent, _ = gradient(send_order, down_pairs, None, (), 512)
    down_arrived = to_sibling(down_sent)
    *up_sent, _ = gradient(send_order, [(norm2_halves, g_pre)], None, down_sent, 1024)
    up_arrived = to_sibling(up_sent)
    down_send, down_keep, _ = gradient(first_order, down_pairs, down_arrived, up_sent, 512)
    down_arrived = swap_first(down_send)
    g_long, g_gate, g_resid, g_branch, middle_sums, token = middle_backward(
        bounds,
        first,
        long,
        proj,
        short_weight,
        short_bias,
        resid,
        grad,
        ln2_gain,
        out_weight,
        g_pre,
        up_weight,
        down_send,
    )
    g_long_all = exchanged(g_long)
    g_next = passed_along(g_gate[:, :HALO].astype(BF16), "seq", -1)

    def shaped(array, lead):
        return array.reshape(lead + (-1, array.shape[-1]))

    *out_sent, _ = gradient(send_order, [(mixed_halves, g_branch)], None, (), 1024)
    up_send, up_keep, token = gradient(
        first_order,
        [(norm2_halves, g_pre), (mixed_halves, g_branch)],
        up_arrived + to_sibling(out_sent),
        (),
        1024,
    )
    up_arrived = swap_first(up_send)
    down_send, down_keep = stage(
        shaped(down_keep, (2, 2, 2)),
        shaped(down_arrived, (2, 2, 2)),
        choose_bit(index + token[0], 3, 1),
    )
    down_arrived = swap_bit(3)(down_send)
    g_series, g_taps, g_skip, token = long_backward(
        table, g_long_all, carried, taps_spec, skip, tables, (up_send, down_send)
    )
    g_carried = exchanged(g_series)
    output, token = down_forward(resid, act, down_weight, down_bias, (g_series,))
    output = output.reshape(rows, count, width)
    later = index + token[0]
    down_send, down_keep = stage(down_keep, down_arrived, choose_bit(later, 4, 0))
    down_arrived = swap_bit(4)(down_send)
    up_send, up_keep = stage(
        shaped(up_keep, (4, 2)), shaped(up_arrived, (4, 2)), choose_second(later, 1)
    )
    up_arrived = swap_second(up_send)
    g_proj, short_sums, g_tokens, norm_sums, token = in_backward(
        bounds,
        first,
        g_carried,
        g_gate,
        g_next,
        proj,
        short_weight,
        short_bias,
        in_weight,
        x,
        ln1_gain,
        g_resid,
        (down_send, up_send),
    )
    later = index + token[0]
    down_send = stage_sent(down_keep, down_arrived, choose_second(later, 0))
    down_last = swap_second(down_send)
    up_send, up_keep = stage(
        shaped(up_keep, (2, 2)), shaped(up_arrived, (2, 2)), choose_bit(later, 3, 1)
    )
    up_arrived = swap_bit(3)(up_send)
    in_pairs = [(norm_halves, g_proj)]
    *in_sent, _ = gradient(send_order, in_pairs, None, (down_send, up_send), 1024, MUCH)
    in_send, in_keep, token = gradient(first_order, in_pairs, to_sibling(in_sent), (), 1024)
    in_arrived = swap_first(in_send)
    row_count = lax.axis_size("rows")
    seq_bits = seq_count.bit_length() - 1
    payloads = filter_backward(
        first_channel.reshape(1),
        lax.axis_index("rows").astype(jnp.int32).reshape(1),
        row_count,
        g_taps.reshape(length, lanes),
        kept,
        f2_weight,
        f3_weight,
        g_skip,
        (middle_sums, g_up_b, norm_sums, short_sums),
        (in_send,),
    )
    arrived = [payloads[0]] + [
        swapped(payloads[k], lambda one, k=k: k << seq_bits) for k in range(1, row_count)
    ]
    later = index + mark(*payloads)[0]
    up_send = stage_sent(up_keep, up_arrived, choose_bit(later, 4, 0))
    up_last = swap_bit(4)(up_send)
    left = jnp.where(bit_of(index, 0) == 0, bit_of(index, 2), bit_of(index, 1))
    (g_down_w,), token = finished(
        down_keep, down_arrived, left, down_last, (width,), (up_send,)
    )
    units, bands = f3_weight.shape[0], f1_weight.shape[0]
    top, mine, token = summed_lines(arrived, units + 8, (token,))
    in_send, in_keep = stage(
        shaped(in_keep, (4, 2)),
        shaped(in_arrived, (4, 2)),
        choose_second(index + token[0], 1),
    )
    in_arrived = swap_second(in_send)
    arrived = swapped(mine, lambda one: 1)
    _, mine, token = summed_lines([mine, arrived], 8, (in_send,), False)
    in_send, in_keep = stage(
        shaped(in_keep, (2, 2)), shaped(in_arrived, (2, 2)), choose_bit(index + token[0], 3, 1)
    )
    in_arrived = swap_bit(3)(in_send)
    arrived = swapped(mine, lambda one: 2)
    _, mine, token = summed_lines([mine, arrived], 8, (in_send,), False)
    (g_up_w, g_out_w), token = finished(
        up_keep, up_arrived, bit_of(index, 4), up_last, (up_weight.shape[1], width), (token,)
    )
    in_send = stage_sent(in_keep, in_arrived, choose_bit(index + token[0], 4, 0))
    in_last = swap_bit(4)(in_send)
    arrived = swapped(mine, lambda one: 4)
    shares = 1 << device_bits()
    sizes = ((6, width // shares), (1, up_weight.shape[1] // shares), (5, 3 * width // shares))
    seq = lax.axis_index("seq").astype(jnp.int32).reshape(1)
    *small, token = unpacked(
        seq, seq_count, top, [mine, arrived], units, bands, sizes, (in_send,)
    )
    (g_in_w,), _ = finished(
        in_keep, in_arrived, bit_of(index, 4), in_last, (3 * width,), (token,)
    )
    (g_f1_w, g_f1_b, g_f2_w, g_f2_b, g_f3_w, g_skip, *small) = small
    (g_ln2_gain, g_ln2_bias, g_out_b, g_down_b, g_ln1_gain, g_ln1_bias, g_up_b, *small) = small
    *g_short_w, g_short_b, g_in_b = small
    g_short_w = jnp.stack(g_short_w)
    grad_tokens = g_tokens.reshape(rows, count, width)
    return (
        output,
        grad_tokens,
        g_ln1_gain,
        g_ln1_bias,
        g_in_w,
        g_in_b,
        g_short_w,
        g_short_b,
        g_f1_w,
        g_f1_b,
        g_f2_w,
        g_f2_b,
        g_f3_w,
        g_skip,
        g_out_w,
        g_out_b,
        g_ln2_gain,
        g_ln2_bias,
        g_up_w,
        g_up_b,
        g_down_w,
        g_down_b,
    )


def per_device(tokens, *others):
    shares = lax.axis_size("rows") * lax.axis_size("seq")
    count, width = tokens.shape[1:]
    hidden = others[20].shape[0]
    lanes = width // lax.axis_size("seq")
    fits = shares == 32 and width == 1024 and hidden == 4096 and lanes == 128 and count % 128 == 0
    return (block_device if fits else plain_device)(tokens, *others)


def solution(mesh):
    return jax.shard_map(
        per_device,
        mesh=mesh,
        in_specs=(
            P("rows", "seq", None),
            P("rows", "seq", None),
            P("rows", None),
            P(),
            P(),
            P(),
            P(),
            P(),
            P(),
            P(),
            P(),
            P(),
            P(),
            P(None, "seq"),
            P("seq"),
            P(),
            P(),
            P(),
            P(),
            P(),
            P(),
            P(),
            P(),
        ),
        out_specs=(
            P("rows", "seq", None),
            P("rows", "seq", None),
            P(("rows", "seq")),
            P(("rows", "seq")),
            P(("rows", "seq"), None),
            P(("rows", "seq")),
            P(None, ("rows", "seq")),
            P(("rows", "seq")),
            P(),
            P(),
            P(),
            P(),
            P(None, "seq"),
            P("seq"),
            P(("rows", "seq"), None),
            P(("rows", "seq")),
            P(("rows", "seq")),
            P(("rows", "seq")),
            P(("rows", "seq"), None),
            P(("rows", "seq")),
            P(("rows", "seq"), None),
            P(("rows", "seq")),
        ),
        check_vma=False,
    )
```

```python
import functools
import math

import jax
import jax.numpy as jnp
import ml_dtypes
import numpy as np
from jax import lax
from jax.experimental import pallas as pl
from jax.experimental.pallas import tpu as pltpu
from jax.sharding import PartitionSpec as P

D = 1024
EMB = 33
HIGH = lax.Precision.HIGHEST
eps = 1e-05
slow_rate = math.log(100.0) / 1.5
fast_rate = math.log(100.0) / 0.3
BOTH = ("rows", "seq")
F32 = jnp.float32
BF16 = jnp.bfloat16
VMEM_MIB = 58
LITTLE = pl.CostEstimate(flops=1, bytes_accessed=1, transcendentals=0)
MUCH = pl.CostEstimate(flops=5 * 10**10, bytes_accessed=2 * 10**8, transcendentals=0)


def passed_along(value, axis, steps):
    count = lax.axis_size(axis)
    first, last = (max(0, -steps), min(count, count - steps))
    return lax.ppermute(value, axis, [(source, source + steps) for source in range(first, last)])


def layer_norm(values, gain, shift):
    center = values - jnp.mean(values, axis=-1, keepdims=True)
    spread = jnp.mean(center * center, axis=-1, keepdims=True)
    return center * lax.rsqrt(spread + eps) * gain + shift


def gelu_tanh(values):
    return jax.nn.gelu(values, approximate=True)


def features(length):
    steps = np.arange(length, dtype=np.float64)
    bands = (EMB - 1) // 2
    freqs = 0.0001 + np.arange(bands, dtype=np.float64) * ((bands - 1 - 0.0001) / (bands - 1))
    angles = (steps * (2.0 * math.pi / length))[:, None] * freqs[None, :]
    timeline = steps / (length - 1)
    table = np.concatenate([timeline[:, None], np.cos(angles), -np.sin(angles)], axis=1)
    return jnp.asarray(table.astype(np.float32)), jnp.asarray(timeline.astype(np.float32))


def filter_taps(w_one, b_one, w_two, b_two, w_three, first, length):
    feats, timeline = features(length)
    hidden = jnp.sin(jnp.dot(feats, w_one, precision=HIGH) + b_one)
    hidden = jnp.sin(jnp.dot(hidden, w_two, precision=HIGH) + b_two)
    raw_taps = jnp.dot(hidden, w_three, precision=HIGH)
    channels = (first + jnp.arange(w_three.shape[1], dtype=jnp.int32)).astype(F32)
    rates = slow_rate + channels * ((fast_rate - slow_rate) / (D - 1))
    return raw_taps * jnp.exp(-timeline[:, None] * rates[None, :])


def close_dot(left, right, dims):
    def one(a, b):
        return lax.dot_general(a, b, (dims, ((), ())), preferred_element_type=F32)

    (a, a_rest), (b, b_rest) = split32(left), split32(right)
    return one(a, b) + one(a, b_rest) + one(a_rest, b)


def line_up(out_ref, count, parts):
    line = 0
    for ref, lead, rows in parts:
        width = ref.shape[-1]
        share = rows * width // count // 128
        for z in range(count):
            for k in range(share):
                at = (z * share + k) * 128
                row, lane = at // width, at % width
                index = ((row,) if rows > 1 else ()) + tuple(lead)
                value = ref[index + (slice(lane, lane + 128),)]
                out_ref[z, line + k : line + k + 1] = value.reshape(1, 128)
        line += share


def filter_backward_kernel(
    first_ref,
    row_ref,
    grad_ref,
    feats_ref,
    one_ref,
    two_ref,
    w2_ref,
    w3_ref,
    skip_ref,
    middle_ref,
    up_ref,
    norm_ref,
    short_ref,
    outs,
    lines,
    out_ref,
):
    lines[...] = jnp.zeros_like(lines)
    parts = [(middle_ref, (k,), 1) for k in range(4)] + [(norm_ref, (k,), 1) for k in range(2)]
    parts += [(up_ref, (0,), 1)] + [(short_ref, (k,), 3) for k in range(5)]
    line_up(lines, len(outs), parts)
    length, lanes = grad_ref.shape
    units = one_ref.shape[1] // 2
    bands = feats_ref.shape[1]
    inner = grad_ref[...] * decay(first_ref, 0, length, lanes, length)
    over_time, over_last = ((0,), (0,)), ((1,), (1,))
    out_ref[...] = jnp.zeros_like(out_ref)
    out_ref[:units] = close_dot(two_ref[:, :units], inner, over_time)
    out_ref[units : units + 1] = skip_ref[...]
    two = close_dot(inner, w3_ref[...].astype(F32), over_last) * two_ref[:, units:]
    one = close_dot(two, w2_ref[...].astype(F32), over_last) * one_ref[:, units:]
    below = units + 8
    out_ref[below : below + units, :units] = close_dot(one_ref[:, :units], two, over_time)
    out_ref[below : below + bands, units:] = close_dot(feats_ref[...], one, over_time)
    out_ref[below + bands : below + bands + 1, units:] = jnp.sum(one, axis=0, keepdims=True)
    out_ref[below + bands + 1 : below + bands + 2, units:] = jnp.sum(two, axis=0, keepdims=True)
    for k, payload in enumerate(outs):
        payload[: 2 * units + 8] = out_ref[...]
        payload[2 * units + 8 :] = lines[row_ref[0] ^ k]


LINES = 56


def filter_backward(first, row, count, g_taps, kept, w_two, w_three, g_skip, sums, ready):
    feats, one, two = kept
    units, lanes = w_three.shape
    vmem = pl.BlockSpec(memory_space=pltpu.VMEM)
    height = 2 * units + 8

    def kernel(*refs):
        outs, scratch = refs[13 + len(ready) : -2], refs[-2:]
        filter_backward_kernel(*refs[:13], outs, *scratch)

    return pl.pallas_call(
        kernel,
        in_specs=[smem()] * 2 + [vmem] * 11 + [pl.BlockSpec(memory_space=pl.ANY)] * len(ready),
        out_specs=[vmem] * count,
        out_shape=[jax.ShapeDtypeStruct((height + LINES, lanes), F32)] * count,
        scratch_shapes=[
            pltpu.VMEM((count, LINES, lanes), F32),
            pltpu.VMEM((height, lanes), F32),
        ],
        compiler_params=pltpu.CompilerParams(vmem_limit_bytes=VMEM_MIB * 2**20),
        cost_estimate=MUCH,
        name="filter_backward",
    )(first, row, g_taps, feats, one, two, w_two, w_three, g_skip, *sums, *ready)


def split16(values):
    high = values.astype(ml_dtypes.bfloat16)
    return high, (values - high.astype(np.float64)).astype(ml_dtypes.bfloat16)


def transform_tables(block):
    freq = np.arange(block)[:, None]
    time = np.arange(block)[None, :]
    angles = ((2 * freq + 1) * time % (4 * block)) * (math.pi / (2 * block))
    ahead = np.concatenate([np.cos(angles), -np.sin(angles)], axis=0)
    ahead_high, ahead_low = split16(ahead)
    back_high, back_low = split16(ahead.T / block)
    return tuple(jnp.asarray(t) for t in (ahead_high, ahead_low, back_high, back_low))


def piece_table(bounds, blocks, block):
    length = blocks * block
    edges = jnp.broadcast_to(jnp.arange(blocks, dtype=jnp.int32) * block, (bounds.shape[0], blocks))
    for cut in range(bounds.shape[1]):
        one = bounds[:, cut : cut + 1]
        low = jnp.concatenate([jnp.full_like(one, -1), edges], axis=1)
        high = jnp.concatenate([edges, jnp.full_like(one, length)], axis=1)
        edges = jnp.maximum(low, jnp.minimum(one, high))
    ends = jnp.concatenate([edges[:, 1:], jnp.full_like(edges[:, :1], length)], axis=1)
    index = jnp.minimum(edges // block, blocks - 1)
    start = jnp.max(
        jnp.where(bounds[:, :, None] <= edges[:, None, :], bounds[:, :, None], 0), axis=1
    )
    stop = jnp.min(
        jnp.where(bounds[:, :, None] > edges[:, None, :], bounds[:, :, None], length), axis=1
    )
    empty = ends <= edges
    earlier = jnp.where(empty, 0, index - start // block + 1)
    later = jnp.where(empty, 0, (stop - 1) // block - index + 1)
    return jnp.stack([edges, ends, index, earlier, later]).astype(jnp.int32)


def dot32(left, right):
    return jnp.dot(left, right, preferred_element_type=F32)


def split32(values):
    high = values.astype(BF16)
    return high, (values - high.astype(F32)).astype(BF16)


def wide_dot(high, low, values):
    top, rest = split32(values)
    return dot32(high, top) + dot32(high, rest) + dot32(low, top)


def alternating(rows, lanes):
    odd = lax.broadcasted_iota(jnp.int32, (rows, lanes), 0) % 2
    return 1.0 - 2.0 * odd.astype(F32)


def sine_cosine(angle):
    turns = jnp.floor(angle * (2.0 / math.pi) + 0.5)
    rest = angle - turns * 1.5703125
    rest = rest - turns * 4.837512969970703125e-4
    rest = rest - turns * 7.549789948768648e-8
    square = rest * rest
    sine = ((-1.9515295891e-4 * square + 8.3321608736e-3) * square - 1.6666654611e-1) * square
    sine = sine * rest + rest
    cosine = (2.443315711809948e-5 * square - 1.388731625493765e-3) * square
    cosine = (cosine + 4.166664568298827e-2) * square * square - 0.5 * square + 1.0
    quarter = turns.astype(jnp.int32)
    swap = (quarter & 1) == 1
    sine, cosine = jnp.where(swap, cosine, sine), jnp.where(swap, sine, cosine)
    return (
        jnp.where((quarter & 2) == 2, -sine, sine),
        jnp.where(((quarter + 1) & 2) == 2, -cosine, cosine),
    )


def near_dot(left, right):
    top, rest = split32(left)
    return dot32(top, right) + dot32(rest, right)


def decay(first_ref, begin, count, lanes, length):
    spot = (lax.broadcasted_iota(jnp.int32, (count, lanes), 0) + begin).astype(F32)
    channel = (lax.broadcasted_iota(jnp.int32, (1, lanes), 1) + first_ref[0]).astype(F32)
    rates = slow_rate + channel * ((fast_rate - slow_rate) / (D - 1))
    return jnp.exp(-(spot * (1.0 / (length - 1))) * rates)


def taps_kernel(
    first_ref, feats_ref, w1, b1, w2, b2, w3, high_ref, low_ref, _, out_ref, one_ref, two_ref, own
):
    blocks, double, lanes = out_ref.shape
    block = double // 2
    for k in range(blocks):
        at = slice(k * block, (k + 1) * block)
        sine, cosine = sine_cosine(near_dot(feats_ref[at], w1[...]) + row_of(b1))
        one_ref[at] = jnp.concatenate([sine, cosine], axis=1)
        sine, cosine = sine_cosine(near_dot(sine, w2[...]) + row_of(b2))
        two_ref[at] = jnp.concatenate([sine, cosine], axis=1)
        taps = near_dot(sine, w3[...]) * decay(first_ref, k * block, block, lanes, blocks * block)
        own[k] = wide_dot(high_ref[...], low_ref[...], taps)
    sign = alternating(block, lanes)
    out_ref[0] = own[0]
    for k in range(1, blocks):
        out_ref[k, :block] = own[k, :block] - sign * own[k - 1, block:]
        out_ref[k, block:] = own[k, block:] + sign * own[k - 1, :block]


def taps_and_spectrum(first, blocks, block, w1, b1, w2, b2, w3, tables, ready):
    lanes, units = w3.shape[1], w2.shape[0]
    length = blocks * block
    feats, _ = features(length)
    vmem = pl.BlockSpec(memory_space=pltpu.VMEM)
    spectra, one, two = pl.pallas_call(
        taps_kernel,
        in_specs=[smem()] + [vmem] * 8 + [pl.BlockSpec(memory_space=pl.ANY)],
        out_specs=[vmem] * 3,
        out_shape=[jax.ShapeDtypeStruct((blocks, 2 * block, lanes), F32)]
        + [jax.ShapeDtypeStruct((length, 2 * units), F32)] * 2,
        scratch_shapes=[pltpu.VMEM((blocks, 2 * block, lanes), F32)],
        compiler_params=pltpu.CompilerParams(vmem_limit_bytes=VMEM_MIB * 2**20),
        cost_estimate=LITTLE,
        name="taps_and_spectrum",
    )(first, feats, w1, b1, w2, b2, w3, tables[0], tables[1], ready)
    return spectra, (feats, one, two)


def piece_mask(table_ref, row, piece, block, lanes):
    at = table_ref[2, row, piece]
    spot = lax.broadcasted_iota(jnp.int32, (block, lanes), 0) + at * block
    return at, (spot >= table_ref[0, row, piece]) & (spot < table_ref[1, row, piece])


def piece_spectra(table_ref, series_ref, ahead_ref, out_ref):
    blocks, rows, block, lanes = series_ref.shape
    for piece in range(out_ref.shape[0]):
        parts = []
        for row in range(rows):
            at, inside = piece_mask(table_ref, row, piece, block, lanes)
            values = series_ref[at, row].astype(F32)
            parts.append(jnp.where(inside, values, 0.0).astype(BF16))
        out_ref[piece] = dot32(ahead_ref[...], jnp.concatenate(parts, axis=1))


def each_piece(table_ref, which, pieces, rows, lanes, blocks, visit):
    def body(index, carry):
        piece, row = index // rows, index % rows
        lane = pl.ds(pl.multiple_of(row * lanes, lanes), lanes)
        found = table_ref[which, row, piece]
        for count in range(blocks + 1):

            @pl.when(found == count)
            def _(count=count):
                visit(piece, lane, count)

        return carry

    lax.fori_loop(0, pieces * rows, body, 0)


def halves_of(block, tile):
    for begin in range(0, block, tile):
        yield pl.ds(begin, tile), pl.ds(block + begin, tile)


def couple(table_ref, step, taps_ref, series_ref, into_ref):
    blocks, double, lanes = taps_ref.shape
    block = double // 2
    pieces, _, both = series_ref.shape

    def visit(piece, lane, count):
        for real_rows, imag_rows in halves_of(block, 32):
            real = imag = jnp.zeros((32, lanes), F32)
            for k in range(count):
                tap_r, tap_i = taps_ref[k, real_rows, :], taps_ref[k, imag_rows, :]
                val_r = series_ref[piece + step * k, real_rows, lane]
                val_i = series_ref[piece + step * k, imag_rows, lane]
                if step > 0:
                    real = real + (tap_r * val_r + tap_i * val_i)
                    imag = imag + (tap_r * val_i - tap_i * val_r)
                else:
                    real = real + (tap_r * val_r - tap_i * val_i)
                    imag = imag + (tap_r * val_i + tap_i * val_r)
            into_ref[piece, real_rows, lane] = real
            into_ref[piece, imag_rows, lane] = imag

    each_piece(table_ref, 3 if step < 0 else 4, pieces, both // lanes, lanes, blocks, visit)


def correlate(table_ref, series_ref, grad_ref, into_ref):
    blocks, double, lanes = into_ref.shape
    block = double // 2
    pieces, _, both = series_ref.shape
    into_ref[...] = jnp.zeros_like(into_ref)

    def visit(piece, lane, count):
        for real_rows, imag_rows in halves_of(block, 32):
            if count:
                out_r, out_i = grad_ref[piece, real_rows, lane], grad_ref[piece, imag_rows, lane]
            for k in range(count):
                val_r = series_ref[piece - k, real_rows, lane]
                val_i = series_ref[piece - k, imag_rows, lane]
                into_ref[k, real_rows, :] += val_r * out_r + val_i * out_i
                into_ref[k, imag_rows, :] += val_r * out_i - val_i * out_r

    each_piece(table_ref, 3, pieces, both // lanes, lanes, blocks, visit)


def write_pieces(table_ref, work, back_ref, series_ref, skip_ref, out_ref):
    blocks, rows, block, lanes = series_ref.shape
    for piece in range(work.shape[0]):
        result = dot32(back_ref[...], work[piece].astype(BF16))
        for row in range(rows):
            at, inside = piece_mask(table_ref, row, piece, block, lanes)
            direct = skip_ref[...].astype(F32).reshape(1, -1) * series_ref[at, row].astype(F32)
            value = result[:, row * lanes : (row + 1) * lanes] + direct
            kept = out_ref[at, row, :block].astype(F32)
            out_ref[at, row, :block] = jnp.where(inside, value, kept).astype(BF16)


def long_forward_kernel(
    table_ref, series_ref, taps_ref, skip_ref, ahead_ref, back_ref, out_ref, spec, work
):
    piece_spectra(table_ref, series_ref, ahead_ref, spec)
    couple(table_ref, -1, taps_ref, spec, work)
    write_pieces(table_ref, work, back_ref, series_ref, skip_ref, out_ref)


def long_forward(table, series, taps_spec, skip, tables):
    blocks, rows, block, lanes = series.shape
    pieces = table.shape[2]
    vmem = pl.BlockSpec(memory_space=pltpu.VMEM)
    return pl.pallas_call(
        long_forward_kernel,
        in_specs=[smem()] + [vmem] * 5,
        out_specs=vmem,
        out_shape=jax.ShapeDtypeStruct(series.shape, BF16),
        scratch_shapes=[pltpu.VMEM((pieces, 2 * block, rows * lanes), F32)] * 2,
        compiler_params=pltpu.CompilerParams(vmem_limit_bytes=VMEM_MIB * 2**20),
        cost_estimate=MUCH,
        name="long_forward",
    )(table, series, taps_spec, skip, tables[0], tables[2])


def long_backward_kernel(
    table_ref, grad_ref, series_ref, taps_ref, skip_ref, ahead_ref, back_ref, *others
):
    out_ref, taps_out_ref, skip_out_ref, token_out, spec, grad_spec, work, cross = others[-8:]
    token_out[0] = 0
    blocks, rows, block, lanes = series_ref.shape
    piece_spectra(table_ref, grad_ref, ahead_ref, grad_spec)
    couple(table_ref, 1, taps_ref, grad_spec, work)
    write_pieces(table_ref, work, back_ref, grad_ref, skip_ref, out_ref)
    for at in range(blocks):
        for row in range(rows):
            if at + 1 < blocks:
                out_ref[at, row, block:] = out_ref[at + 1, row, : out_ref.shape[2] - block]
            else:
                out_ref[at, row, block:] = jnp.zeros_like(out_ref[at, row, block:])
    piece_spectra(table_ref, series_ref, ahead_ref, spec)
    correlate(table_ref, spec, grad_spec, cross)
    sign = alternating(block, lanes)
    for k in range(blocks):
        if k + 1 < blocks:
            cross[k, :block] = cross[k, :block] + sign * cross[k + 1, block:]
            cross[k, block:] = cross[k, block:] - sign * cross[k + 1, :block]
        taps_out_ref[k] = dot32(back_ref[...], cross[k].astype(BF16))
    total = jnp.zeros((8, lanes), F32)
    for at in range(blocks):
        for row in range(rows):
            both = grad_ref[at, row].astype(F32) * series_ref[at, row].astype(F32)
            total = total + jnp.sum(both.reshape(block // 8, 8, lanes), axis=0)
    skip_out_ref[...] = jnp.sum(total, axis=0, keepdims=True)


def long_backward(table, grad, series, taps_spec, skip, tables, ready):
    blocks, rows, block, lanes = series.shape
    pieces = table.shape[2]
    vmem = pl.BlockSpec(memory_space=pltpu.VMEM)
    return pl.pallas_call(
        long_backward_kernel,
        in_specs=[smem()] + [vmem] * 6 + [pl.BlockSpec(memory_space=pl.ANY)] * len(ready),
        out_specs=[vmem] * 3 + [smem()],
        out_shape=[
            jax.ShapeDtypeStruct((blocks, rows, block + HALO, lanes), BF16),
            jax.ShapeDtypeStruct((blocks, block, lanes), F32),
            jax.ShapeDtypeStruct((1, lanes), F32),
            jax.ShapeDtypeStruct((1,), jnp.int32),
        ],
        scratch_shapes=[pltpu.VMEM((pieces, 2 * block, rows * lanes), F32)] * 3
        + [pltpu.VMEM((blocks, 2 * block, lanes), F32)],
        compiler_params=pltpu.CompilerParams(vmem_limit_bytes=VMEM_MIB * 2**20),
        cost_estimate=MUCH,
        name="long_backward",
    )(table, grad, series, taps_spec, skip, tables[0], tables[2], *ready)


def document_masks(bounds, positions, length):
    lower = jnp.concatenate([jnp.zeros_like(bounds[:, :1]), bounds], axis=1)
    upper = jnp.concatenate([bounds, jnp.full_like(bounds[:, :1], length)], axis=1)
    inside = (positions[None, None, :] >= lower[:, :, None]) & (
        positions[None, None, :] < upper[:, :, None]
    )
    return inside.astype(F32)


def cos_sin(count_a, count_b, modulus):
    table = (
        jnp.arange(count_a, dtype=jnp.int32)[:, None]
        * jnp.arange(count_b, dtype=jnp.int32)[None, :]
        % modulus
    )
    angles = table.astype(F32) * (2.0 * math.pi / modulus)
    return (jnp.cos(angles), jnp.sin(angles))


def make_plan(blocks, block_len):
    outer = 2 * blocks
    cos_outer, sin_outer = cos_sin(outer, outer, outer)
    cos_twist, sin_twist = cos_sin(outer, block_len, outer * block_len)
    cos_inner, sin_inner = cos_sin(block_len, block_len, block_len)
    return (blocks, block_len, cos_outer, sin_outer, cos_twist, sin_twist, cos_inner, sin_inner)


def right_mul(left, table):
    return jnp.einsum("...km,mj->...kj", left, table, precision=HIGH)


def spectrum(series, plan):
    blocks, block_len, cos_outer, sin_outer, cos_twist, sin_twist, cos_inner, sin_inner = plan
    folded = series.reshape(series.shape[:-1] + (blocks, block_len))
    real_a = jnp.einsum("kn,...nm->...km", cos_outer[:, :blocks], folded, precision=HIGH)
    imag_a = -jnp.einsum("kn,...nm->...km", sin_outer[:, :blocks], folded, precision=HIGH)
    real_t = real_a * cos_twist + imag_a * sin_twist
    imag_t = imag_a * cos_twist - real_a * sin_twist
    real_x = right_mul(real_t, cos_inner) + right_mul(imag_t, sin_inner)
    imag_x = right_mul(imag_t, cos_inner) - right_mul(real_t, sin_inner)
    return (real_x, imag_x)


def inverse(real_x, imag_x, plan):
    blocks, block_len, cos_outer, sin_outer, cos_twist, sin_twist, cos_inner, sin_inner = plan
    real_b = right_mul(real_x, cos_inner) - right_mul(imag_x, sin_inner)
    imag_b = right_mul(imag_x, cos_inner) + right_mul(real_x, sin_inner)
    real_u = real_b * cos_twist - imag_b * sin_twist
    imag_u = imag_b * cos_twist + real_b * sin_twist
    folded = jnp.einsum("nk,...km->...nm", cos_outer[:blocks], real_u, precision=HIGH) - jnp.einsum(
        "nk,...km->...nm", sin_outer[:blocks], imag_u, precision=HIGH
    )
    folded = folded * (1.0 / (2 * blocks * block_len))
    return folded.reshape(folded.shape[:-2] + (blocks * block_len,))


def by_channel(blocked):
    blocks, rows, block, lanes = blocked.shape
    return blocked.astype(F32).transpose(1, 3, 0, 2).reshape(rows, lanes, blocks * block)


def by_block(series, blocks):
    rows, lanes, length = series.shape
    return series.reshape(rows, lanes, blocks, length // blocks).transpose(2, 0, 3, 1).astype(BF16)


class WholeSpectra:
    def __init__(self, bounds, taps, skip):
        blocks, block, lanes = taps.shape
        self.blocks, self.plan = blocks, make_plan(blocks, block)
        length = blocks * block
        everywhere = jnp.arange(length, dtype=jnp.int32)
        self.masks = document_masks(bounds, everywhere, length)[:, :, None, :]
        self.skip = skip[0][None, :, None]
        self.taps_real, self.taps_imag = spectrum(taps.reshape(length, lanes).T, self.plan)

    def forward(self, series):
        carried = by_channel(series)
        self.carried = carried
        real, imag = spectrum(self.masks * carried[:, None], self.plan)
        self.spec = real, imag
        docs = inverse(
            real * self.taps_real - imag * self.taps_imag,
            real * self.taps_imag + imag * self.taps_real,
            self.plan,
        )
        conv = jnp.sum(self.masks * docs, axis=1) + self.skip * carried
        return by_block(conv, self.blocks)

    def backward(self, grad):
        g_long = by_channel(grad)
        spec_real, spec_imag = self.spec
        g_skip = jnp.sum(g_long * self.carried, axis=(0, 2))
        real, imag = spectrum(self.masks * g_long[:, None], self.plan)
        docs = inverse(
            self.taps_real * real + self.taps_imag * imag,
            self.taps_real * imag - self.taps_imag * real,
            self.plan,
        )
        g_carried = jnp.sum(self.masks * docs, axis=1) + self.skip * g_long
        cross_real = jnp.sum(real * spec_real + imag * spec_imag, axis=(0, 1))
        cross_imag = jnp.sum(imag * spec_real - real * spec_imag, axis=(0, 1))
        g_taps = inverse(cross_real, cross_imag, self.plan)
        return by_block(g_carried, self.blocks), g_taps.T, g_skip[None, :]


def device_index():
    return lax.axis_index("rows") * lax.axis_size("seq") + lax.axis_index("seq")


def device_bits():
    return int(math.log2(lax.axis_size("rows") * lax.axis_size("seq")))


def swapped(value, mask_of):
    count = lax.axis_size("rows") * lax.axis_size("seq")
    return lax.ppermute(value, BOTH, [(one, one ^ mask_of(one)) for one in range(count)])


def pick(array, index, axis):
    return lax.dynamic_index_in_dim(array, index, axis=axis, keepdims=False)


def added(kept, arrived, kind):
    return (kept.astype(F32) + arrived.astype(F32)).astype(kind)


def halved(pieces, bit, axis, kind):
    mine = (device_index() >> bit) & 1
    arrived = swapped(pick(pieces, 1 - mine, axis), lambda one: 1 << bit)
    return added(pick(pieces, mine, axis), arrived, kind)


def quartered(pieces, axis, kind):
    index = device_index()
    core, low, high = index & 1, (index >> 1) & 1, (index >> 2) & 1

    def two(low_bit, high_bit):
        return jnp.stack(
            [
                pick(pieces, jnp.where(core == 0, 2 * j + low_bit, 2 * high_bit + j), axis)
                for j in range(2)
            ],
            axis=axis,
        )

    arrived = swapped(two(1 - low, 1 - high), lambda one: 4 if one & 1 else 2)
    pieces = added(two(low, high), arrived, kind)
    mine = jnp.where(core == 0, high, low)
    arrived = swapped(pick(pieces, 1 - mine, axis), lambda one: 2 if one & 1 else 4)
    return added(pick(pieces, mine, axis), arrived, kind)


def scattered(pieces, kind):
    rest = pieces.shape[1:]
    bits = device_bits()
    pieces = quartered(pieces.reshape((-1, 4) + rest), 1, kind)
    for bit in range(3, bits):
        last = bit == bits - 1
        pieces = halved(pieces.reshape((-1, 2) + rest), bit, 1, F32 if last else kind)
    return pieces.reshape(rest)


def weight_gradient(first, second):
    tokens, width = first.shape
    shares = 1 << device_bits()
    share = width // shares
    core = device_index() & 1
    halves = first.reshape(tokens, shares // 2, 2, share).transpose(2, 0, 1, 3)
    halves = halves.reshape(2, tokens, width // 2)

    def product(which):
        return jnp.einsum(
            "ti,tj->ij", pick(halves, which, 0), second, preferred_element_type=F32
        )

    arrived = swapped(product(1 - core).astype(BF16), lambda one: 1)
    kept = added(product(core), arrived, BF16)
    return scattered(kept.reshape(shares // 2, share, second.shape[1]), BF16)


def small_scattered(vectors):
    pieces = halved(vectors.reshape(-1, 2, vectors.shape[1]), 0, 1, F32)
    return scattered(pieces, F32)


def summed(value, bits):
    for bit in bits:
        value = value + swapped(value, lambda one, bit=bit: 1 << bit)
    return value


def back_product(grad_low, weight):
    return jnp.einsum("tj,ij->ti", grad_low, weight, preferred_element_type=F32)


def plain_device(
    tokens,
    cotangent,
    bounds,
    ln1_gain,
    ln1_bias,
    in_weight,
    in_bias,
    short_weight,
    short_bias,
    f1_weight,
    f1_bias,
    f2_weight,
    f2_bias,
    f3_weight,
    filter_skip,
    out_weight,
    out_bias,
    ln2_gain,
    ln2_bias,
    up_weight,
    up_bias,
    down_weight,
    down_bias,
):
    seq_count = lax.axis_size("seq")
    row_count, tok_count, width = tokens.shape
    flat_count = row_count * tok_count
    length = tok_count * seq_count
    lanes = f3_weight.shape[1]
    first_channel = lax.axis_index("seq") * lanes
    x_in = tokens.astype(F32).reshape(flat_count, width)
    n1, ln1_pull = jax.vjp(layer_norm, x_in, ln1_gain.astype(F32), ln1_bias.astype(F32))
    n1_low = n1.astype(BF16)
    proj = jnp.dot(n1_low, in_weight, preferred_element_type=F32) + in_bias.astype(F32)
    proj_low = proj.astype(BF16).reshape(row_count, tok_count, 3 * width)
    here = lax.axis_index("seq") * tok_count + jnp.arange(tok_count, dtype=jnp.int32)
    starts = jnp.max(
        jnp.where(bounds[:, :, None] <= here[None, None, :], bounds[:, :, None], 0), axis=1
    )
    keep_one = (here[None, :] - 1 >= starts).astype(F32)[:, :, None]
    keep_two = (here[None, :] - 2 >= starts).astype(F32)[:, :, None]
    rim = passed_along(proj_low[:, tok_count - 2 :, :], "seq", 1)
    extended = jnp.concatenate([rim, proj_low], axis=1).astype(F32)
    current = extended[:, 2:, :]
    before_one = extended[:, 1:-1, :]
    before_two = extended[:, :-2, :]
    taps_short = short_weight.astype(F32)
    shorted = (
        taps_short[0] * current
        + keep_one * taps_short[1] * before_one
        + keep_two * taps_short[2] * before_two
        + short_bias.astype(F32)
    )
    gate_out = shorted[:, :, :width]
    gate_in = shorted[:, :, width : 2 * width]
    values = shorted[:, :, 2 * width :]
    carried_low = (gate_in * values).astype(BF16)

    def to_channels(array):
        array = array.reshape(row_count, tok_count, seq_count, lanes).transpose(2, 0, 1, 3)
        return lax.all_to_all(array, "seq", split_axis=0, concat_axis=0, tiled=True)

    def to_positions(array):
        array = lax.all_to_all(array, "seq", split_axis=0, concat_axis=0, tiled=True)
        return array.transpose(1, 2, 0, 3).reshape(row_count, tok_count, width)

    carried = to_channels(carried_low)

    def make_taps(w_one, b_one, w_two, b_two, w_three):
        return filter_taps(w_one, b_one, w_two, b_two, w_three, first_channel, length)

    taps, filter_pull = jax.vjp(
        make_taps,
        f1_weight.astype(F32),
        f1_bias.astype(F32),
        f2_weight.astype(F32),
        f2_bias.astype(F32),
        f3_weight.astype(F32),
    )
    long_filter = WholeSpectra(
        bounds, taps.reshape(seq_count, tok_count, lanes), filter_skip.astype(F32)[None, :]
    )
    long_low = long_filter.forward(carried)
    long_seq = to_positions(long_low).astype(F32)
    mixed_low = (gate_out * long_seq).astype(BF16).reshape(flat_count, width)
    branch = jnp.dot(mixed_low, out_weight, preferred_element_type=F32) + out_bias.astype(F32)
    resid = x_in + branch
    n2, ln2_pull = jax.vjp(layer_norm, resid, ln2_gain.astype(F32), ln2_bias.astype(F32))
    n2_low = n2.astype(BF16)
    pre = jnp.dot(n2_low, up_weight, preferred_element_type=F32) + up_bias.astype(F32)
    act, gelu_pull = jax.vjp(gelu_tanh, pre)
    act_low = act.astype(BF16)
    result = (
        resid
        + jnp.dot(act_low, down_weight, preferred_element_type=F32)
        + down_bias.astype(F32)
    )
    output = result.astype(BF16).reshape(row_count, tok_count, width)
    grad_low = cotangent.reshape(flat_count, width)
    grad_float = grad_low.astype(F32)
    g_down_w = weight_gradient(act_low, grad_low)
    g_down_b = jnp.sum(grad_float, axis=0)
    g_act = back_product(grad_low, down_weight)
    (g_pre,) = gelu_pull(g_act)
    g_pre_low = g_pre.astype(BF16)
    g_up_w = weight_gradient(n2_low, g_pre_low)
    g_up_b = jnp.sum(g_pre_low.astype(F32), axis=0)
    g_n2 = back_product(g_pre_low, up_weight)
    g_resid_part, g_ln2_gain, g_ln2_bias = ln2_pull(g_n2)
    g_resid = grad_float + g_resid_part
    g_branch_low = g_resid.astype(BF16)
    g_out_w = weight_gradient(mixed_low, g_branch_low)
    g_out_b = jnp.sum(g_branch_low.astype(F32), axis=0)
    g_mixed = back_product(g_branch_low, out_weight).reshape(row_count, tok_count, width)
    g_gate_out = g_mixed * long_seq
    g_long_low = (g_mixed * gate_out).astype(BF16)
    g_carried_low, g_taps, g_skip = long_filter.backward(to_channels(g_long_low))
    g_f1_w, g_f1_b, g_f2_w, g_f2_b, g_f3_w = filter_pull(g_taps)
    g_carried_seq = to_positions(g_carried_low).astype(F32)
    g_shorted = jnp.concatenate(
        [g_gate_out, g_carried_seq * values, g_carried_seq * gate_in], axis=-1
    )
    lead_one = keep_one * g_shorted
    lead_two = keep_two * g_shorted
    ahead = passed_along(
        jnp.concatenate([lead_one[:, :2], lead_two[:, :2]], axis=1).astype(BF16), "seq", -1
    ).astype(F32)
    after_one = jnp.concatenate([lead_one[:, 1:], ahead[:, :1]], axis=1)
    after_two = jnp.concatenate([lead_two[:, 2:], ahead[:, 2:4]], axis=1)
    g_proj = taps_short[0] * g_shorted + taps_short[1] * after_one + taps_short[2] * after_two
    g_short_w = jnp.stack(
        [
            jnp.sum(g_shorted * current, axis=(0, 1)),
            jnp.sum(lead_one * before_one, axis=(0, 1)),
            jnp.sum(lead_two * before_two, axis=(0, 1)),
        ],
        axis=0,
    )
    g_short_b = jnp.sum(g_shorted, axis=(0, 1))
    g_proj_low = g_proj.astype(BF16).reshape(flat_count, 3 * width)
    g_in_w = weight_gradient(n1_low, g_proj_low)
    g_in_b = jnp.sum(g_proj_low.astype(F32), axis=0)
    g_n1 = back_product(g_proj_low, in_weight)
    g_x_part, g_ln1_gain, g_ln1_bias = ln1_pull(g_n1)
    grad_tokens = (g_resid + g_x_part).reshape(row_count, tok_count, width)

    def lined(parts):
        flat = jnp.concatenate([part.reshape(-1) for part in parts])
        return jnp.pad(flat, (0, -flat.shape[0] % 128)).reshape(-1, 128)

    net = lined((g_f1_w, g_f1_b, g_f2_w, g_f2_b))
    net_rows = net.shape[0]
    own = lined((g_f3_w, g_skip))
    bits = device_bits()
    seq_bits = int(math.log2(seq_count))
    joint = summed(jnp.concatenate([net, own]), range(seq_bits, bits))
    net = summed(joint[:net_rows], range(seq_bits)).reshape(-1)
    own = joint[net_rows:].reshape(-1)
    g_f1_w, g_f1_b, g_f2_w, g_f2_b = (
        part.reshape(like.shape)
        for part, like in zip(
            jnp.split(net, np.cumsum([f1_weight.size, f1_bias.size, f2_weight.size, f2_bias.size])),
            (f1_weight, f1_bias, f2_weight, f2_bias),
        )
    )
    g_f3_w = own[: f3_weight.size].reshape(f3_weight.shape)
    g_skip = own[f3_weight.size : f3_weight.size + lanes]

    shares = 1 << bits
    vectors = (g_ln2_gain, g_ln2_bias, g_up_b, g_down_b, g_out_b)
    vectors += (g_ln1_gain, g_ln1_bias, g_in_b, g_short_b) + tuple(g_short_w)
    rows = jnp.concatenate([v.reshape(shares, -1) for v in vectors], axis=1)
    sums = small_scattered(rows)
    cuts = np.cumsum([v.shape[0] // shares for v in vectors])[:-1]
    (
        g_ln2_gain,
        g_ln2_bias,
        g_up_b,
        g_down_b,
        g_out_b,
        g_ln1_gain,
        g_ln1_bias,
        g_in_b,
        g_short_b,
        *g_short_w,
    ) = jnp.split(sums, cuts)
    return (
        output,
        grad_tokens,
        g_ln1_gain,
        g_ln1_bias,
        g_in_w,
        g_in_b,
        jnp.stack(g_short_w),
        g_short_b,
        g_f1_w,
        g_f1_b,
        g_f2_w,
        g_f2_b,
        g_f3_w,
        g_skip,
        g_out_w,
        g_out_b,
        g_ln2_gain,
        g_ln2_bias,
        g_up_w,
        g_up_b,
        g_down_w,
        g_down_b,
    )


HALO = 16


def turned_halves(values, share, out_ref, at):
    turned = values.T.astype(BF16)
    for run in range(turned.shape[0] // share):
        into = pl.ds(run // 2 * share, share)
        out_ref[run % 2, into, at] = turned[run * share : (run + 1) * share]


def row_of(ref):
    return ref[...].astype(F32).reshape(1, -1)


def keeps(cuts_ref, first_ref, row, count, lanes):
    spot = lax.broadcasted_iota(jnp.int32, (count, lanes), 0) + first_ref[0]

    def begins(at):
        found = at == 0
        for cut in range(cuts_ref.shape[1]):
            found = found | (at == cuts_ref[row, cut])
        return found

    here, before = begins(spot), begins(spot - 1)
    return jnp.where(here, 0.0, 1.0), jnp.where(here | before, 0.0, 1.0)


def short_filter(values, weight, shift, keep_one, keep_two, begin, count):
    one = pltpu.roll(values, 1, 0)[begin : begin + count]
    two = pltpu.roll(values, 2, 0)[begin : begin + count]
    here = values[begin : begin + count]
    return weight[0:1] * here + keep_one * (weight[1:2] * one) + keep_two * (weight[2:3] * two) + shift


def normed(values):
    center = values - jnp.mean(values, axis=-1, keepdims=True)
    spread = jnp.mean(center * center, axis=-1, keepdims=True)
    scale = lax.rsqrt(spread + eps)
    return center * scale, scale


def in_forward_kernel(
    cuts_ref,
    first_ref,
    before_ref,
    x_ref,
    beyond_ref,
    gain_ref,
    bias_ref,
    w0,
    w1,
    w2,
    b0,
    b1,
    b2,
    s1,
    s2,
    c1,
    c2,
    norm_out,
    proj_out,
    carried_out,
    norm,
):
    rows, count, width = x_ref.shape
    extent = count + 2 * HALO
    group = carried_out.shape[3]

    @pl.when(pl.program_id(0) == 0)
    def _():
        for row in range(rows):
            around = [ref[row].astype(F32) for ref in (before_ref, x_ref, beyond_ref)]
            hat, _ = normed(jnp.concatenate(around, axis=0))
            value = hat * row_of(gain_ref) + row_of(bias_ref)
            norm[row * extent : (row + 1) * extent] = value.astype(BF16)
            turned_halves(
                value[HALO : HALO + count], 32, norm_out, pl.ds(row * count, count)
            )

    parts = []
    for third, (w, b) in enumerate(((w0, b0), (w1, b1), (w2, b2))):
        part = dot32(norm[...], w[...]) + row_of(b)
        low = part.astype(BF16)
        for row in range(rows):
            proj_out[third, row] = low[row * extent : (row + 1) * extent]
        parts.append(low.astype(F32))
    lanes = parts[0].shape[1]
    for row in range(rows):
        keep_one, keep_two = keeps(cuts_ref, first_ref, row, count, lanes)
        sides = [
            short_filter(
                parts[third][row * extent : (row + 1) * extent],
                s[...].astype(F32),
                row_of(c),
                keep_one,
                keep_two,
                HALO,
                count,
            )
            for third, s, c in ((1, s1, c1), (2, s2, c2))
        ]
        carried = (sides[0] * sides[1]).astype(BF16)
        for index in range(lanes // group):
            carried_out[index, row] = carried[:, index * group : (index + 1) * group]


def smem():
    return pl.BlockSpec(memory_space=pltpu.SMEM)


def whole(shape):
    return pl.BlockSpec(shape, lambda i: (0,) * len(shape), pipeline_mode=pl.Buffered(1))


def params():
    return pltpu.CompilerParams(
        vmem_limit_bytes=VMEM_MIB * 2**20, dimension_semantics=("arbitrary",)
    )


def third_block(shape, which, steps):
    lead = (0,) * (len(shape) - 1)
    return pl.BlockSpec(shape, lambda i: lead + (which * steps + i,))


def in_forward(
    cuts, first, before, x, beyond, gain, bias, in_weight, in_bias, short_weight, short_bias, group
):
    rows, count, width = x.shape
    extent = count + 2 * HALO
    lanes = 256
    steps = width // lanes
    return pl.pallas_call(
        in_forward_kernel,
        grid=(steps,),
        in_specs=[smem(), smem(), whole(before.shape), whole(x.shape), whole(beyond.shape)]
        + [whole(gain.shape), whole(bias.shape)]
        + [third_block((width, lanes), t, steps) for t in range(3)]
        + [third_block((lanes,), t, steps) for t in range(3)]
        + [third_block((3, lanes), t, steps) for t in (1, 2)]
        + [third_block((lanes,), t, steps) for t in (1, 2)],
        out_specs=[
            whole((2, width // 2, rows * count)),
            pl.BlockSpec((3, rows, extent, lanes), lambda i: (0, 0, 0, i)),
            pl.BlockSpec((lanes // group, rows, count, group), lambda i: (i, 0, 0, 0)),
        ],
        out_shape=[
            jax.ShapeDtypeStruct((2, width // 2, rows * count), BF16),
            jax.ShapeDtypeStruct((3, rows, extent, width), BF16),
            jax.ShapeDtypeStruct((width // group, rows, count, group), BF16),
        ],
        scratch_shapes=[pltpu.VMEM((rows * extent, width), BF16)],
        compiler_params=params(),
        cost_estimate=MUCH,
        name="in_forward",
    )(
        cuts,
        first,
        before,
        x,
        beyond,
        gain,
        bias,
        *[in_weight] * 3,
        *[in_bias] * 3,
        *[short_weight] * 2,
        *[short_bias] * 2,
    )


def gates(cuts_ref, first_ref, proj_ref, weight_ref, shift_ref, row, index, group):
    at = pl.ds(index * group, group)
    extent = proj_ref.shape[2]
    count = extent - 2 * HALO
    keep_one, keep_two = keeps(cuts_ref, first_ref, row, count, group)
    return short_filter(
        proj_ref[0, row, :, at].astype(F32),
        weight_ref[:, at].astype(F32),
        shift_ref[at].astype(F32).reshape(1, -1),
        keep_one,
        keep_two,
        HALO,
        count,
    )


def middle_forward_kernel(
    cuts_ref,
    first_ref,
    long_ref,
    proj_ref,
    weight_ref,
    shift_ref,
    x_ref,
    out_w_ref,
    out_b_ref,
    gain_ref,
    bias_ref,
    up_ref,
    up_b_ref,
    g_act_ref,
    mixed_out,
    resid_out,
    norm_out,
    act_out,
    split_out,
    g_pre_out,
    g_up_b_out,
    mixed,
    norm,
):
    groups, rows, count, group = long_ref.shape

    @pl.when(pl.program_id(0) == 0)
    def _():
        for row in range(rows):
            own = pl.ds(row * count, count)
            for index in range(groups):
                gate = gates(cuts_ref, first_ref, proj_ref, weight_ref, shift_ref, row, index, group)
                value = gate * long_ref[index, row].astype(F32)
                mixed[own, pl.ds(index * group, group)] = value.astype(BF16)
        for row in range(rows):
            own = pl.ds(row * count, count)
            turned_halves(mixed[own, :].astype(F32), 32, mixed_out, own)
            branch = dot32(mixed[own, :], out_w_ref[...]) + row_of(out_b_ref)
            resid = x_ref[own, :].astype(F32) + branch
            resid_out[own, :] = resid
            hat, _ = normed(resid)
            value = hat * row_of(gain_ref) + row_of(bias_ref)
            norm[own, :] = value.astype(BF16)
            turned_halves(value, 32, norm_out, own)

    pre = dot32(norm[...], up_ref[...]) + row_of(up_b_ref)
    scale = math.sqrt(2.0 / math.pi)
    square = pre * pre
    inner = pre * (scale + (scale * 0.044715) * square)
    half = 0.5 + 0.5 * jnp.tanh(inner)
    act = pre * half
    act_out[...] = act.astype(BF16)
    turned_halves(act, 128, split_out, pl.ds(0, act.shape[0]))
    slope = pre * (2.0 * scale + (6.0 * scale * 0.044715) * square)
    slope = half + slope * (half * (1.0 - half))
    g_pre = (g_act_ref[...].astype(F32) * slope).astype(BF16)
    g_pre_out[...] = g_pre
    g_up_b_out[...] = jnp.sum(g_pre.astype(F32), axis=0, keepdims=True)


def middle_forward(
    cuts, first, long, proj, short_weight, short_bias, x, out_w, out_b, gain, bias, up, up_b, g_act
):
    groups, rows, count, group = long.shape
    extent = proj.shape[2]
    tokens, width = x.shape
    hidden = up.shape[1]
    lanes = width
    steps = hidden // lanes

    def part(height):
        return pl.BlockSpec((height, lanes), lambda i: (0, i))

    return pl.pallas_call(
        middle_forward_kernel,
        grid=(steps,),
        in_specs=[
            smem(),
            smem(),
            whole(long.shape),
            whole((1, rows, extent, width)),
            whole((3, width)),
            whole((width,)),
            whole((tokens, width)),
            whole((width, width)),
            whole((width,)),
            whole((width,)),
            whole((width,)),
            part(width),
            pl.BlockSpec((lanes,), lambda i: (i,)),
            part(tokens),
        ],
        out_specs=[
            whole((2, width // 2, tokens)),
            whole((tokens, width)),
            whole((2, width // 2, tokens)),
            part(tokens),
            pl.BlockSpec((2, lanes // 2, tokens), lambda i: (0, i, 0)),
            part(tokens),
            part(1),
        ],
        out_shape=[
            jax.ShapeDtypeStruct((2, width // 2, tokens), BF16),
            jax.ShapeDtypeStruct((tokens, width), F32),
            jax.ShapeDtypeStruct((2, width // 2, tokens), BF16),
            jax.ShapeDtypeStruct((tokens, hidden), BF16),
            jax.ShapeDtypeStruct((2, hidden // 2, tokens), BF16),
            jax.ShapeDtypeStruct((tokens, hidden), BF16),
            jax.ShapeDtypeStruct((1, hidden), F32),
        ],
        scratch_shapes=[pltpu.VMEM((tokens, width), BF16), pltpu.VMEM((tokens, width), BF16)],
        compiler_params=params(),
        cost_estimate=MUCH,
        name="middle_forward",
    )(
        cuts,
        first,
        long,
        proj,
        short_weight,
        short_bias,
        x,
        out_w,
        out_b,
        gain,
        bias,
        up,
        up_b,
        g_act,
    )


def turned_dot(left, right):
    return lax.dot_general(left, right, (((1,), (1,)), ((), ())), preferred_element_type=F32)


def normed_back(values, grad, gain):
    hat, scale = normed(values)
    inward = grad * gain
    mean = jnp.mean(inward, axis=-1, keepdims=True)
    along = jnp.mean(inward * hat, axis=-1, keepdims=True)
    g_gain = jnp.sum(grad * hat, axis=0, keepdims=True)
    return scale * (inward - mean - hat * along), g_gain, jnp.sum(grad, axis=0, keepdims=True)


def fetched(step, last, sources, targets, sems):
    @pl.when(step == 0)
    def _():
        for k, (source, target) in enumerate(zip(sources, targets)):
            pltpu.make_async_copy(source, target, sems.at[k]).start()

    @pl.when(step == last)
    def _():
        for k, (source, target) in enumerate(zip(sources, targets)):
            pltpu.make_async_copy(source, target, sems.at[k]).wait()


def middle_backward_kernel(
    cuts_ref,
    first_ref,
    long_at,
    proj_at,
    weight_ref,
    shift_ref,
    resid_at,
    grad_at,
    gain_ref,
    out_w_at,
    g_pre_ref,
    up_ref,
    _,
    g_long_out,
    g_gate_out,
    g_resid_out,
    g_branch_out,
    sums_out,
    token_out,
    total,
    long_ref,
    proj_ref,
    resid_ref,
    grad_ref,
    out_w_ref,
    sems,
):
    groups, rows, count, group = long_ref.shape
    step = pl.program_id(0)
    token_out[0] = 0
    fetched(
        step,
        pl.num_programs(0) - 1,
        (long_at, proj_at.at[pl.ds(0, 1)], resid_at, grad_at, out_w_at),
        (long_ref, proj_ref, resid_ref, grad_ref, out_w_ref),
        sems,
    )

    @pl.when(step == 0)
    def _():
        total[...] = turned_dot(g_pre_ref[...], up_ref[...])

    @pl.when(step > 0)
    def _():
        total[...] += turned_dot(g_pre_ref[...], up_ref[...])

    @pl.when(step == pl.num_programs(0) - 1)
    def _():
        sums = [0.0] * 4
        for row in range(rows):
            own = pl.ds(row * count, count)
            grad = grad_ref[own, :].astype(F32)
            back, g_gain, g_bias = normed_back(
                resid_ref[own, :], total[own, :], row_of(gain_ref)
            )
            g_resid = grad + back
            g_resid_out[own, :] = g_resid
            low = g_resid.astype(BF16)
            g_branch_out[own, :] = low
            g_out_b = jnp.sum(low.astype(F32), axis=0, keepdims=True)
            g_down_b = jnp.sum(grad, axis=0, keepdims=True)
            sums = [a + b for a, b in zip(sums, (g_gain, g_bias, g_out_b, g_down_b))]
            total[own, :] = turned_dot(low, out_w_ref[...])
        sums_out[...] = jnp.concatenate(sums + [jnp.zeros_like(sums[0])] * 4, axis=0)
        for row in range(rows):
            own = pl.ds(row * count, count)
            for index in range(groups):
                at = pl.ds(index * group, group)
                g_mixed = total[own, at]
                gate = gates(cuts_ref, first_ref, proj_ref, weight_ref, shift_ref, row, index, group)
                g_gate_out[row, :, at] = g_mixed * long_ref[index, row].astype(F32)
                g_long_out[index, row] = (g_mixed * gate).astype(BF16)


def middle_backward(
    cuts, first, long, proj, short_weight, short_bias, resid, grad, gain, out_w, g_pre, up, ready
):
    groups, rows, count, group = long.shape
    extent = proj.shape[2]
    tokens, width = resid.shape
    hidden = up.shape[1]
    lanes = 1024
    steps = hidden // lanes

    def part(height):
        return pl.BlockSpec((height, lanes), lambda i: (0, i))

    anywhere = pl.BlockSpec(memory_space=pl.ANY)
    return pl.pallas_call(
        middle_backward_kernel,
        grid=(steps,),
        in_specs=[
            smem(),
            smem(),
            anywhere,
            anywhere,
            whole((3, width)),
            whole((width,)),
            anywhere,
            anywhere,
            whole((width,)),
            anywhere,
            part(tokens),
            part(width),
            pl.BlockSpec(memory_space=pl.ANY),
        ],
        out_specs=[
            whole(long.shape),
            whole((rows, count, width)),
            whole((tokens, width)),
            whole((tokens, width)),
            whole((8, width)),
            smem(),
        ],
        out_shape=[
            jax.ShapeDtypeStruct(long.shape, BF16),
            jax.ShapeDtypeStruct((rows, count, width), F32),
            jax.ShapeDtypeStruct((tokens, width), F32),
            jax.ShapeDtypeStruct((tokens, width), BF16),
            jax.ShapeDtypeStruct((8, width), F32),
            jax.ShapeDtypeStruct((1,), jnp.int32),
        ],
        scratch_shapes=[
            pltpu.VMEM((tokens, width), F32),
            pltpu.VMEM(long.shape, BF16),
            pltpu.VMEM((1, rows, extent, width), BF16),
            pltpu.VMEM((tokens, width), F32),
            pltpu.VMEM((tokens, width), BF16),
            pltpu.VMEM((width, width), BF16),
            pltpu.SemaphoreType.DMA((5,)),
        ],
        compiler_params=params(),
        cost_estimate=MUCH,
        name="middle_backward",
    )(
        cuts,
        first,
        long,
        proj,
        short_weight,
        short_bias,
        resid,
        grad,
        gain,
        out_w,
        g_pre,
        up,
        ready,
    )


def in_backward_kernel(
    cuts_ref,
    first_ref,
    g_carried_ref,
    g_gate_ref,
    g_next_ref,
    proj_ref,
    s0,
    s1,
    s2,
    c1,
    c2,
    w0,
    w1,
    w2,
    x_at,
    gain_ref,
    g_resid_at,
    *others,
):
    g_proj_out, sums_out, g_tokens_out, norm_sums_out, token_out = others[-9:-4]
    total, x_ref, g_resid_ref, sems = others[-4:]
    token_out[0] = 0
    fetched(
        pl.program_id(0),
        pl.num_programs(0) - 1,
        (x_at, g_resid_at),
        (x_ref, g_resid_ref),
        sems,
    )
    weights = [s[...].astype(F32) for s in (s0, s1, s2)]
    shifts = [None, row_of(c1), row_of(c2)]
    _, rows, extent, lanes = proj_ref.shape
    count = extent - 2 * HALO
    reach = count + HALO
    group = g_carried_ref.shape[3]
    step = pl.program_id(0)
    sums = [[0.0] * 5 for _ in range(3)]
    for row in range(rows):
        keep_one, keep_two = keeps(cuts_ref, first_ref, row, reach, lanes)
        values = [proj_ref[third, row].astype(F32) for third in range(3)]
        sides = [
            short_filter(
                values[t], weights[t], shifts[t], keep_one, keep_two, HALO, reach
            )
            for t in (1, 2)
        ]
        g_carried = jnp.concatenate(
            [g_carried_ref[index, row] for index in range(lanes // group)], axis=1
        ).astype(F32)
        g_gate = jnp.concatenate([g_gate_ref[row], g_next_ref[row].astype(F32)], axis=0)
        grads = (g_gate, g_carried * sides[1], g_carried * sides[0])
        for third, grad in enumerate(grads):
            weight = weights[third]
            lead_one, lead_two = keep_one * grad, keep_two * grad
            g_proj = (
                weight[0:1] * grad
                + weight[1:2] * pltpu.roll(lead_one, reach - 1, 0)
                + weight[2:3] * pltpu.roll(lead_two, reach - 2, 0)
            )[:count]
            low = g_proj.astype(BF16)
            g_proj_out[third, row * count : (row + 1) * count] = low
            before_one = pltpu.roll(values[third], 1, 0)[HALO : HALO + count]
            before_two = pltpu.roll(values[third], 2, 0)[HALO : HALO + count]
            here = values[third][HALO : HALO + count]
            parts = (
                grad[:count] * here,
                lead_one[:count] * before_one,
                lead_two[:count] * before_two,
                grad[:count],
                low.astype(F32),
            )
            sums[third] = [
                a + jnp.sum(b, axis=0, keepdims=True) for a, b in zip(sums[third], parts)
            ]
    for third in range(3):
        sums_out[third] = jnp.concatenate(
            sums[third] + [jnp.zeros((3, lanes), F32)], axis=0
        )
    product = sum(
        turned_dot(g_proj_out[third], w[...]) for third, w in enumerate((w0, w1, w2))
    )

    @pl.when(step == 0)
    def _():
        total[...] = product

    @pl.when(step > 0)
    def _():
        total[...] += product

    @pl.when(step == pl.num_programs(0) - 1)
    def _():
        norm_sums = [0.0, 0.0]
        for row in range(rows):
            own = pl.ds(row * count, count)
            back, g_gain, g_shift = normed_back(
                x_ref[own, :].astype(F32), total[own, :], row_of(gain_ref)
            )
            g_tokens_out[own, :] = g_resid_ref[own, :] + back
            norm_sums = [norm_sums[0] + g_gain, norm_sums[1] + g_shift]
        norm_sums_out[...] = jnp.concatenate(
            norm_sums + [jnp.zeros((6, x_ref.shape[1]), F32)], axis=0
        )


def in_backward(
    cuts,
    first,
    g_carried,
    g_gate,
    g_next,
    proj,
    short_weight,
    short_bias,
    in_w,
    x,
    gain,
    g_resid,
    ready,
):
    _, rows, extent, width = proj.shape
    count = extent - 2 * HALO
    tokens = rows * count
    group = g_carried.shape[3]
    lanes = 256
    steps = width // lanes

    anywhere = pl.BlockSpec(memory_space=pl.ANY)
    return pl.pallas_call(
        in_backward_kernel,
        grid=(steps,),
        in_specs=[
            smem(),
            smem(),
            pl.BlockSpec((lanes // group, rows, count + HALO, group), lambda i: (i, 0, 0, 0)),
            pl.BlockSpec((rows, count, lanes), lambda i: (0, 0, i)),
            pl.BlockSpec((rows, HALO, lanes), lambda i: (0, 0, i)),
            pl.BlockSpec((3, rows, extent, lanes), lambda i: (0, 0, 0, i)),
        ]
        + [third_block((3, lanes), t, steps) for t in range(3)]
        + [third_block((lanes,), t, steps) for t in (1, 2)]
        + [third_block((width, lanes), t, steps) for t in range(3)]
        + [anywhere, whole((width,)), anywhere]
        + [pl.BlockSpec(memory_space=pl.ANY)] * len(ready),
        out_specs=[
            pl.BlockSpec((3, tokens, lanes), lambda i: (0, 0, i)),
            pl.BlockSpec((3, 8, lanes), lambda i: (0, 0, i)),
            whole((tokens, width)),
            whole((8, width)),
            smem(),
        ],
        out_shape=[
            jax.ShapeDtypeStruct((3, tokens, width), BF16),
            jax.ShapeDtypeStruct((3, 8, width), F32),
            jax.ShapeDtypeStruct((tokens, width), F32),
            jax.ShapeDtypeStruct((8, width), F32),
            jax.ShapeDtypeStruct((1,), jnp.int32),
        ],
        scratch_shapes=[
            pltpu.VMEM((tokens, width), F32),
            pltpu.VMEM((tokens, width), BF16),
            pltpu.VMEM((tokens, width), F32),
            pltpu.SemaphoreType.DMA((2,)),
        ],
        compiler_params=params(),
        cost_estimate=MUCH,
        name="in_backward",
    )(
        cuts,
        first,
        g_carried,
        g_gate,
        g_next,
        proj,
        *[short_weight] * 3,
        *[short_bias] * 2,
        *[in_w] * 3,
        x,
        gain,
        g_resid,
        *ready,
    )


def mark(*others):
    def kernel(*refs):
        refs[-1][0] = 0

    return pl.pallas_call(
        kernel,
        in_specs=[pl.BlockSpec(memory_space=pl.ANY)] * len(others),
        out_specs=smem(),
        out_shape=jax.ShapeDtypeStruct((1,), jnp.int32),
        cost_estimate=LITTLE,
        name="mark",
    )(*others)


def matmul_turned(left, right, columns, ready):
    def kernel(left_ref, right_ref, _, out_ref):
        out_ref[...] = turned_dot(left_ref[...], right_ref[...]).astype(BF16)

    height, depth = left.shape
    width = right.shape[0]
    return pl.pallas_call(
        kernel,
        grid=(width // columns,),
        in_specs=[
            whole((height, depth)),
            pl.BlockSpec((columns, depth), lambda i: (i, 0)),
            pl.BlockSpec(memory_space=pl.ANY),
        ],
        out_specs=pl.BlockSpec((height, columns), lambda i: (0, i)),
        out_shape=jax.ShapeDtypeStruct((height, width), BF16),
        compiler_params=params(),
        cost_estimate=LITTLE,
        name="matmul_turned",
    )(left, right, ready)


def down_forward(resid, act, down, bias, ready):
    tokens, width = resid.shape
    depth = 1024
    steps = act.shape[1] // depth

    def kernel(resid_ref, act_ref, down_ref, bias_ref, *refs):
        out_ref, token_out, total = refs[-3:]
        step = pl.program_id(0)
        token_out[0] = 0
        product = dot32(act_ref[...], down_ref[...])

        @pl.when(step == 0)
        def _():
            total[...] = resid_ref[...] + row_of(bias_ref) + product

        @pl.when(step > 0)
        def _():
            total[...] += product

        @pl.when(step == steps - 1)
        def _():
            out_ref[...] = total[...].astype(BF16)

    return pl.pallas_call(
        kernel,
        grid=(steps,),
        in_specs=[
            whole((tokens, width)),
            pl.BlockSpec((tokens, depth), lambda i: (0, i)),
            pl.BlockSpec((depth, width), lambda i: (i, 0)),
            whole((width,)),
        ]
        + [pl.BlockSpec(memory_space=pl.ANY)] * len(ready),
        out_specs=[whole((tokens, width)), smem()],
        out_shape=[
            jax.ShapeDtypeStruct((tokens, width), BF16),
            jax.ShapeDtypeStruct((1,), jnp.int32),
        ],
        scratch_shapes=[pltpu.VMEM((tokens, width), F32)],
        compiler_params=params(),
        cost_estimate=LITTLE,
        name="down_forward",
    )(resid, act, down, bias, *ready)


def after(value, *others):
    return lax.optimization_barrier((value, others))[0]


def gradient_kernel(counts, order_ref, firsts, seconds, arrived, sent, kept, token, total):
    step = pl.program_id(0)
    token[0] = 0

    def write(values, which):
        if not kept:
            sent[0][...] = values.astype(BF16)
            return
        (send,), (keep,), (total_ref,) = sent, kept, total
        total_ref[...] = values
        share = total_ref.shape[0] // 16
        for spot in range(16):
            piece = pl.ds(pl.multiple_of(order_ref[1 + spot] * share, share), share)
            into = (send, keep)[spot // 8]
            into[pl.ds(spot % 8 * share, share)] = (
                total_ref[piece] + arrived[which][piece].astype(F32)
            ).astype(BF16)

    begin = 0
    for which, (steps, first, second) in enumerate(zip(counts, firsts, seconds)):

        @pl.when((step >= begin) & (step < begin + steps))
        def _(first=first, second=second, which=which):
            write(dot32(first[0], second[...]), which)

        begin += steps


def gradient(order, pairs, arrived, ready, columns, cost=LITTLE):
    height, tokens = pairs[0][0].shape[1:]
    counts, first_specs, second_specs, arrived_specs, begin = [], [], [], [], 0
    for first, second in pairs:
        parts = second.shape[-1] // columns
        steps = parts * (second.shape[0] if second.ndim == 3 else 1)
        first_specs.append(pl.BlockSpec((1, height, tokens), lambda i, o: (o[0], 0, 0)))

        def place(i, o, begin=begin, steps=steps, parts=parts, deep=second.ndim == 3):
            at = jnp.clip(i - begin, 0, steps - 1)
            return (at // parts, 0, at % parts) if deep else (0, at)

        def flat(i, o, begin=begin, steps=steps):
            return 0, jnp.clip(i - begin, 0, steps - 1)

        shape = (None, tokens, columns) if second.ndim == 3 else (tokens, columns)
        second_specs.append(pl.BlockSpec(shape, place))
        arrived_specs.append(pl.BlockSpec((height, columns), flat))
        counts.append(steps)
        begin += steps
    anywhere = pl.BlockSpec(memory_space=pl.ANY)
    if arrived is None:
        arrived, arrived_specs = (), []
        heights, scratch = [height], []
    else:
        heights, scratch = [height // 2] * 2, [pltpu.VMEM((height, columns), F32)]
    outputs = [jax.ShapeDtypeStruct((rows, begin * columns), BF16) for rows in heights]
    out_specs = [pl.BlockSpec((rows, columns), lambda i, o: (0, i)) for rows in heights]

    def kernel(order_ref, *refs):
        refs = list(refs)

        def take(count):
            taken, refs[:] = refs[:count], refs[count:]
            return taken

        firsts, seconds, arrived_refs = take(len(pairs)), take(len(pairs)), take(len(arrived))
        take(len(ready))
        sent_refs, kept_refs, (token,) = take(1), take(len(heights) - 1), take(1)
        gradient_kernel(
            counts, order_ref, firsts, seconds, arrived_refs, sent_refs, kept_refs, token, refs
        )

    inputs = [p[0] for p in pairs] + [p[1] for p in pairs] + list(arrived) + list(ready)
    return pl.pallas_call(
        kernel,
        grid_spec=pltpu.PrefetchScalarGridSpec(
            num_scalar_prefetch=1,
            grid=(begin,),
            in_specs=first_specs + second_specs + arrived_specs + [anywhere] * len(ready),
            out_specs=out_specs + [smem()],
            scratch_shapes=scratch,
        ),
        out_shape=outputs + [jax.ShapeDtypeStruct((1,), jnp.int32)],
        compiler_params=params(),
        cost_estimate=cost,
        name="gradient",
    )(order, *inputs)


def to_sibling(blocks):
    return [swapped(block, lambda one: 1) for block in blocks]


def bit_of(index, bit):
    return (index >> bit) & 1


def choose_bit(index, bit, axis):
    def choose(array, mine):
        own = bit_of(index, bit)
        return pick(array, own if mine else 1 - own, axis)

    return choose


def choose_second(index, axis):
    def choose(array, mine):
        own = jnp.where(bit_of(index, 0) == 0, bit_of(index, 2), bit_of(index, 1))
        return pick(array, own if mine else 1 - own, axis)

    return choose


def choose_first(index, axis):
    def choose(array, mine):
        low, high = bit_of(index, 1), bit_of(index, 2)
        if not mine:
            low, high = 1 - low, 1 - high
        core = bit_of(index, 0)
        return jnp.stack(
            [
                pick(array, jnp.where(core == 0, 2 * j + low, 2 * high + j), axis)
                for j in range(2)
            ],
            axis=axis,
        )

    return choose


def swap_bit(bit):
    return lambda value: swapped(value, lambda one: 1 << bit)


def swap_first(value):
    return swapped(value, lambda one: 4 if one & 1 else 2)


def swap_second(value):
    return swapped(value, lambda one: 2 if one & 1 else 4)


def order_first(index):
    core, low, high = bit_of(index, 0), bit_of(index, 1), bit_of(index, 2)

    def some(low, high):
        return [
            4 * z + jnp.where(core == 0, 2 * j + low, 2 * high + j) for z in range(4) for j in range(2)
        ]

    return jnp.stack([core] + some(1 - low, 1 - high) + some(low, high)).astype(jnp.int32)


def stage_sent(kept, arrived, choose):
    return added(choose(kept, False), choose(arrived, False), BF16)


def stage(kept, arrived, choose):
    sent = stage_sent(kept, arrived, choose)
    return sent, added(choose(kept, True), choose(arrived, True), BF16)


def finished(kept, arrived, own, last, cuts, ready):
    rows, width = last.shape[-2:]
    last = last.reshape(rows, width)

    def kernel(own_ref, kept_ref, arrived_ref, last_ref, *refs):
        outs = refs[len(ready) : len(ready) + len(cuts)]
        refs[-1][0] = 0
        begin = 0
        for out, size in zip(outs, cuts):
            at = slice(begin, begin + size)
            first = kept_ref[:, at].astype(F32) + arrived_ref[:, at].astype(F32)
            out[...] = first + last_ref[:, at].astype(F32)
            begin += size

    half = pl.BlockSpec((None, rows, width), lambda i, o: (o[0], 0, 0))

    def flat(columns):
        return pl.BlockSpec((rows, columns), lambda i, o: (0, 0))

    *outs, token = pl.pallas_call(
        kernel,
        grid_spec=pltpu.PrefetchScalarGridSpec(
            num_scalar_prefetch=1,
            grid=(1,),
            in_specs=[half, half, flat(width)]
            + [pl.BlockSpec(memory_space=pl.ANY)] * len(ready),
            out_specs=[flat(size) for size in cuts] + [smem()],
        ),
        out_shape=[jax.ShapeDtypeStruct((rows, size), F32) for size in cuts]
        + [jax.ShapeDtypeStruct((1,), jnp.int32)],
        compiler_params=params(),
        cost_estimate=LITTLE,
        name="finished",
    )(
        own.astype(jnp.int32).reshape(1),
        kept.reshape(2, rows, width),
        arrived.reshape(2, rows, width),
        last,
        *ready,
    )
    return outs, token


def paired(values):
    while len(values) > 1:
        values = [values[k] + values[k + 1] for k in range(0, len(values), 2)]
    return values[0]


def summed_lines(values, top, ready, cut=True):
    rows, lanes = values[0].shape
    rest = top if cut else 0
    count = len(values)

    def kernel(*refs):
        total = paired([ref[...] for ref in refs[:count]])
        refs[-3][...] = total[:top]
        refs[-2][...] = total[rest:]
        refs[-1][0] = 0

    return pl.pallas_call(
        kernel,
        grid=(1,),
        in_specs=[whole((rows, lanes))] * count + [pl.BlockSpec(memory_space=pl.ANY)] * len(ready),
        out_specs=[whole((top, lanes)), whole((rows - rest, lanes)), smem()],
        out_shape=[
            jax.ShapeDtypeStruct((top, lanes), F32),
            jax.ShapeDtypeStruct((rows - rest, lanes), F32),
            jax.ShapeDtypeStruct((1,), jnp.int32),
        ],
        compiler_params=params(),
        cost_estimate=LITTLE,
        name="summed_lines",
    )(*values, *ready)


def unpacked(seq, seq_count, top, values, units, bands, sizes, ready):
    lanes = top.shape[1]
    count = len(values)

    def kernel(seq_ref, top_ref, *refs):
        outs, below, token = refs[count + len(ready) : -2], refs[-1], refs[-2]
        token[0] = 0
        below[...] = paired([ref[...] for ref in refs[:count]])
        f1_w, f1_b, f2_w, f2_b, f3_w, skip = outs[:6]
        f3_w[...] = top_ref[:units]
        skip[...] = top_ref[units]
        f2_w[...] = below[:units, :units]
        f1_w[...] = below[:bands, units:]
        f1_b[...] = below[bands, units:]
        f2_b[...] = below[bands + 1, units:]
        line, seq = units, seq_ref[0]
        outs = list(outs[6:])
        for kinds, size in sizes:
            begin = seq * size
            for kind in range(kinds):
                at = line + begin // lanes
                two = jnp.concatenate([below[pl.ds(at, 1)], below[pl.ds(at + 1, 1)]], axis=1)
                shift = lax.rem(2 * lanes - begin % lanes, 2 * lanes)
                outs.pop(0)[...] = pltpu.roll(two, shift, 1)[0, :size]
                line += size * seq_count // lanes

    shapes = [(bands, units), (units,), (units, units), (units,), (units, lanes), (lanes,)]
    shapes += [(size,) for kinds, size in sizes for _ in range(kinds)]
    return pl.pallas_call(
        kernel,
        grid=(1,),
        in_specs=[smem(), whole(top.shape)]
        + [whole(values[0].shape)] * count
        + [pl.BlockSpec(memory_space=pl.ANY)] * len(ready),
        out_specs=[whole(shape) for shape in shapes] + [smem()],
        out_shape=[jax.ShapeDtypeStruct(shape, F32) for shape in shapes]
        + [jax.ShapeDtypeStruct((1,), jnp.int32)],
        scratch_shapes=[pltpu.VMEM(values[0].shape, F32)],
        compiler_params=params(),
        cost_estimate=LITTLE,
        name="unpacked",
    )(seq, top, *values, *ready)


def block_device(
    tokens,
    cotangent,
    bounds,
    ln1_gain,
    ln1_bias,
    in_weight,
    in_bias,
    short_weight,
    short_bias,
    f1_weight,
    f1_bias,
    f2_weight,
    f2_bias,
    f3_weight,
    filter_skip,
    out_weight,
    out_bias,
    ln2_gain,
    ln2_bias,
    up_weight,
    up_bias,
    down_weight,
    down_bias,
):
    seq_count = lax.axis_size("seq")
    rows, count, width = tokens.shape
    flat = rows * count
    length = count * seq_count
    lanes = f3_weight.shape[1]
    first_channel = (lax.axis_index("seq") * lanes).astype(jnp.int32)
    first = (lax.axis_index("seq") * count).astype(jnp.int32).reshape(1)

    def exchanged(array):
        return lax.all_to_all(array, "seq", split_axis=0, concat_axis=0, tiled=True)

    index = device_index()
    before = passed_along(tokens[:, count - HALO :], "seq", 1)
    beyond = passed_along(tokens[:, :HALO], "seq", -1)
    norm_halves, proj, carried_own = in_forward(
        bounds,
        first,
        before,
        tokens,
        beyond,
        ln1_gain,
        ln1_bias,
        in_weight,
        in_bias,
        short_weight,
        short_bias,
        lanes,
    )
    carried = exchanged(carried_own)

    tables = transform_tables(count)
    table = piece_table(bounds, seq_count, count)
    skip = filter_skip
    taps_spec, kept = taps_and_spectrum(
        first_channel.reshape(1),
        seq_count,
        count,
        f1_weight,
        f1_bias,
        f2_weight,
        f2_bias,
        f3_weight,
        tables,
        carried_own,
    )
    long_own = long_forward(table, carried, taps_spec, skip, tables)
    long = exchanged(long_own)
    x = tokens.reshape(flat, width)
    grad = cotangent.reshape(flat, width)
    g_act = matmul_turned(grad, down_weight, 1024, long_own)
    mixed_halves, resid, norm2_halves, act, act_halves, g_pre, g_up_b = middle_forward(
        bounds,
        first,
        long,
        proj,
        short_weight,
        short_bias,
        x,
        out_weight,
        out_bias,
        ln2_gain,
        ln2_bias,
        up_weight,
        up_bias,
        g_act,
    )
    first_order = order_first(index)
    send_order = (1 - bit_of(index, 0)).astype(jnp.int32).reshape(1)
    down_pairs = [(act_halves, grad)]
    *down_sent, _ = gradient(send_order, down_pairs, None, (), 512)
    down_arrived = to_sibling(down_sent)
    *up_sent, _ = gradient(send_order, [(norm2_halves, g_pre)], None, down_sent, 1024)
    up_arrived = to_sibling(up_sent)
    down_send, down_keep, _ = gradient(first_order, down_pairs, down_arrived, up_sent, 512)
    down_arrived = swap_first(down_send)
    g_long, g_gate, g_resid, g_branch, middle_sums, token = middle_backward(
        bounds,
        first,
        long,
        proj,
        short_weight,
        short_bias,
        resid,
        grad,
        ln2_gain,
        out_weight,
        g_pre,
        up_weight,
        down_send,
    )
    g_long_all = exchanged(g_long)
    g_next = passed_along(g_gate[:, :HALO].astype(BF16), "seq", -1)

    def shaped(array, lead):
        return array.reshape(lead + (-1, array.shape[-1]))

    *out_sent, _ = gradient(send_order, [(mixed_halves, g_branch)], None, (), 1024)
    up_send, up_keep, token = gradient(
        first_order,
        [(norm2_halves, g_pre), (mixed_halves, g_branch)],
        up_arrived + to_sibling(out_sent),
        (),
        1024,
    )
    up_arrived = swap_first(up_send)
    down_send, down_keep = stage(
        shaped(down_keep, (2, 2, 2)),
        shaped(down_arrived, (2, 2, 2)),
        choose_bit(index + token[0], 3, 1),
    )
    down_arrived = swap_bit(3)(down_send)
    g_series, g_taps, g_skip, token = long_backward(
        table, g_long_all, carried, taps_spec, skip, tables, (up_send, down_send)
    )
    g_carried = exchanged(g_series)
    output, token = down_forward(resid, act, down_weight, down_bias, (g_series,))
    output = output.reshape(rows, count, width)
    later = index + token[0]
    down_send, down_keep = stage(down_keep, down_arrived, choose_bit(later, 4, 0))
    down_arrived = swap_bit(4)(down_send)
    up_send, up_keep = stage(
        shaped(up_keep, (4, 2)), shaped(up_arrived, (4, 2)), choose_second(later, 1)
    )
    up_arrived = swap_second(up_send)
    g_proj, short_sums, g_tokens, norm_sums, token = in_backward(
        bounds,
        first,
        g_carried,
        g_gate,
        g_next,
        proj,
        short_weight,
        short_bias,
        in_weight,
        x,
        ln1_gain,
        g_resid,
        (down_send, up_send),
    )
    later = index + token[0]
    down_send = stage_sent(down_keep, down_arrived, choose_second(later, 0))
    down_last = swap_second(down_send)
    up_send, up_keep = stage(
        shaped(up_keep, (2, 2)), shaped(up_arrived, (2, 2)), choose_bit(later, 3, 1)
    )
    up_arrived = swap_bit(3)(up_send)
    in_pairs = [(norm_halves, g_proj)]
    *in_sent, _ = gradient(send_order, in_pairs, None, (down_send, up_send), 1024, MUCH)
    in_send, in_keep, token = gradient(first_order, in_pairs, to_sibling(in_sent), (), 1024)
    in_arrived = swap_first(in_send)
    row_count = lax.axis_size("rows")
    seq_bits = seq_count.bit_length() - 1
    payloads = filter_backward(
        first_channel.reshape(1),
        lax.axis_index("rows").astype(jnp.int32).reshape(1),
        row_count,
        g_taps.reshape(length, lanes),
        kept,
        f2_weight,
        f3_weight,
        g_skip,
        (middle_sums, g_up_b, norm_sums, short_sums),
        (in_send,),
    )
    arrived = [payloads[0]] + [
        swapped(payloads[k], lambda one, k=k: k << seq_bits) for k in range(1, row_count)
    ]
    later = index + mark(*payloads)[0]
    up_send = stage_sent(up_keep, up_arrived, choose_bit(later, 4, 0))
    up_last = swap_bit(4)(up_send)
    left = jnp.where(bit_of(index, 0) == 0, bit_of(index, 2), bit_of(index, 1))
    (g_down_w,), token = finished(
        down_keep, down_arrived, left, down_last, (width,), (up_send,)
    )
    units, bands = f3_weight.shape[0], f1_weight.shape[0]
    top, mine, token = summed_lines(arrived, units + 8, (token,))
    in_send, in_keep = stage(
        shaped(in_keep, (4, 2)),
        shaped(in_arrived, (4, 2)),
        choose_second(index + token[0], 1),
    )
    in_arrived = swap_second(in_send)
    arrived = swapped(mine, lambda one: 1)
    _, mine, token = summed_lines([mine, arrived], 8, (in_send,), False)
    in_send, in_keep = stage(
        shaped(in_keep, (2, 2)), shaped(in_arrived, (2, 2)), choose_bit(index + token[0], 3, 1)
    )
    in_arrived = swap_bit(3)(in_send)
    arrived = swapped(mine, lambda one: 2)
    _, mine, token = summed_lines([mine, arrived], 8, (in_send,), False)
    (g_up_w, g_out_w), token = finished(
        up_keep, up_arrived, bit_of(index, 4), up_last, (up_weight.shape[1], width), (token,)
    )
    in_send = stage_sent(in_keep, in_arrived, choose_bit(index + token[0], 4, 0))
    in_last = swap_bit(4)(in_send)
    arrived = swapped(mine, lambda one: 4)
    shares = 1 << device_bits()
    sizes = ((6, width // shares), (1, up_weight.shape[1] // shares), (5, 3 * width // shares))
    seq = lax.axis_index("seq").astype(jnp.int32).reshape(1)
    *small, token = unpacked(
        seq, seq_count, top, [mine, arrived], units, bands, sizes, (in_send,)
    )
    (g_in_w,), _ = finished(
        in_keep, in_arrived, bit_of(index, 4), in_last, (3 * width,), (token,)
    )
    (g_f1_w, g_f1_b, g_f2_w, g_f2_b, g_f3_w, g_skip, *small) = small
    (g_ln2_gain, g_ln2_bias, g_out_b, g_down_b, g_ln1_gain, g_ln1_bias, g_up_b, *small) = small
    *g_short_w, g_short_b, g_in_b = small
    g_short_w = jnp.stack(g_short_w)
    grad_tokens = g_tokens.reshape(rows, count, width)
    return (
        output,
        grad_tokens,
        g_ln1_gain,
        g_ln1_bias,
        g_in_w,
        g_in_b,
        g_short_w,
        g_short_b,
        g_f1_w,
        g_f1_b,
        g_f2_w,
        g_f2_b,
        g_f3_w,
        g_skip,
        g_out_w,
        g_out_b,
        g_ln2_gain,
        g_ln2_bias,
        g_up_w,
        g_up_b,
        g_down_w,
        g_down_b,
    )


def per_device(tokens, *others):
    shares = lax.axis_size("rows") * lax.axis_size("seq")
    count, width = tokens.shape[1:]
    hidden = others[20].shape[0]
    lanes = width // lax.axis_size("seq")
    fits = shares == 32 and width == 1024 and hidden == 4096 and lanes == 128 and count % 128 == 0
    return (block_device if fits else plain_device)(tokens, *others)


def solution(mesh):
    return jax.shard_map(
        per_device,
        mesh=mesh,
        in_specs=(
            P("rows", "seq", None),
            P("rows", "seq", None),
            P("rows", None),
            P(),
            P(),
            P(),
            P(),
            P(),
            P(),
            P(),
            P(),
            P(),
            P(),
            P(None, "seq"),
            P("seq"),
            P(),
            P(),
            P(),
            P(),
            P(),
            P(),
            P(),
            P(),
        ),
        out_specs=(
            P("rows", "seq", None),
            P("rows", "seq", None),
            P(("rows", "seq")),
            P(("rows", "seq")),
            P(("rows", "seq"), None),
            P(("rows", "seq")),
            P(None, ("rows", "seq")),
            P(("rows", "seq")),
            P(),
            P(),
            P(),
            P(),
            P(None, "seq"),
            P("seq"),
            P(("rows", "seq"), None),
            P(("rows", "seq")),
            P(("rows", "seq")),
            P(("rows", "seq")),
            P(("rows", "seq"), None),
            P(("rows", "seq")),
            P(("rows", "seq"), None),
            P(("rows", "seq")),
        ),
        check_vma=False,
    )
```

```python
import functools
import math

import jax
import jax.numpy as jnp
import ml_dtypes
import numpy as np
from jax import lax
from jax.experimental import pallas as pl
from jax.experimental.pallas import tpu as pltpu
from jax.sharding import PartitionSpec as P

D = 1024
EMB = 33
HIGH = lax.Precision.HIGHEST
eps = 1e-05
slow_rate = math.log(100.0) / 1.5
fast_rate = math.log(100.0) / 0.3
BOTH = ("rows", "seq")
F32 = jnp.float32
BF16 = jnp.bfloat16
VMEM_MIB = 58
LITTLE = pl.CostEstimate(flops=1, bytes_accessed=1, transcendentals=0)
MUCH = pl.CostEstimate(flops=5 * 10**10, bytes_accessed=2 * 10**8, transcendentals=0)


def passed_along(value, axis, steps):
    count = lax.axis_size(axis)
    first, last = (max(0, -steps), min(count, count - steps))
    return lax.ppermute(value, axis, [(source, source + steps) for source in range(first, last)])


def layer_norm(values, gain, shift):
    center = values - jnp.mean(values, axis=-1, keepdims=True)
    spread = jnp.mean(center * center, axis=-1, keepdims=True)
    return center * lax.rsqrt(spread + eps) * gain + shift


def gelu_tanh(values):
    return jax.nn.gelu(values, approximate=True)


def features(length):
    steps = np.arange(length, dtype=np.float64)
    bands = (EMB - 1) // 2
    freqs = 0.0001 + np.arange(bands, dtype=np.float64) * ((bands - 1 - 0.0001) / (bands - 1))
    angles = (steps * (2.0 * math.pi / length))[:, None] * freqs[None, :]
    timeline = steps / (length - 1)
    table = np.concatenate([timeline[:, None], np.cos(angles), -np.sin(angles)], axis=1)
    return jnp.asarray(table.astype(np.float32)), jnp.asarray(timeline.astype(np.float32))


def filter_taps(w_one, b_one, w_two, b_two, w_three, first, length):
    feats, timeline = features(length)
    hidden = jnp.sin(jnp.dot(feats, w_one, precision=HIGH) + b_one)
    hidden = jnp.sin(jnp.dot(hidden, w_two, precision=HIGH) + b_two)
    raw_taps = jnp.dot(hidden, w_three, precision=HIGH)
    channels = (first + jnp.arange(w_three.shape[1], dtype=jnp.int32)).astype(F32)
    rates = slow_rate + channels * ((fast_rate - slow_rate) / (D - 1))
    return raw_taps * jnp.exp(-timeline[:, None] * rates[None, :])


def close_dot(left, right, dims):
    def one(a, b):
        return lax.dot_general(a, b, (dims, ((), ())), preferred_element_type=F32)

    (a, a_rest), (b, b_rest) = split32(left), split32(right)
    return one(a, b) + one(a, b_rest) + one(a_rest, b)


def line_up(out_ref, count, parts):
    line = 0
    for ref, lead, rows in parts:
        width = ref.shape[-1]
        share = rows * width // count // 128
        for z in range(count):
            for k in range(share):
                at = (z * share + k) * 128
                row, lane = at // width, at % width
                index = ((row,) if rows > 1 else ()) + tuple(lead)
                value = ref[index + (slice(lane, lane + 128),)]
                out_ref[z, line + k : line + k + 1] = value.reshape(1, 128)
        line += share


def filter_backward_kernel(
    first_ref,
    row_ref,
    grad_ref,
    feats_ref,
    one_ref,
    two_ref,
    w2_ref,
    w3_ref,
    skip_ref,
    middle_ref,
    up_ref,
    norm_ref,
    short_ref,
    outs,
    lines,
    out_ref,
):
    lines[...] = jnp.zeros_like(lines)
    parts = [(middle_ref, (k,), 1) for k in range(4)] + [(norm_ref, (k,), 1) for k in range(2)]
    parts += [(up_ref, (0,), 1)] + [(short_ref, (k,), 3) for k in range(5)]
    line_up(lines, len(outs), parts)
    length, lanes = grad_ref.shape
    units = one_ref.shape[1] // 2
    bands = feats_ref.shape[1]
    inner = grad_ref[...] * decay(first_ref, 0, length, lanes, length)
    over_time, over_last = ((0,), (0,)), ((1,), (1,))
    out_ref[...] = jnp.zeros_like(out_ref)
    out_ref[:units] = close_dot(two_ref[:, :units], inner, over_time)
    out_ref[units : units + 1] = skip_ref[...]
    two = close_dot(inner, w3_ref[...].astype(F32), over_last) * two_ref[:, units:]
    one = close_dot(two, w2_ref[...].astype(F32), over_last) * one_ref[:, units:]
    below = units + 8
    out_ref[below : below + units, :units] = close_dot(one_ref[:, :units], two, over_time)
    out_ref[below : below + bands, units:] = close_dot(feats_ref[...], one, over_time)
    out_ref[below + bands : below + bands + 1, units:] = jnp.sum(one, axis=0, keepdims=True)
    out_ref[below + bands + 1 : below + bands + 2, units:] = jnp.sum(two, axis=0, keepdims=True)
    for k, payload in enumerate(outs):
        payload[: 2 * units + 8] = out_ref[...]
        payload[2 * units + 8 :] = lines[row_ref[0] ^ k]


LINES = 56


def filter_backward(first, row, count, g_taps, kept, w_two, w_three, g_skip, sums, ready):
    feats, one, two = kept
    units, lanes = w_three.shape
    vmem = pl.BlockSpec(memory_space=pltpu.VMEM)
    height = 2 * units + 8

    def kernel(*refs):
        outs, scratch = refs[13 + len(ready) : -2], refs[-2:]
        filter_backward_kernel(*refs[:13], outs, *scratch)

    return pl.pallas_call(
        kernel,
        in_specs=[smem()] * 2 + [vmem] * 11 + [pl.BlockSpec(memory_space=pl.ANY)] * len(ready),
        out_specs=[vmem] * count,
        out_shape=[jax.ShapeDtypeStruct((height + LINES, lanes), F32)] * count,
        scratch_shapes=[
            pltpu.VMEM((count, LINES, lanes), F32),
            pltpu.VMEM((height, lanes), F32),
        ],
        compiler_params=pltpu.CompilerParams(vmem_limit_bytes=VMEM_MIB * 2**20),
        cost_estimate=MUCH,
        name="filter_backward",
    )(first, row, g_taps, feats, one, two, w_two, w_three, g_skip, *sums, *ready)


def split16(values):
    high = values.astype(ml_dtypes.bfloat16)
    return high, (values - high.astype(np.float64)).astype(ml_dtypes.bfloat16)


def transform_tables(block):
    freq = np.arange(block)[:, None]
    time = np.arange(block)[None, :]
    angles = ((2 * freq + 1) * time % (4 * block)) * (math.pi / (2 * block))
    ahead = np.concatenate([np.cos(angles), -np.sin(angles)], axis=0)
    ahead_high, ahead_low = split16(ahead)
    back_high, back_low = split16(ahead.T / block)
    return tuple(jnp.asarray(t) for t in (ahead_high, ahead_low, back_high, back_low))


def piece_table(bounds, blocks, block):
    length = blocks * block
    edges = jnp.broadcast_to(jnp.arange(blocks, dtype=jnp.int32) * block, (bounds.shape[0], blocks))
    for cut in range(bounds.shape[1]):
        one = bounds[:, cut : cut + 1]
        low = jnp.concatenate([jnp.full_like(one, -1), edges], axis=1)
        high = jnp.concatenate([edges, jnp.full_like(one, length)], axis=1)
        edges = jnp.maximum(low, jnp.minimum(one, high))
    ends = jnp.concatenate([edges[:, 1:], jnp.full_like(edges[:, :1], length)], axis=1)
    index = jnp.minimum(edges // block, blocks - 1)
    start = jnp.max(
        jnp.where(bounds[:, :, None] <= edges[:, None, :], bounds[:, :, None], 0), axis=1
    )
    stop = jnp.min(
        jnp.where(bounds[:, :, None] > edges[:, None, :], bounds[:, :, None], length), axis=1
    )
    empty = ends <= edges
    earlier = jnp.where(empty, 0, index - start // block + 1)
    later = jnp.where(empty, 0, (stop - 1) // block - index + 1)
    return jnp.stack([edges, ends, index, earlier, later]).astype(jnp.int32)


def dot32(left, right):
    return jnp.dot(left, right, preferred_element_type=F32)


def split32(values):
    high = values.astype(BF16)
    return high, (values - high.astype(F32)).astype(BF16)


def wide_dot(high, low, values):
    top, rest = split32(values)
    return dot32(high, top) + dot32(high, rest) + dot32(low, top)


def alternating(rows, lanes):
    odd = lax.broadcasted_iota(jnp.int32, (rows, lanes), 0) % 2
    return 1.0 - 2.0 * odd.astype(F32)


def sine_cosine(angle):
    turns = jnp.floor(angle * (2.0 / math.pi) + 0.5)
    rest = angle - turns * 1.5703125
    rest = rest - turns * 4.837512969970703125e-4
    rest = rest - turns * 7.549789948768648e-8
    square = rest * rest
    sine = ((-1.9515295891e-4 * square + 8.3321608736e-3) * square - 1.6666654611e-1) * square
    sine = sine * rest + rest
    cosine = (2.443315711809948e-5 * square - 1.388731625493765e-3) * square
    cosine = (cosine + 4.166664568298827e-2) * square * square - 0.5 * square + 1.0
    quarter = turns.astype(jnp.int32)
    swap = (quarter & 1) == 1
    sine, cosine = jnp.where(swap, cosine, sine), jnp.where(swap, sine, cosine)
    return (
        jnp.where((quarter & 2) == 2, -sine, sine),
        jnp.where(((quarter + 1) & 2) == 2, -cosine, cosine),
    )


def near_dot(left, right):
    top, rest = split32(left)
    return dot32(top, right) + dot32(rest, right)


def decay(first_ref, begin, count, lanes, length):
    spot = (lax.broadcasted_iota(jnp.int32, (count, lanes), 0) + begin).astype(F32)
    channel = (lax.broadcasted_iota(jnp.int32, (1, lanes), 1) + first_ref[0]).astype(F32)
    rates = slow_rate + channel * ((fast_rate - slow_rate) / (D - 1))
    return jnp.exp(-(spot * (1.0 / (length - 1))) * rates)


def taps_kernel(
    first_ref, feats_ref, w1, b1, w2, b2, w3, high_ref, low_ref, _, out_ref, one_ref, two_ref, own
):
    blocks, double, lanes = out_ref.shape
    block = double // 2
    for k in range(blocks):
        at = slice(k * block, (k + 1) * block)
        sine, cosine = sine_cosine(near_dot(feats_ref[at], w1[...]) + row_of(b1))
        one_ref[at] = jnp.concatenate([sine, cosine], axis=1)
        sine, cosine = sine_cosine(near_dot(sine, w2[...]) + row_of(b2))
        two_ref[at] = jnp.concatenate([sine, cosine], axis=1)
        taps = near_dot(sine, w3[...]) * decay(first_ref, k * block, block, lanes, blocks * block)
        own[k] = wide_dot(high_ref[...], low_ref[...], taps)
    sign = alternating(block, lanes)
    out_ref[0] = own[0]
    for k in range(1, blocks):
        out_ref[k, :block] = own[k, :block] - sign * own[k - 1, block:]
        out_ref[k, block:] = own[k, block:] + sign * own[k - 1, :block]


def taps_and_spectrum(first, blocks, block, w1, b1, w2, b2, w3, tables, ready):
    lanes, units = w3.shape[1], w2.shape[0]
    length = blocks * block
    feats, _ = features(length)
    vmem = pl.BlockSpec(memory_space=pltpu.VMEM)
    spectra, one, two = pl.pallas_call(
        taps_kernel,
        in_specs=[smem()] + [vmem] * 8 + [pl.BlockSpec(memory_space=pl.ANY)],
        out_specs=[vmem] * 3,
        out_shape=[jax.ShapeDtypeStruct((blocks, 2 * block, lanes), F32)]
        + [jax.ShapeDtypeStruct((length, 2 * units), F32)] * 2,
        scratch_shapes=[pltpu.VMEM((blocks, 2 * block, lanes), F32)],
        compiler_params=pltpu.CompilerParams(vmem_limit_bytes=VMEM_MIB * 2**20),
        cost_estimate=LITTLE,
        name="taps_and_spectrum",
    )(first, feats, w1, b1, w2, b2, w3, tables[0], tables[1], ready)
    return spectra, (feats, one, two)


def piece_mask(table_ref, row, piece, block, lanes):
    at = table_ref[2, row, piece]
    spot = lax.broadcasted_iota(jnp.int32, (block, lanes), 0) + at * block
    return at, (spot >= table_ref[0, row, piece]) & (spot < table_ref[1, row, piece])


def piece_spectra(table_ref, series_ref, ahead_ref, out_ref):
    blocks, rows, block, lanes = series_ref.shape
    for piece in range(out_ref.shape[0]):
        parts = []
        for row in range(rows):
            at, inside = piece_mask(table_ref, row, piece, block, lanes)
            values = series_ref[at, row].astype(F32)
            parts.append(jnp.where(inside, values, 0.0).astype(BF16))
        out_ref[piece] = dot32(ahead_ref[...], jnp.concatenate(parts, axis=1))


def each_piece(table_ref, which, pieces, rows, lanes, blocks, visit):
    def body(index, carry):
        piece, row = index // rows, index % rows
        lane = pl.ds(pl.multiple_of(row * lanes, lanes), lanes)
        found = table_ref[which, row, piece]
        for count in range(blocks + 1):

            @pl.when(found == count)
            def _(count=count):
                visit(piece, lane, count)

        return carry

    lax.fori_loop(0, pieces * rows, body, 0)


def halves_of(block, tile):
    for begin in range(0, block, tile):
        yield pl.ds(begin, tile), pl.ds(block + begin, tile)


def couple(table_ref, step, taps_ref, series_ref, into_ref):
    blocks, double, lanes = taps_ref.shape
    block = double // 2
    pieces, _, both = series_ref.shape

    def visit(piece, lane, count):
        for real_rows, imag_rows in halves_of(block, 32):
            real = imag = jnp.zeros((32, lanes), F32)
            for k in range(count):
                tap_r, tap_i = taps_ref[k, real_rows, :], taps_ref[k, imag_rows, :]
                val_r = series_ref[piece + step * k, real_rows, lane]
                val_i = series_ref[piece + step * k, imag_rows, lane]
                if step > 0:
                    real = real + (tap_r * val_r + tap_i * val_i)
                    imag = imag + (tap_r * val_i - tap_i * val_r)
                else:
                    real = real + (tap_r * val_r - tap_i * val_i)
                    imag = imag + (tap_r * val_i + tap_i * val_r)
            into_ref[piece, real_rows, lane] = real
            into_ref[piece, imag_rows, lane] = imag

    each_piece(table_ref, 3 if step < 0 else 4, pieces, both // lanes, lanes, blocks, visit)


def correlate(table_ref, series_ref, grad_ref, into_ref):
    blocks, double, lanes = into_ref.shape
    block = double // 2
    pieces, _, both = series_ref.shape
    into_ref[...] = jnp.zeros_like(into_ref)

    def visit(piece, lane, count):
        for real_rows, imag_rows in halves_of(block, 32):
            if count:
                out_r, out_i = grad_ref[piece, real_rows, lane], grad_ref[piece, imag_rows, lane]
            for k in range(count):
                val_r = series_ref[piece - k, real_rows, lane]
                val_i = series_ref[piece - k, imag_rows, lane]
                into_ref[k, real_rows, :] += val_r * out_r + val_i * out_i
                into_ref[k, imag_rows, :] += val_r * out_i - val_i * out_r

    each_piece(table_ref, 3, pieces, both // lanes, lanes, blocks, visit)


def write_pieces(table_ref, work, back_ref, series_ref, skip_ref, out_ref):
    blocks, rows, block, lanes = series_ref.shape
    for piece in range(work.shape[0]):
        result = dot32(back_ref[...], work[piece].astype(BF16))
        for row in range(rows):
            at, inside = piece_mask(table_ref, row, piece, block, lanes)
            direct = skip_ref[...].astype(F32).reshape(1, -1) * series_ref[at, row].astype(F32)
            value = result[:, row * lanes : (row + 1) * lanes] + direct
            kept = out_ref[at, row, :block].astype(F32)
            out_ref[at, row, :block] = jnp.where(inside, value, kept).astype(BF16)


def long_forward_kernel(
    table_ref, series_ref, taps_ref, skip_ref, ahead_ref, back_ref, out_ref, spec, work
):
    piece_spectra(table_ref, series_ref, ahead_ref, spec)
    couple(table_ref, -1, taps_ref, spec, work)
    write_pieces(table_ref, work, back_ref, series_ref, skip_ref, out_ref)


def long_forward(table, series, taps_spec, skip, tables):
    blocks, rows, block, lanes = series.shape
    pieces = table.shape[2]
    vmem = pl.BlockSpec(memory_space=pltpu.VMEM)
    return pl.pallas_call(
        long_forward_kernel,
        in_specs=[smem()] + [vmem] * 5,
        out_specs=vmem,
        out_shape=jax.ShapeDtypeStruct(series.shape, BF16),
        scratch_shapes=[pltpu.VMEM((pieces, 2 * block, rows * lanes), F32)] * 2,
        compiler_params=pltpu.CompilerParams(vmem_limit_bytes=VMEM_MIB * 2**20),
        cost_estimate=MUCH,
        name="long_forward",
    )(table, series, taps_spec, skip, tables[0], tables[2])


def long_backward_kernel(
    table_ref, grad_ref, series_ref, taps_ref, skip_ref, ahead_ref, back_ref, *others
):
    out_ref, taps_out_ref, skip_out_ref, token_out, spec, grad_spec, work, cross = others[-8:]
    token_out[0] = 0
    blocks, rows, block, lanes = series_ref.shape
    piece_spectra(table_ref, grad_ref, ahead_ref, grad_spec)
    couple(table_ref, 1, taps_ref, grad_spec, work)
    write_pieces(table_ref, work, back_ref, grad_ref, skip_ref, out_ref)
    for at in range(blocks):
        for row in range(rows):
            if at + 1 < blocks:
                out_ref[at, row, block:] = out_ref[at + 1, row, : out_ref.shape[2] - block]
            else:
                out_ref[at, row, block:] = jnp.zeros_like(out_ref[at, row, block:])
    piece_spectra(table_ref, series_ref, ahead_ref, spec)
    correlate(table_ref, spec, grad_spec, cross)
    sign = alternating(block, lanes)
    for k in range(blocks):
        if k + 1 < blocks:
            cross[k, :block] = cross[k, :block] + sign * cross[k + 1, block:]
            cross[k, block:] = cross[k, block:] - sign * cross[k + 1, :block]
        taps_out_ref[k] = dot32(back_ref[...], cross[k].astype(BF16))
    total = jnp.zeros((8, lanes), F32)
    for at in range(blocks):
        for row in range(rows):
            both = grad_ref[at, row].astype(F32) * series_ref[at, row].astype(F32)
            total = total + jnp.sum(both.reshape(block // 8, 8, lanes), axis=0)
    skip_out_ref[...] = jnp.sum(total, axis=0, keepdims=True)


def long_backward(table, grad, series, taps_spec, skip, tables, ready):
    blocks, rows, block, lanes = series.shape
    pieces = table.shape[2]
    vmem = pl.BlockSpec(memory_space=pltpu.VMEM)
    return pl.pallas_call(
        long_backward_kernel,
        in_specs=[smem()] + [vmem] * 6 + [pl.BlockSpec(memory_space=pl.ANY)] * len(ready),
        out_specs=[vmem] * 3 + [smem()],
        out_shape=[
            jax.ShapeDtypeStruct((blocks, rows, block + HALO, lanes), BF16),
            jax.ShapeDtypeStruct((blocks, block, lanes), F32),
            jax.ShapeDtypeStruct((1, lanes), F32),
            jax.ShapeDtypeStruct((1,), jnp.int32),
        ],
        scratch_shapes=[pltpu.VMEM((pieces, 2 * block, rows * lanes), F32)] * 3
        + [pltpu.VMEM((blocks, 2 * block, lanes), F32)],
        compiler_params=pltpu.CompilerParams(vmem_limit_bytes=VMEM_MIB * 2**20),
        cost_estimate=MUCH,
        name="long_backward",
    )(table, grad, series, taps_spec, skip, tables[0], tables[2], *ready)


def document_masks(bounds, positions, length):
    lower = jnp.concatenate([jnp.zeros_like(bounds[:, :1]), bounds], axis=1)
    upper = jnp.concatenate([bounds, jnp.full_like(bounds[:, :1], length)], axis=1)
    inside = (positions[None, None, :] >= lower[:, :, None]) & (
        positions[None, None, :] < upper[:, :, None]
    )
    return inside.astype(F32)


def cos_sin(count_a, count_b, modulus):
    table = (
        jnp.arange(count_a, dtype=jnp.int32)[:, None]
        * jnp.arange(count_b, dtype=jnp.int32)[None, :]
        % modulus
    )
    angles = table.astype(F32) * (2.0 * math.pi / modulus)
    return (jnp.cos(angles), jnp.sin(angles))


def make_plan(blocks, block_len):
    outer = 2 * blocks
    cos_outer, sin_outer = cos_sin(outer, outer, outer)
    cos_twist, sin_twist = cos_sin(outer, block_len, outer * block_len)
    cos_inner, sin_inner = cos_sin(block_len, block_len, block_len)
    return (blocks, block_len, cos_outer, sin_outer, cos_twist, sin_twist, cos_inner, sin_inner)


def right_mul(left, table):
    return jnp.einsum("...km,mj->...kj", left, table, precision=HIGH)


def spectrum(series, plan):
    blocks, block_len, cos_outer, sin_outer, cos_twist, sin_twist, cos_inner, sin_inner = plan
    folded = series.reshape(series.shape[:-1] + (blocks, block_len))
    real_a = jnp.einsum("kn,...nm->...km", cos_outer[:, :blocks], folded, precision=HIGH)
    imag_a = -jnp.einsum("kn,...nm->...km", sin_outer[:, :blocks], folded, precision=HIGH)
    real_t = real_a * cos_twist + imag_a * sin_twist
    imag_t = imag_a * cos_twist - real_a * sin_twist
    real_x = right_mul(real_t, cos_inner) + right_mul(imag_t, sin_inner)
    imag_x = right_mul(imag_t, cos_inner) - right_mul(real_t, sin_inner)
    return (real_x, imag_x)


def inverse(real_x, imag_x, plan):
    blocks, block_len, cos_outer, sin_outer, cos_twist, sin_twist, cos_inner, sin_inner = plan
    real_b = right_mul(real_x, cos_inner) - right_mul(imag_x, sin_inner)
    imag_b = right_mul(imag_x, cos_inner) + right_mul(real_x, sin_inner)
    real_u = real_b * cos_twist - imag_b * sin_twist
    imag_u = imag_b * cos_twist + real_b * sin_twist
    folded = jnp.einsum("nk,...km->...nm", cos_outer[:blocks], real_u, precision=HIGH) - jnp.einsum(
        "nk,...km->...nm", sin_outer[:blocks], imag_u, precision=HIGH
    )
    folded = folded * (1.0 / (2 * blocks * block_len))
    return folded.reshape(folded.shape[:-2] + (blocks * block_len,))


def by_channel(blocked):
    blocks, rows, block, lanes = blocked.shape
    return blocked.astype(F32).transpose(1, 3, 0, 2).reshape(rows, lanes, blocks * block)


def by_block(series, blocks):
    rows, lanes, length = series.shape
    return series.reshape(rows, lanes, blocks, length // blocks).transpose(2, 0, 3, 1).astype(BF16)


class WholeSpectra:
    def __init__(self, bounds, taps, skip):
        blocks, block, lanes = taps.shape
        self.blocks, self.plan = blocks, make_plan(blocks, block)
        length = blocks * block
        everywhere = jnp.arange(length, dtype=jnp.int32)
        self.masks = document_masks(bounds, everywhere, length)[:, :, None, :]
        self.skip = skip[0][None, :, None]
        self.taps_real, self.taps_imag = spectrum(taps.reshape(length, lanes).T, self.plan)

    def forward(self, series):
        carried = by_channel(series)
        self.carried = carried
        real, imag = spectrum(self.masks * carried[:, None], self.plan)
        self.spec = real, imag
        docs = inverse(
            real * self.taps_real - imag * self.taps_imag,
            real * self.taps_imag + imag * self.taps_real,
            self.plan,
        )
        conv = jnp.sum(self.masks * docs, axis=1) + self.skip * carried
        return by_block(conv, self.blocks)

    def backward(self, grad):
        g_long = by_channel(grad)
        spec_real, spec_imag = self.spec
        g_skip = jnp.sum(g_long * self.carried, axis=(0, 2))
        real, imag = spectrum(self.masks * g_long[:, None], self.plan)
        docs = inverse(
            self.taps_real * real + self.taps_imag * imag,
            self.taps_real * imag - self.taps_imag * real,
            self.plan,
        )
        g_carried = jnp.sum(self.masks * docs, axis=1) + self.skip * g_long
        cross_real = jnp.sum(real * spec_real + imag * spec_imag, axis=(0, 1))
        cross_imag = jnp.sum(imag * spec_real - real * spec_imag, axis=(0, 1))
        g_taps = inverse(cross_real, cross_imag, self.plan)
        return by_block(g_carried, self.blocks), g_taps.T, g_skip[None, :]


def device_index():
    return lax.axis_index("rows") * lax.axis_size("seq") + lax.axis_index("seq")


def device_bits():
    return int(math.log2(lax.axis_size("rows") * lax.axis_size("seq")))


def swapped(value, mask_of):
    count = lax.axis_size("rows") * lax.axis_size("seq")
    return lax.ppermute(value, BOTH, [(one, one ^ mask_of(one)) for one in range(count)])


def pick(array, index, axis):
    return lax.dynamic_index_in_dim(array, index, axis=axis, keepdims=False)


def added(kept, arrived, kind):
    return (kept.astype(F32) + arrived.astype(F32)).astype(kind)


def halved(pieces, bit, axis, kind):
    mine = (device_index() >> bit) & 1
    arrived = swapped(pick(pieces, 1 - mine, axis), lambda one: 1 << bit)
    return added(pick(pieces, mine, axis), arrived, kind)


def quartered(pieces, axis, kind):
    index = device_index()
    core, low, high = index & 1, (index >> 1) & 1, (index >> 2) & 1

    def two(low_bit, high_bit):
        return jnp.stack(
            [
                pick(pieces, jnp.where(core == 0, 2 * j + low_bit, 2 * high_bit + j), axis)
                for j in range(2)
            ],
            axis=axis,
        )

    arrived = swapped(two(1 - low, 1 - high), lambda one: 4 if one & 1 else 2)
    pieces = added(two(low, high), arrived, kind)
    mine = jnp.where(core == 0, high, low)
    arrived = swapped(pick(pieces, 1 - mine, axis), lambda one: 2 if one & 1 else 4)
    return added(pick(pieces, mine, axis), arrived, kind)


def scattered(pieces, kind):
    rest = pieces.shape[1:]
    bits = device_bits()
    pieces = quartered(pieces.reshape((-1, 4) + rest), 1, kind)
    for bit in range(3, bits):
        last = bit == bits - 1
        pieces = halved(pieces.reshape((-1, 2) + rest), bit, 1, F32 if last else kind)
    return pieces.reshape(rest)


def weight_gradient(first, second):
    tokens, width = first.shape
    shares = 1 << device_bits()
    share = width // shares
    core = device_index() & 1
    halves = first.reshape(tokens, shares // 2, 2, share).transpose(2, 0, 1, 3)
    halves = halves.reshape(2, tokens, width // 2)

    def product(which):
        return jnp.einsum(
            "ti,tj->ij", pick(halves, which, 0), second, preferred_element_type=F32
        )

    arrived = swapped(product(1 - core).astype(BF16), lambda one: 1)
    kept = added(product(core), arrived, BF16)
    return scattered(kept.reshape(shares // 2, share, second.shape[1]), BF16)


def small_scattered(vectors):
    pieces = halved(vectors.reshape(-1, 2, vectors.shape[1]), 0, 1, F32)
    return scattered(pieces, F32)


def summed(value, bits):
    for bit in bits:
        value = value + swapped(value, lambda one, bit=bit: 1 << bit)
    return value


def back_product(grad_low, weight):
    return jnp.einsum("tj,ij->ti", grad_low, weight, preferred_element_type=F32)


def plain_device(
    tokens,
    cotangent,
    bounds,
    ln1_gain,
    ln1_bias,
    in_weight,
    in_bias,
    short_weight,
    short_bias,
    f1_weight,
    f1_bias,
    f2_weight,
    f2_bias,
    f3_weight,
    filter_skip,
    out_weight,
    out_bias,
    ln2_gain,
    ln2_bias,
    up_weight,
    up_bias,
    down_weight,
    down_bias,
):
    seq_count = lax.axis_size("seq")
    row_count, tok_count, width = tokens.shape
    flat_count = row_count * tok_count
    length = tok_count * seq_count
    lanes = f3_weight.shape[1]
    first_channel = lax.axis_index("seq") * lanes
    x_in = tokens.astype(F32).reshape(flat_count, width)
    n1, ln1_pull = jax.vjp(layer_norm, x_in, ln1_gain.astype(F32), ln1_bias.astype(F32))
    n1_low = n1.astype(BF16)
    proj = jnp.dot(n1_low, in_weight, preferred_element_type=F32) + in_bias.astype(F32)
    proj_low = proj.astype(BF16).reshape(row_count, tok_count, 3 * width)
    here = lax.axis_index("seq") * tok_count + jnp.arange(tok_count, dtype=jnp.int32)
    starts = jnp.max(
        jnp.where(bounds[:, :, None] <= here[None, None, :], bounds[:, :, None], 0), axis=1
    )
    keep_one = (here[None, :] - 1 >= starts).astype(F32)[:, :, None]
    keep_two = (here[None, :] - 2 >= starts).astype(F32)[:, :, None]
    rim = passed_along(proj_low[:, tok_count - 2 :, :], "seq", 1)
    extended = jnp.concatenate([rim, proj_low], axis=1).astype(F32)
    current = extended[:, 2:, :]
    before_one = extended[:, 1:-1, :]
    before_two = extended[:, :-2, :]
    taps_short = short_weight.astype(F32)
    shorted = (
        taps_short[0] * current
        + keep_one * taps_short[1] * before_one
        + keep_two * taps_short[2] * before_two
        + short_bias.astype(F32)
    )
    gate_out = shorted[:, :, :width]
    gate_in = shorted[:, :, width : 2 * width]
    values = shorted[:, :, 2 * width :]
    carried_low = (gate_in * values).astype(BF16)

    def to_channels(array):
        array = array.reshape(row_count, tok_count, seq_count, lanes).transpose(2, 0, 1, 3)
        return lax.all_to_all(array, "seq", split_axis=0, concat_axis=0, tiled=True)

    def to_positions(array):
        array = lax.all_to_all(array, "seq", split_axis=0, concat_axis=0, tiled=True)
        return array.transpose(1, 2, 0, 3).reshape(row_count, tok_count, width)

    carried = to_channels(carried_low)

    def make_taps(w_one, b_one, w_two, b_two, w_three):
        return filter_taps(w_one, b_one, w_two, b_two, w_three, first_channel, length)

    taps, filter_pull = jax.vjp(
        make_taps,
        f1_weight.astype(F32),
        f1_bias.astype(F32),
        f2_weight.astype(F32),
        f2_bias.astype(F32),
        f3_weight.astype(F32),
    )
    long_filter = WholeSpectra(
        bounds, taps.reshape(seq_count, tok_count, lanes), filter_skip.astype(F32)[None, :]
    )
    long_low = long_filter.forward(carried)
    long_seq = to_positions(long_low).astype(F32)
    mixed_low = (gate_out * long_seq).astype(BF16).reshape(flat_count, width)
    branch = jnp.dot(mixed_low, out_weight, preferred_element_type=F32) + out_bias.astype(F32)
    resid = x_in + branch
    n2, ln2_pull = jax.vjp(layer_norm, resid, ln2_gain.astype(F32), ln2_bias.astype(F32))
    n2_low = n2.astype(BF16)
    pre = jnp.dot(n2_low, up_weight, preferred_element_type=F32) + up_bias.astype(F32)
    act, gelu_pull = jax.vjp(gelu_tanh, pre)
    act_low = act.astype(BF16)
    result = (
        resid
        + jnp.dot(act_low, down_weight, preferred_element_type=F32)
        + down_bias.astype(F32)
    )
    output = result.astype(BF16).reshape(row_count, tok_count, width)
    grad_low = cotangent.reshape(flat_count, width)
    grad_float = grad_low.astype(F32)
    g_down_w = weight_gradient(act_low, grad_low)
    g_down_b = jnp.sum(grad_float, axis=0)
    g_act = back_product(grad_low, down_weight)
    (g_pre,) = gelu_pull(g_act)
    g_pre_low = g_pre.astype(BF16)
    g_up_w = weight_gradient(n2_low, g_pre_low)
    g_up_b = jnp.sum(g_pre_low.astype(F32), axis=0)
    g_n2 = back_product(g_pre_low, up_weight)
    g_resid_part, g_ln2_gain, g_ln2_bias = ln2_pull(g_n2)
    g_resid = grad_float + g_resid_part
    g_branch_low = g_resid.astype(BF16)
    g_out_w = weight_gradient(mixed_low, g_branch_low)
    g_out_b = jnp.sum(g_branch_low.astype(F32), axis=0)
    g_mixed = back_product(g_branch_low, out_weight).reshape(row_count, tok_count, width)
    g_gate_out = g_mixed * long_seq
    g_long_low = (g_mixed * gate_out).astype(BF16)
    g_carried_low, g_taps, g_skip = long_filter.backward(to_channels(g_long_low))
    g_f1_w, g_f1_b, g_f2_w, g_f2_b, g_f3_w = filter_pull(g_taps)
    g_carried_seq = to_positions(g_carried_low).astype(F32)
    g_shorted = jnp.concatenate(
        [g_gate_out, g_carried_seq * values, g_carried_seq * gate_in], axis=-1
    )
    lead_one = keep_one * g_shorted
    lead_two = keep_two * g_shorted
    ahead = passed_along(
        jnp.concatenate([lead_one[:, :2], lead_two[:, :2]], axis=1).astype(BF16), "seq", -1
    ).astype(F32)
    after_one = jnp.concatenate([lead_one[:, 1:], ahead[:, :1]], axis=1)
    after_two = jnp.concatenate([lead_two[:, 2:], ahead[:, 2:4]], axis=1)
    g_proj = taps_short[0] * g_shorted + taps_short[1] * after_one + taps_short[2] * after_two
    g_short_w = jnp.stack(
        [
            jnp.sum(g_shorted * current, axis=(0, 1)),
            jnp.sum(lead_one * before_one, axis=(0, 1)),
            jnp.sum(lead_two * before_two, axis=(0, 1)),
        ],
        axis=0,
    )
    g_short_b = jnp.sum(g_shorted, axis=(0, 1))
    g_proj_low = g_proj.astype(BF16).reshape(flat_count, 3 * width)
    g_in_w = weight_gradient(n1_low, g_proj_low)
    g_in_b = jnp.sum(g_proj_low.astype(F32), axis=0)
    g_n1 = back_product(g_proj_low, in_weight)
    g_x_part, g_ln1_gain, g_ln1_bias = ln1_pull(g_n1)
    grad_tokens = (g_resid + g_x_part).reshape(row_count, tok_count, width)

    def lined(parts):
        flat = jnp.concatenate([part.reshape(-1) for part in parts])
        return jnp.pad(flat, (0, -flat.shape[0] % 128)).reshape(-1, 128)

    net = lined((g_f1_w, g_f1_b, g_f2_w, g_f2_b))
    net_rows = net.shape[0]
    own = lined((g_f3_w, g_skip))
    bits = device_bits()
    seq_bits = int(math.log2(seq_count))
    joint = summed(jnp.concatenate([net, own]), range(seq_bits, bits))
    net = summed(joint[:net_rows], range(seq_bits)).reshape(-1)
    own = joint[net_rows:].reshape(-1)
    g_f1_w, g_f1_b, g_f2_w, g_f2_b = (
        part.reshape(like.shape)
        for part, like in zip(
            jnp.split(net, np.cumsum([f1_weight.size, f1_bias.size, f2_weight.size, f2_bias.size])),
            (f1_weight, f1_bias, f2_weight, f2_bias),
        )
    )
    g_f3_w = own[: f3_weight.size].reshape(f3_weight.shape)
    g_skip = own[f3_weight.size : f3_weight.size + lanes]

    shares = 1 << bits
    vectors = (g_ln2_gain, g_ln2_bias, g_up_b, g_down_b, g_out_b)
    vectors += (g_ln1_gain, g_ln1_bias, g_in_b, g_short_b) + tuple(g_short_w)
    rows = jnp.concatenate([v.reshape(shares, -1) for v in vectors], axis=1)
    sums = small_scattered(rows)
    cuts = np.cumsum([v.shape[0] // shares for v in vectors])[:-1]
    (
        g_ln2_gain,
        g_ln2_bias,
        g_up_b,
        g_down_b,
        g_out_b,
        g_ln1_gain,
        g_ln1_bias,
        g_in_b,
        g_short_b,
        *g_short_w,
    ) = jnp.split(sums, cuts)
    return (
        output,
        grad_tokens,
        g_ln1_gain,
        g_ln1_bias,
        g_in_w,
        g_in_b,
        jnp.stack(g_short_w),
        g_short_b,
        g_f1_w,
        g_f1_b,
        g_f2_w,
        g_f2_b,
        g_f3_w,
        g_skip,
        g_out_w,
        g_out_b,
        g_ln2_gain,
        g_ln2_bias,
        g_up_w,
        g_up_b,
        g_down_w,
        g_down_b,
    )


HALO = 16


def turned_halves(values, share, out_ref, at):
    turned = values.T.astype(BF16)
    for run in range(turned.shape[0] // share):
        into = pl.ds(run // 2 * share, share)
        out_ref[run % 2, into, at] = turned[run * share : (run + 1) * share]


def row_of(ref):
    return ref[...].astype(F32).reshape(1, -1)


def keeps(cuts_ref, first_ref, row, count, lanes):
    spot = lax.broadcasted_iota(jnp.int32, (count, lanes), 0) + first_ref[0]

    def begins(at):
        found = at == 0
        for cut in range(cuts_ref.shape[1]):
            found = found | (at == cuts_ref[row, cut])
        return found

    here, before = begins(spot), begins(spot - 1)
    return jnp.where(here, 0.0, 1.0), jnp.where(here | before, 0.0, 1.0)


def short_filter(values, weight, shift, keep_one, keep_two, begin, count):
    one = pltpu.roll(values, 1, 0)[begin : begin + count]
    two = pltpu.roll(values, 2, 0)[begin : begin + count]
    here = values[begin : begin + count]
    return weight[0:1] * here + keep_one * (weight[1:2] * one) + keep_two * (weight[2:3] * two) + shift


def normed(values):
    center = values - jnp.mean(values, axis=-1, keepdims=True)
    spread = jnp.mean(center * center, axis=-1, keepdims=True)
    scale = lax.rsqrt(spread + eps)
    return center * scale, scale


def in_forward_kernel(
    cuts_ref,
    first_ref,
    before_ref,
    x_ref,
    beyond_ref,
    gain_ref,
    bias_ref,
    w0,
    w1,
    w2,
    b0,
    b1,
    b2,
    s1,
    s2,
    c1,
    c2,
    norm_out,
    proj_out,
    carried_out,
    norm,
):
    rows, count, width = x_ref.shape
    extent = count + 2 * HALO
    group = carried_out.shape[3]

    @pl.when(pl.program_id(0) == 0)
    def _():
        for row in range(rows):
            around = [ref[row].astype(F32) for ref in (before_ref, x_ref, beyond_ref)]
            hat, _ = normed(jnp.concatenate(around, axis=0))
            value = hat * row_of(gain_ref) + row_of(bias_ref)
            norm[row * extent : (row + 1) * extent] = value.astype(BF16)
            turned_halves(
                value[HALO : HALO + count], 32, norm_out, pl.ds(row * count, count)
            )

    parts = []
    for third, (w, b) in enumerate(((w0, b0), (w1, b1), (w2, b2))):
        part = dot32(norm[...], w[...]) + row_of(b)
        low = part.astype(BF16)
        for row in range(rows):
            proj_out[third, row] = low[row * extent : (row + 1) * extent]
        parts.append(low.astype(F32))
    lanes = parts[0].shape[1]
    for row in range(rows):
        keep_one, keep_two = keeps(cuts_ref, first_ref, row, count, lanes)
        sides = [
            short_filter(
                parts[third][row * extent : (row + 1) * extent],
                s[...].astype(F32),
                row_of(c),
                keep_one,
                keep_two,
                HALO,
                count,
            )
            for third, s, c in ((1, s1, c1), (2, s2, c2))
        ]
        carried = (sides[0] * sides[1]).astype(BF16)
        for index in range(lanes // group):
            carried_out[index, row] = carried[:, index * group : (index + 1) * group]


def smem():
    return pl.BlockSpec(memory_space=pltpu.SMEM)


def whole(shape):
    return pl.BlockSpec(shape, lambda i: (0,) * len(shape), pipeline_mode=pl.Buffered(1))


def params():
    return pltpu.CompilerParams(
        vmem_limit_bytes=VMEM_MIB * 2**20, dimension_semantics=("arbitrary",)
    )


def third_block(shape, which, steps):
    lead = (0,) * (len(shape) - 1)
    return pl.BlockSpec(shape, lambda i: lead + (which * steps + i,))


def in_forward(
    cuts, first, before, x, beyond, gain, bias, in_weight, in_bias, short_weight, short_bias, group
):
    rows, count, width = x.shape
    extent = count + 2 * HALO
    lanes = 256
    steps = width // lanes
    return pl.pallas_call(
        in_forward_kernel,
        grid=(steps,),
        in_specs=[smem(), smem(), whole(before.shape), whole(x.shape), whole(beyond.shape)]
        + [whole(gain.shape), whole(bias.shape)]
        + [third_block((width, lanes), t, steps) for t in range(3)]
        + [third_block((lanes,), t, steps) for t in range(3)]
        + [third_block((3, lanes), t, steps) for t in (1, 2)]
        + [third_block((lanes,), t, steps) for t in (1, 2)],
        out_specs=[
            whole((2, width // 2, rows * count)),
            pl.BlockSpec((3, rows, extent, lanes), lambda i: (0, 0, 0, i)),
            pl.BlockSpec((lanes // group, rows, count, group), lambda i: (i, 0, 0, 0)),
        ],
        out_shape=[
            jax.ShapeDtypeStruct((2, width // 2, rows * count), BF16),
            jax.ShapeDtypeStruct((3, rows, extent, width), BF16),
            jax.ShapeDtypeStruct((width // group, rows, count, group), BF16),
        ],
        scratch_shapes=[pltpu.VMEM((rows * extent, width), BF16)],
        compiler_params=params(),
        cost_estimate=MUCH,
        name="in_forward",
    )(
        cuts,
        first,
        before,
        x,
        beyond,
        gain,
        bias,
        *[in_weight] * 3,
        *[in_bias] * 3,
        *[short_weight] * 2,
        *[short_bias] * 2,
    )


def gates(cuts_ref, first_ref, proj_ref, weight_ref, shift_ref, row, index, group):
    at = pl.ds(index * group, group)
    extent = proj_ref.shape[2]
    count = extent - 2 * HALO
    keep_one, keep_two = keeps(cuts_ref, first_ref, row, count, group)
    return short_filter(
        proj_ref[0, row, :, at].astype(F32),
        weight_ref[:, at].astype(F32),
        shift_ref[at].astype(F32).reshape(1, -1),
        keep_one,
        keep_two,
        HALO,
        count,
    )


def middle_forward_kernel(
    cuts_ref,
    first_ref,
    long_ref,
    proj_ref,
    weight_ref,
    shift_ref,
    x_ref,
    out_w_ref,
    out_b_ref,
    gain_ref,
    bias_ref,
    up_ref,
    up_b_ref,
    g_act_ref,
    mixed_out,
    resid_out,
    norm_out,
    act_out,
    split_out,
    g_pre_out,
    g_up_b_out,
    mixed,
    norm,
):
    groups, rows, count, group = long_ref.shape

    @pl.when(pl.program_id(0) == 0)
    def _():
        for row in range(rows):
            own = pl.ds(row * count, count)
            for index in range(groups):
                gate = gates(cuts_ref, first_ref, proj_ref, weight_ref, shift_ref, row, index, group)
                value = gate * long_ref[index, row].astype(F32)
                mixed[own, pl.ds(index * group, group)] = value.astype(BF16)
        for row in range(rows):
            own = pl.ds(row * count, count)
            turned_halves(mixed[own, :].astype(F32), 32, mixed_out, own)
            branch = dot32(mixed[own, :], out_w_ref[...]) + row_of(out_b_ref)
            resid = x_ref[own, :].astype(F32) + branch
            resid_out[own, :] = resid
            hat, _ = normed(resid)
            value = hat * row_of(gain_ref) + row_of(bias_ref)
            norm[own, :] = value.astype(BF16)
            turned_halves(value, 32, norm_out, own)

    pre = dot32(norm[...], up_ref[...]) + row_of(up_b_ref)
    scale = math.sqrt(2.0 / math.pi)
    square = pre * pre
    inner = pre * (scale + (scale * 0.044715) * square)
    half = 0.5 + 0.5 * jnp.tanh(inner)
    act = pre * half
    act_out[...] = act.astype(BF16)
    turned_halves(act, 128, split_out, pl.ds(0, act.shape[0]))
    slope = pre * (2.0 * scale + (6.0 * scale * 0.044715) * square)
    slope = half + slope * (half * (1.0 - half))
    g_pre = (g_act_ref[...].astype(F32) * slope).astype(BF16)
    g_pre_out[...] = g_pre
    g_up_b_out[...] = jnp.sum(g_pre.astype(F32), axis=0, keepdims=True)


def middle_forward(
    cuts, first, long, proj, short_weight, short_bias, x, out_w, out_b, gain, bias, up, up_b, g_act
):
    groups, rows, count, group = long.shape
    extent = proj.shape[2]
    tokens, width = x.shape
    hidden = up.shape[1]
    lanes = width
    steps = hidden // lanes

    def part(height):
        return pl.BlockSpec((height, lanes), lambda i: (0, i))

    return pl.pallas_call(
        middle_forward_kernel,
        grid=(steps,),
        in_specs=[
            smem(),
            smem(),
            whole(long.shape),
            whole((1, rows, extent, width)),
            whole((3, width)),
            whole((width,)),
            whole((tokens, width)),
            whole((width, width)),
            whole((width,)),
            whole((width,)),
            whole((width,)),
            part(width),
            pl.BlockSpec((lanes,), lambda i: (i,)),
            part(tokens),
        ],
        out_specs=[
            whole((2, width // 2, tokens)),
            whole((tokens, width)),
            whole((2, width // 2, tokens)),
            part(tokens),
            pl.BlockSpec((2, lanes // 2, tokens), lambda i: (0, i, 0)),
            part(tokens),
            part(1),
        ],
        out_shape=[
            jax.ShapeDtypeStruct((2, width // 2, tokens), BF16),
            jax.ShapeDtypeStruct((tokens, width), F32),
            jax.ShapeDtypeStruct((2, width // 2, tokens), BF16),
            jax.ShapeDtypeStruct((tokens, hidden), BF16),
            jax.ShapeDtypeStruct((2, hidden // 2, tokens), BF16),
            jax.ShapeDtypeStruct((tokens, hidden), BF16),
            jax.ShapeDtypeStruct((1, hidden), F32),
        ],
        scratch_shapes=[pltpu.VMEM((tokens, width), BF16), pltpu.VMEM((tokens, width), BF16)],
        compiler_params=params(),
        cost_estimate=MUCH,
        name="middle_forward",
    )(
        cuts,
        first,
        long,
        proj,
        short_weight,
        short_bias,
        x,
        out_w,
        out_b,
        gain,
        bias,
        up,
        up_b,
        g_act,
    )


def turned_dot(left, right):
    return lax.dot_general(left, right, (((1,), (1,)), ((), ())), preferred_element_type=F32)


def normed_back(values, grad, gain):
    hat, scale = normed(values)
    inward = grad * gain
    mean = jnp.mean(inward, axis=-1, keepdims=True)
    along = jnp.mean(inward * hat, axis=-1, keepdims=True)
    g_gain = jnp.sum(grad * hat, axis=0, keepdims=True)
    return scale * (inward - mean - hat * along), g_gain, jnp.sum(grad, axis=0, keepdims=True)


def fetched(step, last, sources, targets, sems):
    @pl.when(step == 0)
    def _():
        for k, (source, target) in enumerate(zip(sources, targets)):
            pltpu.make_async_copy(source, target, sems.at[k]).start()

    @pl.when(step == last)
    def _():
        for k, (source, target) in enumerate(zip(sources, targets)):
            pltpu.make_async_copy(source, target, sems.at[k]).wait()


def middle_backward_kernel(
    cuts_ref,
    first_ref,
    long_at,
    proj_at,
    weight_ref,
    shift_ref,
    resid_at,
    grad_at,
    gain_ref,
    out_w_at,
    g_pre_ref,
    up_ref,
    _,
    g_long_out,
    g_gate_out,
    g_resid_out,
    g_branch_out,
    sums_out,
    token_out,
    total,
    long_ref,
    proj_ref,
    resid_ref,
    grad_ref,
    out_w_ref,
    sems,
):
    groups, rows, count, group = long_ref.shape
    step = pl.program_id(0)
    token_out[0] = 0
    fetched(
        step,
        pl.num_programs(0) - 1,
        (long_at, proj_at.at[pl.ds(0, 1)], resid_at, grad_at, out_w_at),
        (long_ref, proj_ref, resid_ref, grad_ref, out_w_ref),
        sems,
    )

    @pl.when(step == 0)
    def _():
        total[...] = turned_dot(g_pre_ref[...], up_ref[...])

    @pl.when(step > 0)
    def _():
        total[...] += turned_dot(g_pre_ref[...], up_ref[...])

    @pl.when(step == pl.num_programs(0) - 1)
    def _():
        sums = [0.0] * 4
        for row in range(rows):
            own = pl.ds(row * count, count)
            grad = grad_ref[own, :].astype(F32)
            back, g_gain, g_bias = normed_back(
                resid_ref[own, :], total[own, :], row_of(gain_ref)
            )
            g_resid = grad + back
            g_resid_out[own, :] = g_resid
            low = g_resid.astype(BF16)
            g_branch_out[own, :] = low
            g_out_b = jnp.sum(low.astype(F32), axis=0, keepdims=True)
            g_down_b = jnp.sum(grad, axis=0, keepdims=True)
            sums = [a + b for a, b in zip(sums, (g_gain, g_bias, g_out_b, g_down_b))]
            total[own, :] = turned_dot(low, out_w_ref[...])
        sums_out[...] = jnp.concatenate(sums + [jnp.zeros_like(sums[0])] * 4, axis=0)
        for row in range(rows):
            own = pl.ds(row * count, count)
            for index in range(groups):
                at = pl.ds(index * group, group)
                g_mixed = total[own, at]
                gate = gates(cuts_ref, first_ref, proj_ref, weight_ref, shift_ref, row, index, group)
                g_gate_out[row, :, at] = g_mixed * long_ref[index, row].astype(F32)
                g_long_out[index, row] = (g_mixed * gate).astype(BF16)


def middle_backward(
    cuts, first, long, proj, short_weight, short_bias, resid, grad, gain, out_w, g_pre, up, ready
):
    groups, rows, count, group = long.shape
    extent = proj.shape[2]
    tokens, width = resid.shape
    hidden = up.shape[1]
    lanes = 1024
    steps = hidden // lanes

    def part(height):
        return pl.BlockSpec((height, lanes), lambda i: (0, i))

    anywhere = pl.BlockSpec(memory_space=pl.ANY)
    return pl.pallas_call(
        middle_backward_kernel,
        grid=(steps,),
        in_specs=[
            smem(),
            smem(),
            anywhere,
            anywhere,
            whole((3, width)),
            whole((width,)),
            anywhere,
            anywhere,
            whole((width,)),
            anywhere,
            part(tokens),
            part(width),
            pl.BlockSpec(memory_space=pl.ANY),
        ],
        out_specs=[
            whole(long.shape),
            whole((rows, count, width)),
            whole((tokens, width)),
            whole((tokens, width)),
            whole((8, width)),
            smem(),
        ],
        out_shape=[
            jax.ShapeDtypeStruct(long.shape, BF16),
            jax.ShapeDtypeStruct((rows, count, width), F32),
            jax.ShapeDtypeStruct((tokens, width), F32),
            jax.ShapeDtypeStruct((tokens, width), BF16),
            jax.ShapeDtypeStruct((8, width), F32),
            jax.ShapeDtypeStruct((1,), jnp.int32),
        ],
        scratch_shapes=[
            pltpu.VMEM((tokens, width), F32),
            pltpu.VMEM(long.shape, BF16),
            pltpu.VMEM((1, rows, extent, width), BF16),
            pltpu.VMEM((tokens, width), F32),
            pltpu.VMEM((tokens, width), BF16),
            pltpu.VMEM((width, width), BF16),
            pltpu.SemaphoreType.DMA((5,)),
        ],
        compiler_params=params(),
        cost_estimate=MUCH,
        name="middle_backward",
    )(
        cuts,
        first,
        long,
        proj,
        short_weight,
        short_bias,
        resid,
        grad,
        gain,
        out_w,
        g_pre,
        up,
        ready,
    )


def in_backward_kernel(
    cuts_ref,
    first_ref,
    g_carried_ref,
    g_gate_ref,
    g_next_ref,
    proj_ref,
    s0,
    s1,
    s2,
    c1,
    c2,
    w0,
    w1,
    w2,
    x_at,
    gain_ref,
    g_resid_at,
    *others,
):
    g_proj_out, sums_out, g_tokens_out, norm_sums_out, token_out = others[-9:-4]
    total, x_ref, g_resid_ref, sems = others[-4:]
    token_out[0] = 0
    fetched(
        pl.program_id(0),
        pl.num_programs(0) - 1,
        (x_at, g_resid_at),
        (x_ref, g_resid_ref),
        sems,
    )
    weights = [s[...].astype(F32) for s in (s0, s1, s2)]
    shifts = [None, row_of(c1), row_of(c2)]
    _, rows, extent, lanes = proj_ref.shape
    count = extent - 2 * HALO
    reach = count + HALO
    group = g_carried_ref.shape[3]
    step = pl.program_id(0)
    sums = [[0.0] * 5 for _ in range(3)]
    for row in range(rows):
        keep_one, keep_two = keeps(cuts_ref, first_ref, row, reach, lanes)
        values = [proj_ref[third, row].astype(F32) for third in range(3)]
        sides = [
            short_filter(
                values[t], weights[t], shifts[t], keep_one, keep_two, HALO, reach
            )
            for t in (1, 2)
        ]
        g_carried = jnp.concatenate(
            [g_carried_ref[index, row] for index in range(lanes // group)], axis=1
        ).astype(F32)
        g_gate = jnp.concatenate([g_gate_ref[row], g_next_ref[row].astype(F32)], axis=0)
        grads = (g_gate, g_carried * sides[1], g_carried * sides[0])
        for third, grad in enumerate(grads):
            weight = weights[third]
            lead_one, lead_two = keep_one * grad, keep_two * grad
            g_proj = (
                weight[0:1] * grad
                + weight[1:2] * pltpu.roll(lead_one, reach - 1, 0)
                + weight[2:3] * pltpu.roll(lead_two, reach - 2, 0)
            )[:count]
            low = g_proj.astype(BF16)
            g_proj_out[third, row * count : (row + 1) * count] = low
            before_one = pltpu.roll(values[third], 1, 0)[HALO : HALO + count]
            before_two = pltpu.roll(values[third], 2, 0)[HALO : HALO + count]
            here = values[third][HALO : HALO + count]
            parts = (
                grad[:count] * here,
                lead_one[:count] * before_one,
                lead_two[:count] * before_two,
                grad[:count],
                low.astype(F32),
            )
            sums[third] = [
                a + jnp.sum(b, axis=0, keepdims=True) for a, b in zip(sums[third], parts)
            ]
    for third in range(3):
        sums_out[third] = jnp.concatenate(
            sums[third] + [jnp.zeros((3, lanes), F32)], axis=0
        )
    product = sum(
        turned_dot(g_proj_out[third], w[...]) for third, w in enumerate((w0, w1, w2))
    )

    @pl.when(step == 0)
    def _():
        total[...] = product

    @pl.when(step > 0)
    def _():
        total[...] += product

    @pl.when(step == pl.num_programs(0) - 1)
    def _():
        norm_sums = [0.0, 0.0]
        for row in range(rows):
            own = pl.ds(row * count, count)
            back, g_gain, g_shift = normed_back(
                x_ref[own, :].astype(F32), total[own, :], row_of(gain_ref)
            )
            g_tokens_out[own, :] = g_resid_ref[own, :] + back
            norm_sums = [norm_sums[0] + g_gain, norm_sums[1] + g_shift]
        norm_sums_out[...] = jnp.concatenate(
            norm_sums + [jnp.zeros((6, x_ref.shape[1]), F32)], axis=0
        )


def in_backward(
    cuts,
    first,
    g_carried,
    g_gate,
    g_next,
    proj,
    short_weight,
    short_bias,
    in_w,
    x,
    gain,
    g_resid,
    ready,
):
    _, rows, extent, width = proj.shape
    count = extent - 2 * HALO
    tokens = rows * count
    group = g_carried.shape[3]
    lanes = 256
    steps = width // lanes

    anywhere = pl.BlockSpec(memory_space=pl.ANY)
    return pl.pallas_call(
        in_backward_kernel,
        grid=(steps,),
        in_specs=[
            smem(),
            smem(),
            pl.BlockSpec((lanes // group, rows, count + HALO, group), lambda i: (i, 0, 0, 0)),
            pl.BlockSpec((rows, count, lanes), lambda i: (0, 0, i)),
            pl.BlockSpec((rows, HALO, lanes), lambda i: (0, 0, i)),
            pl.BlockSpec((3, rows, extent, lanes), lambda i: (0, 0, 0, i)),
        ]
        + [third_block((3, lanes), t, steps) for t in range(3)]
        + [third_block((lanes,), t, steps) for t in (1, 2)]
        + [third_block((width, lanes), t, steps) for t in range(3)]
        + [anywhere, whole((width,)), anywhere]
        + [pl.BlockSpec(memory_space=pl.ANY)] * len(ready),
        out_specs=[
            pl.BlockSpec((3, tokens, lanes), lambda i: (0, 0, i)),
            pl.BlockSpec((3, 8, lanes), lambda i: (0, 0, i)),
            whole((tokens, width)),
            whole((8, width)),
            smem(),
        ],
        out_shape=[
            jax.ShapeDtypeStruct((3, tokens, width), BF16),
            jax.ShapeDtypeStruct((3, 8, width), F32),
            jax.ShapeDtypeStruct((tokens, width), F32),
            jax.ShapeDtypeStruct((8, width), F32),
            jax.ShapeDtypeStruct((1,), jnp.int32),
        ],
        scratch_shapes=[
            pltpu.VMEM((tokens, width), F32),
            pltpu.VMEM((tokens, width), BF16),
            pltpu.VMEM((tokens, width), F32),
            pltpu.SemaphoreType.DMA((2,)),
        ],
        compiler_params=params(),
        cost_estimate=MUCH,
        name="in_backward",
    )(
        cuts,
        first,
        g_carried,
        g_gate,
        g_next,
        proj,
        *[short_weight] * 3,
        *[short_bias] * 2,
        *[in_w] * 3,
        x,
        gain,
        g_resid,
        *ready,
    )


def mark(*others):
    def kernel(*refs):
        refs[-1][0] = 0

    return pl.pallas_call(
        kernel,
        in_specs=[pl.BlockSpec(memory_space=pl.ANY)] * len(others),
        out_specs=smem(),
        out_shape=jax.ShapeDtypeStruct((1,), jnp.int32),
        cost_estimate=LITTLE,
        name="mark",
    )(*others)


def matmul_turned(left, right, columns, ready):
    def kernel(left_ref, right_ref, _, out_ref):
        out_ref[...] = turned_dot(left_ref[...], right_ref[...]).astype(BF16)

    height, depth = left.shape
    width = right.shape[0]
    return pl.pallas_call(
        kernel,
        grid=(width // columns,),
        in_specs=[
            whole((height, depth)),
            pl.BlockSpec((columns, depth), lambda i: (i, 0)),
            pl.BlockSpec(memory_space=pl.ANY),
        ],
        out_specs=pl.BlockSpec((height, columns), lambda i: (0, i)),
        out_shape=jax.ShapeDtypeStruct((height, width), BF16),
        compiler_params=params(),
        cost_estimate=LITTLE,
        name="matmul_turned",
    )(left, right, ready)


def down_forward(resid, act, down, bias, ready):
    tokens, width = resid.shape
    depth = 2048
    steps = act.shape[1] // depth

    def kernel(resid_ref, act_ref, down_ref, bias_ref, *refs):
        out_ref, token_out, total = refs[-3:]
        step = pl.program_id(0)
        token_out[0] = 0
        product = dot32(act_ref[...], down_ref[...])

        @pl.when(step == 0)
        def _():
            total[...] = resid_ref[...] + row_of(bias_ref) + product

        @pl.when(step > 0)
        def _():
            total[...] += product

        @pl.when(step == steps - 1)
        def _():
            out_ref[...] = total[...].astype(BF16)

    return pl.pallas_call(
        kernel,
        grid=(steps,),
        in_specs=[
            whole((tokens, width)),
            pl.BlockSpec((tokens, depth), lambda i: (0, i)),
            pl.BlockSpec((depth, width), lambda i: (i, 0)),
            whole((width,)),
        ]
        + [pl.BlockSpec(memory_space=pl.ANY)] * len(ready),
        out_specs=[whole((tokens, width)), smem()],
        out_shape=[
            jax.ShapeDtypeStruct((tokens, width), BF16),
            jax.ShapeDtypeStruct((1,), jnp.int32),
        ],
        scratch_shapes=[pltpu.VMEM((tokens, width), F32)],
        compiler_params=params(),
        cost_estimate=LITTLE,
        name="down_forward",
    )(resid, act, down, bias, *ready)


def after(value, *others):
    return lax.optimization_barrier((value, others))[0]


def gradient_kernel(counts, order_ref, firsts, seconds, arrived, sent, kept, token, total):
    step = pl.program_id(0)
    token[0] = 0

    def write(values, which):
        if not kept:
            sent[0][...] = values.astype(BF16)
            return
        (send,), (keep,), (total_ref,) = sent, kept, total
        total_ref[...] = values
        share = total_ref.shape[0] // 16
        for spot in range(16):
            piece = pl.ds(pl.multiple_of(order_ref[1 + spot] * share, share), share)
            into = (send, keep)[spot // 8]
            into[pl.ds(spot % 8 * share, share)] = (
                total_ref[piece] + arrived[which][piece].astype(F32)
            ).astype(BF16)

    begin = 0
    for which, (steps, first, second) in enumerate(zip(counts, firsts, seconds)):

        @pl.when((step >= begin) & (step < begin + steps))
        def _(first=first, second=second, which=which):
            write(dot32(first[0], second[...]), which)

        begin += steps


def gradient(order, pairs, arrived, ready, columns, cost=LITTLE):
    height, tokens = pairs[0][0].shape[1:]
    counts, first_specs, second_specs, arrived_specs, begin = [], [], [], [], 0
    for first, second in pairs:
        parts = second.shape[-1] // columns
        steps = parts * (second.shape[0] if second.ndim == 3 else 1)
        first_specs.append(pl.BlockSpec((1, height, tokens), lambda i, o: (o[0], 0, 0)))

        def place(i, o, begin=begin, steps=steps, parts=parts, deep=second.ndim == 3):
            at = jnp.clip(i - begin, 0, steps - 1)
            return (at // parts, 0, at % parts) if deep else (0, at)

        def flat(i, o, begin=begin, steps=steps):
            return 0, jnp.clip(i - begin, 0, steps - 1)

        shape = (None, tokens, columns) if second.ndim == 3 else (tokens, columns)
        second_specs.append(pl.BlockSpec(shape, place))
        arrived_specs.append(pl.BlockSpec((height, columns), flat))
        counts.append(steps)
        begin += steps
    anywhere = pl.BlockSpec(memory_space=pl.ANY)
    if arrived is None:
        arrived, arrived_specs = (), []
        heights, scratch = [height], []
    else:
        heights, scratch = [height // 2] * 2, [pltpu.VMEM((height, columns), F32)]
    outputs = [jax.ShapeDtypeStruct((rows, begin * columns), BF16) for rows in heights]
    out_specs = [pl.BlockSpec((rows, columns), lambda i, o: (0, i)) for rows in heights]

    def kernel(order_ref, *refs):
        refs = list(refs)

        def take(count):
            taken, refs[:] = refs[:count], refs[count:]
            return taken

        firsts, seconds, arrived_refs = take(len(pairs)), take(len(pairs)), take(len(arrived))
        take(len(ready))
        sent_refs, kept_refs, (token,) = take(1), take(len(heights) - 1), take(1)
        gradient_kernel(
            counts, order_ref, firsts, seconds, arrived_refs, sent_refs, kept_refs, token, refs
        )

    inputs = [p[0] for p in pairs] + [p[1] for p in pairs] + list(arrived) + list(ready)
    return pl.pallas_call(
        kernel,
        grid_spec=pltpu.PrefetchScalarGridSpec(
            num_scalar_prefetch=1,
            grid=(begin,),
            in_specs=first_specs + second_specs + arrived_specs + [anywhere] * len(ready),
            out_specs=out_specs + [smem()],
            scratch_shapes=scratch,
        ),
        out_shape=outputs + [jax.ShapeDtypeStruct((1,), jnp.int32)],
        compiler_params=params(),
        cost_estimate=cost,
        name="gradient",
    )(order, *inputs)


def to_sibling(blocks):
    return [swapped(block, lambda one: 1) for block in blocks]


def bit_of(index, bit):
    return (index >> bit) & 1


def choose_bit(index, bit, axis):
    def choose(array, mine):
        own = bit_of(index, bit)
        return pick(array, own if mine else 1 - own, axis)

    return choose


def choose_second(index, axis):
    def choose(array, mine):
        own = jnp.where(bit_of(index, 0) == 0, bit_of(index, 2), bit_of(index, 1))
        return pick(array, own if mine else 1 - own, axis)

    return choose


def choose_first(index, axis):
    def choose(array, mine):
        low, high = bit_of(index, 1), bit_of(index, 2)
        if not mine:
            low, high = 1 - low, 1 - high
        core = bit_of(index, 0)
        return jnp.stack(
            [
                pick(array, jnp.where(core == 0, 2 * j + low, 2 * high + j), axis)
                for j in range(2)
            ],
            axis=axis,
        )

    return choose


def swap_bit(bit):
    return lambda value: swapped(value, lambda one: 1 << bit)


def swap_first(value):
    return swapped(value, lambda one: 4 if one & 1 else 2)


def swap_second(value):
    return swapped(value, lambda one: 2 if one & 1 else 4)


def order_first(index):
    core, low, high = bit_of(index, 0), bit_of(index, 1), bit_of(index, 2)

    def some(low, high):
        return [
            4 * z + jnp.where(core == 0, 2 * j + low, 2 * high + j) for z in range(4) for j in range(2)
        ]

    return jnp.stack([core] + some(1 - low, 1 - high) + some(low, high)).astype(jnp.int32)


def stage_sent(kept, arrived, choose):
    return added(choose(kept, False), choose(arrived, False), BF16)


def stage(kept, arrived, choose):
    sent = stage_sent(kept, arrived, choose)
    return sent, added(choose(kept, True), choose(arrived, True), BF16)


def finished(kept, arrived, own, last, cuts, ready):
    rows, width = last.shape[-2:]
    last = last.reshape(rows, width)

    def kernel(own_ref, kept_ref, arrived_ref, last_ref, *refs):
        outs = refs[len(ready) : len(ready) + len(cuts)]
        refs[-1][0] = 0
        begin = 0
        for out, size in zip(outs, cuts):
            at = slice(begin, begin + size)
            first = kept_ref[:, at].astype(F32) + arrived_ref[:, at].astype(F32)
            out[...] = first + last_ref[:, at].astype(F32)
            begin += size

    half = pl.BlockSpec((None, rows, width), lambda i, o: (o[0], 0, 0))

    def flat(columns):
        return pl.BlockSpec((rows, columns), lambda i, o: (0, 0))

    *outs, token = pl.pallas_call(
        kernel,
        grid_spec=pltpu.PrefetchScalarGridSpec(
            num_scalar_prefetch=1,
            grid=(1,),
            in_specs=[half, half, flat(width)]
            + [pl.BlockSpec(memory_space=pl.ANY)] * len(ready),
            out_specs=[flat(size) for size in cuts] + [smem()],
        ),
        out_shape=[jax.ShapeDtypeStruct((rows, size), F32) for size in cuts]
        + [jax.ShapeDtypeStruct((1,), jnp.int32)],
        compiler_params=params(),
        cost_estimate=LITTLE,
        name="finished",
    )(
        own.astype(jnp.int32).reshape(1),
        kept.reshape(2, rows, width),
        arrived.reshape(2, rows, width),
        last,
        *ready,
    )
    return outs, token


def paired(values):
    while len(values) > 1:
        values = [values[k] + values[k + 1] for k in range(0, len(values), 2)]
    return values[0]


def summed_lines(values, top, ready, cut=True):
    rows, lanes = values[0].shape
    rest = top if cut else 0
    count = len(values)

    def kernel(*refs):
        total = paired([ref[...] for ref in refs[:count]])
        refs[-3][...] = total[:top]
        refs[-2][...] = total[rest:]
        refs[-1][0] = 0

    return pl.pallas_call(
        kernel,
        grid=(1,),
        in_specs=[whole((rows, lanes))] * count + [pl.BlockSpec(memory_space=pl.ANY)] * len(ready),
        out_specs=[whole((top, lanes)), whole((rows - rest, lanes)), smem()],
        out_shape=[
            jax.ShapeDtypeStruct((top, lanes), F32),
            jax.ShapeDtypeStruct((rows - rest, lanes), F32),
            jax.ShapeDtypeStruct((1,), jnp.int32),
        ],
        compiler_params=params(),
        cost_estimate=LITTLE,
        name="summed_lines",
    )(*values, *ready)


def unpacked(seq, seq_count, top, values, units, bands, sizes, ready):
    lanes = top.shape[1]
    count = len(values)

    def kernel(seq_ref, top_ref, *refs):
        outs, below, token = refs[count + len(ready) : -2], refs[-1], refs[-2]
        token[0] = 0
        below[...] = paired([ref[...] for ref in refs[:count]])
        f1_w, f1_b, f2_w, f2_b, f3_w, skip = outs[:6]
        f3_w[...] = top_ref[:units]
        skip[...] = top_ref[units]
        f2_w[...] = below[:units, :units]
        f1_w[...] = below[:bands, units:]
        f1_b[...] = below[bands, units:]
        f2_b[...] = below[bands + 1, units:]
        line, seq = units, seq_ref[0]
        outs = list(outs[6:])
        for kinds, size in sizes:
            begin = seq * size
            for kind in range(kinds):
                at = line + begin // lanes
                two = jnp.concatenate([below[pl.ds(at, 1)], below[pl.ds(at + 1, 1)]], axis=1)
                shift = lax.rem(2 * lanes - begin % lanes, 2 * lanes)
                outs.pop(0)[...] = pltpu.roll(two, shift, 1)[0, :size]
                line += size * seq_count // lanes

    shapes = [(bands, units), (units,), (units, units), (units,), (units, lanes), (lanes,)]
    shapes += [(size,) for kinds, size in sizes for _ in range(kinds)]
    return pl.pallas_call(
        kernel,
        grid=(1,),
        in_specs=[smem(), whole(top.shape)]
        + [whole(values[0].shape)] * count
        + [pl.BlockSpec(memory_space=pl.ANY)] * len(ready),
        out_specs=[whole(shape) for shape in shapes] + [smem()],
        out_shape=[jax.ShapeDtypeStruct(shape, F32) for shape in shapes]
        + [jax.ShapeDtypeStruct((1,), jnp.int32)],
        scratch_shapes=[pltpu.VMEM(values[0].shape, F32)],
        compiler_params=params(),
        cost_estimate=LITTLE,
        name="unpacked",
    )(seq, top, *values, *ready)


def block_device(
    tokens,
    cotangent,
    bounds,
    ln1_gain,
    ln1_bias,
    in_weight,
    in_bias,
    short_weight,
    short_bias,
    f1_weight,
    f1_bias,
    f2_weight,
    f2_bias,
    f3_weight,
    filter_skip,
    out_weight,
    out_bias,
    ln2_gain,
    ln2_bias,
    up_weight,
    up_bias,
    down_weight,
    down_bias,
):
    seq_count = lax.axis_size("seq")
    rows, count, width = tokens.shape
    flat = rows * count
    length = count * seq_count
    lanes = f3_weight.shape[1]
    first_channel = (lax.axis_index("seq") * lanes).astype(jnp.int32)
    first = (lax.axis_index("seq") * count).astype(jnp.int32).reshape(1)

    def exchanged(array):
        return lax.all_to_all(array, "seq", split_axis=0, concat_axis=0, tiled=True)

    index = device_index()
    before = passed_along(tokens[:, count - HALO :], "seq", 1)
    beyond = passed_along(tokens[:, :HALO], "seq", -1)
    norm_halves, proj, carried_own = in_forward(
        bounds,
        first,
        before,
        tokens,
        beyond,
        ln1_gain,
        ln1_bias,
        in_weight,
        in_bias,
        short_weight,
        short_bias,
        lanes,
    )
    carried = exchanged(carried_own)

    tables = transform_tables(count)
    table = piece_table(bounds, seq_count, count)
    skip = filter_skip
    taps_spec, kept = taps_and_spectrum(
        first_channel.reshape(1),
        seq_count,
        count,
        f1_weight,
        f1_bias,
        f2_weight,
        f2_bias,
        f3_weight,
        tables,
        carried_own,
    )
    long_own = long_forward(table, carried, taps_spec, skip, tables)
    long = exchanged(long_own)
    x = tokens.reshape(flat, width)
    grad = cotangent.reshape(flat, width)
    g_act = matmul_turned(grad, down_weight, 1024, long_own)
    mixed_halves, resid, norm2_halves, act, act_halves, g_pre, g_up_b = middle_forward(
        bounds,
        first,
        long,
        proj,
        short_weight,
        short_bias,
        x,
        out_weight,
        out_bias,
        ln2_gain,
        ln2_bias,
        up_weight,
        up_bias,
        g_act,
    )
    first_order = order_first(index)
    send_order = (1 - bit_of(index, 0)).astype(jnp.int32).reshape(1)
    down_pairs = [(act_halves, grad)]
    *down_sent, _ = gradient(send_order, down_pairs, None, (), 512)
    down_arrived = to_sibling(down_sent)
    *up_sent, _ = gradient(send_order, [(norm2_halves, g_pre)], None, down_sent, 2048)
    up_arrived = to_sibling(up_sent)
    down_send, down_keep, _ = gradient(first_order, down_pairs, down_arrived, up_sent, 512)
    down_arrived = swap_first(down_send)
    g_long, g_gate, g_resid, g_branch, middle_sums, token = middle_backward(
        bounds,
        first,
        long,
        proj,
        short_weight,
        short_bias,
        resid,
        grad,
        ln2_gain,
        out_weight,
        g_pre,
        up_weight,
        down_send,
    )
    g_long_all = exchanged(g_long)
    g_next = passed_along(g_gate[:, :HALO].astype(BF16), "seq", -1)

    def shaped(array, lead):
        return array.reshape(lead + (-1, array.shape[-1]))

    *out_sent, _ = gradient(send_order, [(mixed_halves, g_branch)], None, (), 1024)
    up_send, up_keep, token = gradient(
        first_order,
        [(norm2_halves, g_pre), (mixed_halves, g_branch)],
        up_arrived + to_sibling(out_sent),
        (),
        1024,
    )
    up_arrived = swap_first(up_send)
    down_send, down_keep = stage(
        shaped(down_keep, (2, 2, 2)),
        shaped(down_arrived, (2, 2, 2)),
        choose_bit(index + token[0], 3, 1),
    )
    down_arrived = swap_bit(3)(down_send)
    g_series, g_taps, g_skip, token = long_backward(
        table, g_long_all, carried, taps_spec, skip, tables, (up_send, down_send)
    )
    g_carried = exchanged(g_series)
    output, token = down_forward(resid, act, down_weight, down_bias, (g_series,))
    output = output.reshape(rows, count, width)
    later = index + token[0]
    down_send, down_keep = stage(down_keep, down_arrived, choose_bit(later, 4, 0))
    down_arrived = swap_bit(4)(down_send)
    up_send, up_keep = stage(
        shaped(up_keep, (4, 2)), shaped(up_arrived, (4, 2)), choose_second(later, 1)
    )
    up_arrived = swap_second(up_send)
    g_proj, short_sums, g_tokens, norm_sums, token = in_backward(
        bounds,
        first,
        g_carried,
        g_gate,
        g_next,
        proj,
        short_weight,
        short_bias,
        in_weight,
        x,
        ln1_gain,
        g_resid,
        (down_send, up_send),
    )
    later = index + token[0]
    down_send = stage_sent(down_keep, down_arrived, choose_second(later, 0))
    down_last = swap_second(down_send)
    up_send, up_keep = stage(
        shaped(up_keep, (2, 2)), shaped(up_arrived, (2, 2)), choose_bit(later, 3, 1)
    )
    up_arrived = swap_bit(3)(up_send)
    in_pairs = [(norm_halves, g_proj)]
    *in_sent, _ = gradient(send_order, in_pairs, None, (down_send, up_send), 1024, MUCH)
    in_send, in_keep, token = gradient(first_order, in_pairs, to_sibling(in_sent), (), 1024)
    in_arrived = swap_first(in_send)
    row_count = lax.axis_size("rows")
    seq_bits = seq_count.bit_length() - 1
    payloads = filter_backward(
        first_channel.reshape(1),
        lax.axis_index("rows").astype(jnp.int32).reshape(1),
        row_count,
        g_taps.reshape(length, lanes),
        kept,
        f2_weight,
        f3_weight,
        g_skip,
        (middle_sums, g_up_b, norm_sums, short_sums),
        (in_send,),
    )
    arrived = [payloads[0]] + [
        swapped(payloads[k], lambda one, k=k: k << seq_bits) for k in range(1, row_count)
    ]
    later = index + mark(*payloads)[0]
    up_send = stage_sent(up_keep, up_arrived, choose_bit(later, 4, 0))
    up_last = swap_bit(4)(up_send)
    left = jnp.where(bit_of(index, 0) == 0, bit_of(index, 2), bit_of(index, 1))
    (g_down_w,), token = finished(
        down_keep, down_arrived, left, down_last, (width,), (up_send,)
    )
    units, bands = f3_weight.shape[0], f1_weight.shape[0]
    top, mine, token = summed_lines(arrived, units + 8, (token,))
    in_send, in_keep = stage(
        shaped(in_keep, (4, 2)),
        shaped(in_arrived, (4, 2)),
        choose_second(index + token[0], 1),
    )
    in_arrived = swap_second(in_send)
    arrived = swapped(mine, lambda one: 1)
    _, mine, token = summed_lines([mine, arrived], 8, (in_send,), False)
    in_send, in_keep = stage(
        shaped(in_keep, (2, 2)), shaped(in_arrived, (2, 2)), choose_bit(index + token[0], 3, 1)
    )
    in_arrived = swap_bit(3)(in_send)
    arrived = swapped(mine, lambda one: 2)
    _, mine, token = summed_lines([mine, arrived], 8, (in_send,), False)
    (g_up_w, g_out_w), token = finished(
        up_keep, up_arrived, bit_of(index, 4), up_last, (up_weight.shape[1], width), (token,)
    )
    in_send = stage_sent(in_keep, in_arrived, choose_bit(index + token[0], 4, 0))
    in_last = swap_bit(4)(in_send)
    arrived = swapped(mine, lambda one: 4)
    shares = 1 << device_bits()
    sizes = ((6, width // shares), (1, up_weight.shape[1] // shares), (5, 3 * width // shares))
    seq = lax.axis_index("seq").astype(jnp.int32).reshape(1)
    *small, token = unpacked(
        seq, seq_count, top, [mine, arrived], units, bands, sizes, (in_send,)
    )
    (g_in_w,), _ = finished(
        in_keep, in_arrived, bit_of(index, 4), in_last, (3 * width,), (token,)
    )
    (g_f1_w, g_f1_b, g_f2_w, g_f2_b, g_f3_w, g_skip, *small) = small
    (g_ln2_gain, g_ln2_bias, g_out_b, g_down_b, g_ln1_gain, g_ln1_bias, g_up_b, *small) = small
    *g_short_w, g_short_b, g_in_b = small
    g_short_w = jnp.stack(g_short_w)
    grad_tokens = g_tokens.reshape(rows, count, width)
    return (
        output,
        grad_tokens,
        g_ln1_gain,
        g_ln1_bias,
        g_in_w,
        g_in_b,
        g_short_w,
        g_short_b,
        g_f1_w,
        g_f1_b,
        g_f2_w,
        g_f2_b,
        g_f3_w,
        g_skip,
        g_out_w,
        g_out_b,
        g_ln2_gain,
        g_ln2_bias,
        g_up_w,
        g_up_b,
        g_down_w,
        g_down_b,
    )


def per_device(tokens, *others):
    shares = lax.axis_size("rows") * lax.axis_size("seq")
    count, width = tokens.shape[1:]
    hidden = others[20].shape[0]
    lanes = width // lax.axis_size("seq")
    fits = shares == 32 and width == 1024 and hidden == 4096 and lanes == 128 and count % 128 == 0
    return (block_device if fits else plain_device)(tokens, *others)


def solution(mesh):
    return jax.shard_map(
        per_device,
        mesh=mesh,
        in_specs=(
            P("rows", "seq", None),
            P("rows", "seq", None),
            P("rows", None),
            P(),
            P(),
            P(),
            P(),
            P(),
            P(),
            P(),
            P(),
            P(),
            P(),
            P(None, "seq"),
            P("seq"),
            P(),
            P(),
            P(),
            P(),
            P(),
            P(),
            P(),
            P(),
        ),
        out_specs=(
            P("rows", "seq", None),
            P("rows", "seq", None),
            P(("rows", "seq")),
            P(("rows", "seq")),
            P(("rows", "seq"), None),
            P(("rows", "seq")),
            P(None, ("rows", "seq")),
            P(("rows", "seq")),
            P(),
            P(),
            P(),
            P(),
            P(None, "seq"),
            P("seq"),
            P(("rows", "seq"), None),
            P(("rows", "seq")),
            P(("rows", "seq")),
            P(("rows", "seq")),
            P(("rows", "seq"), None),
            P(("rows", "seq")),
            P(("rows", "seq"), None),
            P(("rows", "seq")),
        ),
        check_vma=False,
    )
```
